32 devices in a mesh: wide: 8 (over y, x, core), narrow: 4 (over z).
Axes of the slice: x: 2, y: 2, z: 4, core: 2. Of those that a mesh axis runs over, the one named last changes fastest.
Arguments:
- tokens: float32 [18464, 1024], P(('wide', 'narrow')), may hold values from -6 to 6
- cotangent: float32 [18464, 1024], P(('wide', 'narrow')), may hold values from -6 to 6
- triple_weight: float32 [1024, 3, 1024], P('wide', None, 'narrow'), may hold values from -0.1875 to 0.1875
- output_weight: float32 [1024, 1024], P('narrow', 'wide'), may hold values from -2 to 2
- expand_weight: float32 [1024, 4096], P('wide', 'narrow'), may hold values from -0.1875 to 0.1875
- shrink_weight: float32 [4096, 1024], P('narrow', 'wide'), may hold values from -0.09375 to 0.09375
- norm_gains: float32 [2, 1024], replicated, may hold values from 0.5 to 1.5
- shift_biases: float32 [4, 1024], replicated, may hold values from -0.6 to 0.6
- head_biases: float32 [2, 1024], P(None, 'narrow'), may hold values from -0.3 to 0.3
- expand_biases: float32 [4096], P('narrow'), may hold values from -0.6 to 0.6
- triple_first: float32 [1024, 3, 1024], P('wide', None, 'narrow'), may hold values from -89.68232 to 89.68232
- output_first: float32 [1024, 1024], P('narrow', 'wide'), may hold values from -10.59882 to 10.59882
- expand_first: float32 [1024, 4096], P('wide', 'narrow'), may hold values from -27.17646 to 27.17646
- shrink_first: float32 [4096, 1024], P('narrow', 'wide'), may hold values from -51.635273 to 51.635273
- gains_first: float32 [2, 1024], replicated, may hold values from -89.68232 to 89.68232
- shifts_first: float32 [4, 1024], replicated, may hold values from -89.68232 to 89.68232
- heads_first: float32 [2, 1024], P(None, 'narrow'), may hold values from -89.68232 to 89.68232
- widen_first: float32 [4096], P('narrow'), may hold values from -27.17646 to 27.17646
- triple_second: float32 [1024, 3, 1024], P('wide', None, 'narrow'), may hold values from 9.232 to 147.712
- output_second: float32 [1024, 1024], P('narrow', 'wide'), may hold values from 0.147712 to 2.21568
- expand_second: float32 [1024, 4096], P('wide', 'narrow'), may hold values from 0.83088 to 13.29408
- shrink_second: float32 [4096, 1024], P('narrow', 'wide'), may hold values from 3.13888 to 49.8528
- gains_second: float32 [2, 1024], replicated, may hold values from 9.232 to 147.712
- shifts_second: float32 [4, 1024], replicated, may hold values from 9.232 to 147.712
- heads_second: float32 [2, 1024], P(None, 'narrow'), may hold values from 9.232 to 147.712
- widen_second: float32 [4096], P('narrow'), may hold values from 0.83088 to 13.29408
Outputs:
- layer_output: float32 [18464, 1024], P(('wide', 'narrow'))
- input_gradient: float32 [18464, 1024], P(('wide', 'narrow'))
- triple_gradient: float32 [1024, 3, 1024], P('wide', None, 'narrow')
- triple_renewed: float32 [1024, 3, 1024], P('wide', None, 'narrow')
- triple_updated: float32 [1024, 3, 1024], P('wide', None, 'narrow')
- output_gradient: float32 [1024, 1024], P('narrow', 'wide')
- output_renewed: float32 [1024, 1024], P('narrow', 'wide')
- output_updated: float32 [1024, 1024], P('narrow', 'wide')
- expand_gradient: float32 [1024, 4096], P('wide', 'narrow')
- expand_renewed: float32 [1024, 4096], P('wide', 'narrow')
- expand_updated: float32 [1024, 4096], P('wide', 'narrow')
- shrink_gradient: float32 [4096, 1024], P('narrow', 'wide')
- shrink_renewed: float32 [4096, 1024], P('narrow', 'wide')
- shrink_updated: float32 [4096, 1024], P('narrow', 'wide')
- gains_gradient: float32 [2, 1024], replicated
- gains_renewed: float32 [2, 1024], replicated
- gains_updated: float32 [2, 1024], replicated
- shifts_gradient: float32 [4, 1024], replicated
- shifts_renewed: float32 [3, 1024], replicated
- leading_renewed: float32 [1024], replicated
- shifts_updated: float32 [4, 1024], replicated
- heads_gradient: float32 [2, 1024], P(None, 'narrow')
- heads_renewed: float32 [2, 1024], P(None, 'narrow')
- heads_updated: float32 [2, 1024], P(None, 'narrow')
- widen_gradient: float32 [4096], P('narrow')
- widen_renewed: float32 [4096], P('narrow')
- widen_updated: float32 [4096], P('narrow')
The draws below stay inside these ranges and needn't reach their ends.
All inputs are finite; a program needn't handle non-finite values.
Results may differ from the reference program's by a relative error of at most 0.019.
Values may be sent and summed in bfloat16 or wider, within the bound.
No kernel may reach another device: no remote copies, remote signals or barrier semaphores. Data moves between devices by JAX's collectives and lax.ppermute only.
A program may use at most 192 MiB of HBM per device.

```python
import math
import jax
import jax.numpy as jnp
from jax import lax

D = 1024
H = 16
FF = 4096
SEQ = 577
STEP = 10
TOKENS = 18464


def block_scale(rng, shape, split, smallest, top_value):
    level, own = 1.0, jax.random.fold_in(rng, 6)
    for axis_at, parts in split:
        steps = jnp.exp(jax.random.uniform(jax.random.fold_in(own, axis_at), (parts,), jnp.float32, smallest / len(split), top_value / len(split)))
        level = level * jnp.repeat(steps, shape[axis_at] // parts).reshape([-1 if axis == axis_at else 1 for axis in range(len(shape))])
    return level


def normal_values(key, extent, scale, bound, pieces=(), held_as=jnp.bfloat16):
    array = jax.random.normal(key, extent, jnp.float32) * scale
    if len(pieces) > 0:
        array = block_scale(key, extent, pieces, -0.22, 0.18) * array
    return jnp.clip(array, min=-bound, max=bound).astype(held_as)


def setup_inputs(seed: int = 0) -> dict:
    key_of = jax.random.split(jax.random.key(seed), 27)
    return {
        "tokens": normal_values(key_of[0], (TOKENS, D), 1.0, 6.0, ((0, 32),), jnp.float32),
        "cotangent": normal_values(key_of[1], (TOKENS, D), 1.0, 6.0, ((0, 32),), jnp.float32),
        "triple_weight": normal_values(key_of[2], (D, 3, D), D ** -0.5, 0.1875, ((0, 8), (2, 4)), jnp.float32),
        "output_weight": normal_values(key_of[3], (D, D), (D * 4 // SEQ) ** -0.5, 2.0, ((0, 4), (1, 8)), jnp.float32),
        "expand_weight": normal_values(key_of[4], (D, FF), D ** -0.5, 0.1875, ((0, 8), (1, 4)), jnp.float32),
        "shrink_weight": normal_values(key_of[5], (FF, D), FF ** -0.5, 0.09375, ((0, 4), (1, 8)), jnp.float32),
        "norm_gains": jnp.clip(1.0 + 0.1 * jax.random.normal(key_of[6], (2, D), jnp.float32), 0.5, 1.5),
        "shift_biases": normal_values(key_of[7], (4, D), 0.1, 0.6, (), jnp.float32),
        "head_biases": normal_values(key_of[8], (2, D), 0.05, 0.3, ((1, 4),), jnp.float32),
        "expand_biases": normal_values(key_of[9], (FF,), 0.1, 0.6, ((0, 4),), jnp.float32),
        "triple_first": normal_values(key_of[10], (D, 3, D), (0.11 * TOKENS ** 0.5), 89.68232, ((0, 8), (2, 4)), jnp.float32),
        "output_first": normal_values(key_of[11], (D, D), (0.013 * TOKENS ** 0.5), 10.59882, ((0, 4), (1, 8)), jnp.float32),
        "expand_first": normal_values(key_of[12], (D, FF), (0.033 * TOKENS ** 0.5), 27.17646, ((0, 8), (1, 4)), jnp.float32),
        "shrink_first": normal_values(key_of[13], (FF, D), (0.064 * TOKENS ** 0.5), 51.635273, ((0, 4), (1, 8)), jnp.float32),
        "gains_first": normal_values(key_of[14], (2, D), (0.11 * TOKENS ** 0.5), 89.68232, (), jnp.float32),
        "shifts_first": normal_values(key_of[15], (4, D), (0.11 * TOKENS ** 0.5), 89.68232, (), jnp.float32),
        "heads_first": normal_values(key_of[16], (2, D), (0.11 * TOKENS ** 0.5), 89.68232, ((1, 4),), jnp.float32),
        "widen_first": normal_values(key_of[17], (FF,), (0.033 * TOKENS ** 0.5), 27.17646, ((0, 4),), jnp.float32),
        "triple_second": jnp.clip(jnp.exp(math.log(147.712) - 2.7725887 * jax.random.uniform(key_of[18], (D, 3, D), jnp.float32) ** block_scale(key_of[18], (D, 3, D), ((0, 8), (2, 4)), -0.2, 0.2)), 9.232, 147.712),
        "output_second": jnp.clip(jnp.exp(math.log(2.21568) - 2.70805 * jax.random.uniform(key_of[19], (D, D), jnp.float32) ** block_scale(key_of[19], (D, D), ((0, 4), (1, 8)), -0.2, 0.2)), 0.147712, 2.21568),
        "expand_second": jnp.clip(jnp.exp(math.log(13.29408) - 2.7725887 * jax.random.uniform(key_of[20], (D, FF), jnp.float32) ** block_scale(key_of[20], (D, FF), ((0, 8), (1, 4)), -0.2, 0.2)), 0.83088, 13.29408),
        "shrink_second": jnp.clip(jnp.exp(math.log(49.8528) - 2.7652086 * jax.random.uniform(key_of[21], (FF, D), jnp.float32) ** block_scale(key_of[21], (FF, D), ((0, 4), (1, 8)), -0.2, 0.2)), 3.13888, 49.8528),
        "gains_second": jnp.clip(jnp.exp(jax.random.uniform(key_of[22], (2, D), jnp.float32, math.log(9.232), math.log(147.712))), 9.232, 147.712),
        "shifts_second": jnp.clip(jnp.exp(jax.random.uniform(key_of[23], (4, D), jnp.float32, math.log(9.232), math.log(147.712))), 9.232, 147.712),
        "heads_second": jnp.clip(jnp.exp(math.log(147.712) - 2.7725887 * jax.random.uniform(key_of[24], (2, D), jnp.float32) ** block_scale(key_of[24], (2, D), ((1, 4),), -0.2, 0.2)), 9.232, 147.712),
        "widen_second": jnp.clip(jnp.exp(math.log(13.29408) - 2.7725887 * jax.random.uniform(key_of[25], (FF,), jnp.float32) ** block_scale(key_of[25], (FF,), ((0, 4),), -0.2, 0.2)), 0.83088, 13.29408),
    }


@jax.custom_vjp
def low(v):
    return lax.optimization_barrier(v.astype(jnp.bfloat16)).astype(jnp.float32)

@jax.custom_vjp
def low_back(v):
    return v

def low_keep(v):
    return (low(v), None)

def low_pass(kept, grad):
    return (grad,)

def back_keep(v):
    return (v, None)

def back_low(kept, grad):
    return (low(grad),)
low.defvjp(low_keep, low_pass)
low_back.defvjp(back_keep, back_low)
norm_eps = 1e-06
beta_first = 0.9
beta_second = 0.999
adam_eps = 1e-08
decay_rate = 0.05
highest = lax.Precision.HIGHEST

def matmul(left, right):
    return jnp.dot(left, right, precision=highest, preferred_element_type=jnp.float32)

def layer_norm(values, gain, shift):
    center = values - lax.optimization_barrier(jnp.mean(values, axis=-1, keepdims=True))
    spread = lax.optimization_barrier(jnp.mean(center * center, axis=-1, keepdims=True))
    return center * lax.rsqrt(spread + norm_eps) * gain + shift

def attend_image(packed):
    queries, keys, values = packed
    scale = 1.0 / math.sqrt(D // H)
    scores = low_back(jnp.einsum('shd,thd->hst', queries, keys, precision=highest) * scale)
    top = lax.optimization_barrier(jnp.max(scores, axis=-1, keepdims=True))
    expon = jnp.exp(scores - top)
    probs = expon / lax.optimization_barrier(jnp.sum(expon, axis=-1, keepdims=True))
    mixed = jnp.einsum('hst,thd->shd', low(probs), values, precision=highest)
    return low_back(low(mixed))

def forward(tokens, triple_weight, output_weight, expand_weight, shrink_weight, norm_gains, shift_biases, head_biases, expand_biases):
    normed = low(layer_norm(tokens, norm_gains[0], shift_biases[0]))
    triple = low_back(jnp.einsum('td,dkc->tkc', normed, low(triple_weight), precision=highest))
    queries = low(triple[:, 0] + head_biases[0])
    keys = low(triple[:, 1])
    values = low(triple[:, 2] + head_biases[1])
    shape_four = (TOKENS // SEQ, SEQ, H, D // H)
    mixed = lax.map(jax.checkpoint(attend_image), (queries.reshape(shape_four), keys.reshape(shape_four), values.reshape(shape_four)))
    mixed = mixed.reshape(TOKENS, D)
    middle = tokens + low_back(matmul(mixed, low(output_weight))) + shift_biases[2]
    normed_two = low(layer_norm(middle, norm_gains[1], shift_biases[1]))
    expanded = low_back(matmul(normed_two, low(expand_weight))) + expand_biases
    active = low(jax.nn.gelu(expanded, approximate=False))
    return middle + low_back(matmul(active, low(shrink_weight))) + shift_biases[3]

def adam_step(weight, grad, first, second, rate, decay):
    first_new = beta_first * first + (1.0 - beta_first) * grad
    second_new = beta_second * second + (1.0 - beta_second) * grad * grad
    first_hat = first_new / (1.0 - beta_first ** STEP)
    second_hat = second_new / (1.0 - beta_second ** STEP)
    updated = weight - rate * (first_hat / (jnp.sqrt(second_hat) + adam_eps) + decay * weight)
    return (second_new, updated)

def reference(tokens, cotangent, triple_weight, output_weight, expand_weight, shrink_weight, norm_gains, shift_biases, head_biases, expand_biases, triple_first, output_first, expand_first, shrink_first, gains_first, shifts_first, heads_first, widen_first, triple_second, output_second, expand_second, shrink_second, gains_second, shifts_second, heads_second, widen_second):
    params = (triple_weight, output_weight, expand_weight, shrink_weight, norm_gains, shift_biases, head_biases, expand_biases)
    firsts = (triple_first, output_first, expand_first, shrink_first, gains_first, shifts_first, heads_first, widen_first)
    seconds = (triple_second, output_second, expand_second, shrink_second, gains_second, shifts_second, heads_second, widen_second)
    rates = (0.1, 1.0, 0.1, 0.05, 1.0, 0.3, 0.2, 0.3)
    decays = (decay_rate, decay_rate, decay_rate, decay_rate, 0.0, 0.0, 0.0, 0.0)
    layer_output, pullback = jax.vjp(forward, tokens, *params)
    grads = pullback(cotangent)
    results = [layer_output, grads[0]]
    for index in range(8):
        renewed, updated = adam_step(params[index], grads[index + 1], firsts[index], seconds[index], rates[index], decays[index])
        if index == 5:
            results.extend([grads[index + 1], renewed[1:], renewed[0], updated])
        else:
            results.extend([grads[index + 1], renewed, updated])
    return (results[0], results[1], results[2], results[3], results[4], results[5], results[6], results[7], results[8], results[9], results[10], results[11], results[12], results[13], results[14], results[15], results[16], results[17], results[18], results[19], results[20], results[21], results[22], results[23], results[24], results[25], results[26])
```

```python
import functools
import math

import jax
import jax.numpy as jnp
from jax import lax
from jax.experimental import pallas as pl
from jax.experimental.pallas import tpu as pltpu
from jax.sharding import PartitionSpec as P

D = 1024
H = 16
SEQ = 577
STEP = 10
HEAD = D // H
LANES = 128
BLOCKS = D // LANES
HALF = D // 2


norm_eps = 1e-06
beta_first = 0.9
beta_second = 0.999
adam_eps = 1e-08
decay_rate = 0.05

low = jnp.bfloat16
full = jnp.float32
big = pltpu.CompilerParams(vmem_limit_bytes=56 * 1024 * 1024)


def adam_step(weight, grad, first, second, rate, decay):
    first_new = beta_first * first + (1.0 - beta_first) * grad
    second_new = beta_second * second + (1.0 - beta_second) * grad * grad
    first_hat = first_new / (1.0 - beta_first**STEP)
    second_hat = second_new / (1.0 - beta_second**STEP)
    updated = weight - rate * (first_hat / (jnp.sqrt(second_hat) + adam_eps) + decay * weight)
    return (second_new, updated)


def dot_nn(left, right):
    return lax.dot_general(left, right, (((1,), (0,)), ((), ())), preferred_element_type=full)


def dot_nt(left, right):
    return lax.dot_general(left, right, (((1,), (1,)), ((), ())), preferred_element_type=full)


def dot_tn(left, right):
    return lax.dot_general(left, right, (((0,), (0,)), ((), ())), preferred_element_type=full)


def lane_block(order, at):
    return pl.ds(pl.multiple_of(order[at] * LANES, LANES), LANES)


def stat(values):
    center = values - jnp.mean(values, axis=-1, keepdims=True)
    inverse = lax.rsqrt(jnp.mean(center * center, axis=-1, keepdims=True) + norm_eps)
    return center * inverse, inverse


def norm_back(values, grad, gain):
    unit, inverse = stat(values)
    scaled = grad * gain
    part = inverse * (
        scaled
        - jnp.mean(scaled, axis=-1, keepdims=True)
        - unit * jnp.mean(scaled * unit, axis=-1, keepdims=True)
    )
    gain_sum = jnp.sum(grad * unit, axis=0, keepdims=True)
    shift_sum = jnp.sum(grad, axis=0, keepdims=True)
    return part, gain_sum, shift_sum


def start_kernel(order, tok, cot, gains, shifts, tok_out, normed, cot_out, cot_low, gains_out, shifts_out, cot_sum):
    values = tok[...]
    mean = jnp.mean(values, axis=-1, keepdims=True)
    center = values - mean
    inverse = lax.rsqrt(jnp.mean(center * center, axis=-1, keepdims=True) + norm_eps)
    cot_sum[...] = jnp.sum(cot[...], axis=0, keepdims=True)
    for at in range(BLOCKS):
        source = lane_block(order, at)
        place = slice(at * LANES, (at + 1) * LANES)
        block = tok[:, source]
        tok_out[:, place] = block
        gain = gains[:, source]
        shift = shifts[:, source]
        gains_out[:, place] = gain
        shifts_out[:, place] = shift
        normed[:, place] = ((block - mean) * inverse * gain[0:1] + shift[0:1]).astype(low)
        other = cot[:, source]
        cot_out[:, place] = other
        cot_low[:, place] = other.astype(low)


def attend_kernel(x, own, twin, bias, packed, mixed, logs):
    value = dot_nn(x[:, :HALF], own[0]) + dot_nn(x[:, HALF:], twin[0]) + bias[0]
    width = value.shape[1] // 3
    value = value.astype(low)
    packed[0] = value
    lane = lax.broadcasted_iota(jnp.int32, (1, LANES), 1)
    scale = 1.0 / math.sqrt(HEAD)
    rows = value.shape[0]
    log_all = jnp.zeros((rows, LANES), full)
    for pair in range(width // LANES):
        cols = slice(pair * LANES, (pair + 1) * LANES)
        query = value[:, cols]
        key = value[:, width + pair * LANES : width + (pair + 1) * LANES]
        val = value[:, 2 * width + pair * LANES : 2 * width + (pair + 1) * LANES]
        outs = []
        for side in range(2):
            keep = jnp.where(lane // HEAD == side, scale, 0.0).astype(low)
            scores = dot_nt(query * keep, key)
            top = jnp.max(scores, axis=-1, keepdims=True)
            expon = jnp.exp(scores - top)
            total = jnp.sum(expon, axis=-1, keepdims=True)
            outs.append(dot_nn(expon.astype(low), val) / total)
            log_all = jnp.where(lane == 2 * pair + side, top + jnp.log(total), log_all)
        mixed[0, :, cols] = jnp.where(lane < HEAD, outs[0], outs[1]).astype(low)
    logs[0] = log_all.T[:8]


def attend(normed, own, twin, bias):
    groups, _, width = own.shape
    rows = normed.shape[0]
    return pl.pallas_call(
        attend_kernel,
        grid=(groups,),
        in_specs=[
            pl.BlockSpec((rows, D), lambda n: (0, 0)),
            pl.BlockSpec((1, HALF, width), lambda n: (n, 0, 0)),
            pl.BlockSpec((1, HALF, width), lambda n: (n, 0, 0)),
            pl.BlockSpec((1, 1, width), lambda n: (n, 0, 0)),
        ],
        out_specs=[
            pl.BlockSpec((1, rows, width), lambda n: (n, 0, 0)),
            pl.BlockSpec((1, rows, width // 3), lambda n: (n, 0, 0)),
            pl.BlockSpec((1, 8, rows), lambda n: (n, 0, 0)),
        ],
        out_shape=[
            jax.ShapeDtypeStruct((groups, rows, width), low),
            jax.ShapeDtypeStruct((groups, rows, width // 3), low),
            jax.ShapeDtypeStruct((groups, 8, rows), full),
        ],
        compiler_params=big,
    )(normed, own, twin, bias)


def attend_back_kernel(grad, own, twin, packed, logs, out, sums):
    upper = (dot_nn(grad[:, :HALF], own[0]) + dot_nn(grad[:, HALF:], twin[0])).astype(low)
    width = upper.shape[1]
    lane = lax.broadcasted_iota(jnp.int32, (1, LANES), 1)
    scale = 1.0 / math.sqrt(HEAD)
    for pair in range(width // LANES):
        cols = slice(pair * LANES, (pair + 1) * LANES)
        query = packed[0, :, cols]
        key = packed[0, :, width + pair * LANES : width + (pair + 1) * LANES]
        val = packed[0, :, 2 * width + pair * LANES : 2 * width + (pair + 1) * LANES]
        up = upper[:, cols]
        parts = []
        for side in range(2):
            head = 2 * pair + side
            inside = lane // HEAD == side
            scores = dot_nt(key * jnp.where(inside, scale, 0.0).astype(low), query)
            probs = jnp.exp(scores - logs[0, head : head + 1, :])
            val_grad = dot_nn(probs.astype(low), up)
            prob_grad = dot_nt(val * jnp.where(inside, 1.0, 0.0).astype(low), up)
            weighted = probs * prob_grad
            score_grad = (weighted - probs * jnp.sum(weighted, axis=0, keepdims=True)).astype(low)
            key_grad = dot_nn(score_grad, query) * scale
            query_grad = dot_tn(score_grad, key) * scale
            parts.append((query_grad, key_grad, val_grad))
        for kind in range(3):
            both = jnp.where(lane < HEAD, parts[0][kind], parts[1][kind])
            start = kind * width + pair * LANES
            out[0, :, start : start + LANES] = both.astype(low)
            if kind != 1:
                sums[0, kind // 2 : kind // 2 + 1, cols] = jnp.sum(both, axis=0, keepdims=True)


def attend_back(grad, own, twin, packed, logs):
    groups, rows, width = packed.shape
    third = width // 3
    return pl.pallas_call(
        attend_back_kernel,
        grid=(groups,),
        in_specs=[
            pl.BlockSpec((rows, D), lambda n: (0, 0)),
            pl.BlockSpec((1, HALF, third), lambda n: (n, 0, 0)),
            pl.BlockSpec((1, HALF, third), lambda n: (n, 0, 0)),
            pl.BlockSpec((1, rows, width), lambda n: (n, 0, 0)),
            pl.BlockSpec((1, 8, rows), lambda n: (n, 0, 0)),
        ],
        out_specs=[
            pl.BlockSpec((1, rows, width), lambda n: (n, 0, 0)),
            pl.BlockSpec((1, 2, third), lambda n: (n, 0, 0)),
        ],
        out_shape=[
            jax.ShapeDtypeStruct((groups, rows, width), low),
            jax.ShapeDtypeStruct((groups, 2, third), full),
        ],
        compiler_params=big,
    )(grad, own, twin, packed, logs)


def middle_kernel(mixed, own, twin, tok, gains, shifts, middle, normed):
    groups = mixed.shape[0]
    for side, weight in enumerate((own, twin)):
        cols = slice(side * HALF, (side + 1) * HALF)
        total = tok[:, cols] + shifts[2:3, cols]
        for n in range(groups):
            total = total + dot_nt(mixed[n], weight[n])
        middle[:, cols] = total
    unit, _ = stat(middle[...])
    normed[...] = (unit * gains[1:2] + shifts[1:2]).astype(low)


def expand_kernel(x, own, twin, bias, active, slope):
    value = dot_nn(x[:, :HALF], own[0]) + dot_nn(x[:, HALF:], twin[0]) + bias[0]
    phi = 0.5 * (1.0 + lax.erf(value * math.sqrt(0.5)))
    active[0] = (value * phi).astype(low)
    slope[0] = (phi + value * (jnp.exp(-0.5 * value * value) * (1.0 / math.sqrt(2.0 * math.pi)))).astype(low)


def expand(normed, own, twin, bias):
    groups, _, width = own.shape
    rows = normed.shape[0]
    block = pl.BlockSpec((1, rows, width), lambda n: (n, 0, 0))
    shape = jax.ShapeDtypeStruct((groups, rows, width), low)
    return pl.pallas_call(
        expand_kernel,
        grid=(groups,),
        in_specs=[
            pl.BlockSpec((rows, D), lambda n: (0, 0)),
            pl.BlockSpec((1, HALF, width), lambda n: (n, 0, 0)),
            pl.BlockSpec((1, HALF, width), lambda n: (n, 0, 0)),
            pl.BlockSpec((1, 1, width), lambda n: (n, 0, 0)),
        ],
        out_specs=[block, block],
        out_shape=[shape, shape],
        compiler_params=big,
    )(normed, own, twin, bias)


def shrink_kernel(order, active, own, twin, middle, shifts, out, total):
    n = pl.program_id(0)

    @pl.when(n == 0)
    def _():
        total[...] = middle[...] + shifts[3:4]

    total[:, :HALF] += dot_nt(active[0], own[0])
    total[:, HALF:] += dot_nt(active[0], twin[0])

    @pl.when(n == pl.num_programs(0) - 1)
    def _():
        for at in range(BLOCKS):
            out[:, lane_block(order, at)] = total[:, at * LANES : (at + 1) * LANES]


def shrink(order, active, own, twin, middle, shifts):
    groups, rows, width = active.shape
    return pl.pallas_call(
        shrink_kernel,
        grid_spec=pltpu.PrefetchScalarGridSpec(
            num_scalar_prefetch=1,
            grid=(groups,),
            in_specs=[
                pl.BlockSpec((1, rows, width), lambda n, s: (n, 0, 0)),
                pl.BlockSpec((1, HALF, width), lambda n, s: (n, 0, 0)),
                pl.BlockSpec((1, HALF, width), lambda n, s: (n, 0, 0)),
                pl.BlockSpec((rows, D), lambda n, s: (0, 0)),
                pl.BlockSpec((4, D), lambda n, s: (0, 0)),
            ],
            out_specs=pl.BlockSpec((rows, D), lambda n, s: (0, 0)),
            scratch_shapes=[pltpu.VMEM((rows, D), full)],
        ),
        out_shape=jax.ShapeDtypeStruct((rows, D), full),
        compiler_params=big,
    )(order, active, own, twin, middle, shifts)


def expand_back_kernel(grad, own, twin, slope, out, sums):
    value = dot_nn(grad[:, :HALF], own[0]) + dot_nn(grad[:, HALF:], twin[0])
    value = value * slope[0].astype(full)
    sums[0] = jnp.sum(value, axis=0, keepdims=True)
    out[0] = value.astype(low)


def expand_back(grad, own, twin, slope):
    groups, rows, width = slope.shape
    block = pl.BlockSpec((1, rows, width), lambda n: (n, 0, 0))
    return pl.pallas_call(
        expand_back_kernel,
        grid=(groups,),
        in_specs=[
            pl.BlockSpec((rows, D), lambda n: (0, 0)),
            pl.BlockSpec((1, HALF, width), lambda n: (n, 0, 0)),
            pl.BlockSpec((1, HALF, width), lambda n: (n, 0, 0)),
            block,
        ],
        out_specs=[block, pl.BlockSpec((1, 1, width), lambda n: (n, 0, 0))],
        out_shape=[
            jax.ShapeDtypeStruct((groups, rows, width), low),
            jax.ShapeDtypeStruct((groups, 1, width), full),
        ],
        compiler_params=big,
    )(grad, own, twin, slope)


def outer_kernel(x, inner, own, twin):
    twin[0] = dot_tn(x[:, HALF:], inner[0]).astype(low)
    own[0] = dot_tn(x[:, :HALF], inner[0]).astype(low)


def outer(x, inner):
    groups, rows, width = inner.shape
    block = pl.BlockSpec((1, HALF, width), lambda n: (n, 0, 0))
    shape = jax.ShapeDtypeStruct((groups, HALF, width), low)
    return pl.pallas_call(
        outer_kernel,
        grid=(groups,),
        in_specs=[
            pl.BlockSpec((rows, D), lambda n: (0, 0)),
            pl.BlockSpec((1, rows, width), lambda n: (n, 0, 0)),
        ],
        out_specs=[block, block],
        out_shape=[shape, shape],
        compiler_params=big,
    )(x, inner)


def norm_two_kernel(order, inner, own, twin, middle, cot, gains, out, out_low, sums, total):
    n = pl.program_id(0)

    @pl.when(n == 0)
    def _():
        total[...] = jnp.zeros_like(total)

    total[:, :HALF] += dot_nt(inner[0], own[0])
    total[:, HALF:] += dot_nt(inner[0], twin[0])

    @pl.when(n == pl.num_programs(0) - 1)
    def _():
        part, gain_sum, shift_sum = norm_back(middle[...], total[...], gains[1:2])
        grad = cot[...] + part
        out[...] = grad
        out_low[...] = grad.astype(low)
        grad_sum = jnp.sum(grad, axis=0, keepdims=True)
        for at in range(BLOCKS):
            place = lane_block(order, at)
            cols = slice(at * LANES, (at + 1) * LANES)
            sums[0:1, place] = gain_sum[:, cols]
            sums[1:2, place] = shift_sum[:, cols]
            sums[2:3, place] = grad_sum[:, cols]


def norm_one_kernel(order, inner, own, twin, tok, grad, gains, out, sums, total):
    n = pl.program_id(0)

    @pl.when(n == 0)
    def _():
        total[...] = jnp.zeros_like(total)

    total[:, :HALF] += dot_nt(inner[0], own[0])
    total[:, HALF:] += dot_nt(inner[0], twin[0])

    @pl.when(n == pl.num_programs(0) - 1)
    def _():
        part, gain_sum, shift_sum = norm_back(tok[...], total[...], gains[0:1])
        result = grad[...] + part
        for at in range(BLOCKS):
            place = lane_block(order, at)
            cols = slice(at * LANES, (at + 1) * LANES)
            out[:, place] = result[:, cols]
            sums[0:1, place] = gain_sum[:, cols]
            sums[1:2, place] = shift_sum[:, cols]


def norm_call(kernel, order, inner, own, twin, values, grad, gains, with_low):
    groups, rows, width = inner.shape
    whole = pl.BlockSpec((rows, D), lambda n, s: (0, 0))
    part = pl.BlockSpec((1, HALF, width), lambda n, s: (n, 0, 0))
    low_spec = [whole] if with_low else []
    low_shape = [jax.ShapeDtypeStruct((rows, D), low)] if with_low else []
    count = 3 if with_low else 2
    return pl.pallas_call(
        kernel,
        grid_spec=pltpu.PrefetchScalarGridSpec(
            num_scalar_prefetch=1,
            grid=(groups,),
            in_specs=[
                pl.BlockSpec((1, rows, width), lambda n, s: (n, 0, 0)),
                part,
                part,
                whole,
                whole,
                pl.BlockSpec((2, D), lambda n, s: (0, 0)),
            ],
            out_specs=[whole] + low_spec + [pl.BlockSpec((count, D), lambda n, s: (0, 0))],
            scratch_shapes=[pltpu.VMEM((rows, D), full)],
        ),
        out_shape=[jax.ShapeDtypeStruct((rows, D), full)] + low_shape + [jax.ShapeDtypeStruct((count, D), full)],
        compiler_params=big,
    )(order, inner, own, twin, values, grad, gains)


def swap(values, bit, size):
    return lax.ppermute(values, "wide", [(at, at ^ bit) for at in range(size)])


def gather_weight(block, wide):
    groups = lax.all_gather(block, "narrow", axis=0, tiled=False)
    if wide != 8:
        whole = lax.all_gather(groups, "wide", axis=1, tiled=True)
        return whole[:, :HALF], whole[:, HALF:]
    over_x = swap(groups, 2, wide)
    over_y = swap(groups, 4, wide)
    cut = groups.shape[0] // 2
    first = swap(over_x[:cut], 4, wide)
    second = swap(over_y[cut:], 2, wide)
    own = jnp.concatenate([groups, over_x, over_y, jnp.concatenate([first, second], axis=0)], axis=1)
    return own, swap(own, 1, wide)


def scatter_grad(own, twin, wide):
    if wide != 8:
        whole = jnp.concatenate([own, twin], axis=1)
        part = lax.psum_scatter(whole, "wide", scatter_dimension=1, tiled=True)
        return lax.psum_scatter(part, "narrow", scatter_dimension=0, tiled=False).astype(full)
    groups, _, width = own.shape
    cut = groups // 2
    rows = HALF // 4
    both = own.astype(full) + swap(twin, 1, wide).astype(full)
    mine, to_x, to_y, far = (both[:, at * rows : (at + 1) * rows] for at in range(4))
    far = far.astype(low)
    from_y = swap(far[:cut], 4, wide).astype(full)
    from_x = swap(far[cut:], 2, wide).astype(full)
    send_x = jnp.concatenate([to_x[:cut] + from_y, to_x[cut:]], axis=0).astype(low)
    send_y = jnp.concatenate([to_y[:cut], to_y[cut:] + from_x], axis=0).astype(low)
    part = mine + swap(send_x, 2, wide).astype(full) + swap(send_y, 4, wide).astype(full)
    return lax.psum_scatter(part.astype(low), "narrow", scatter_dimension=0, tiled=False).astype(full)


def shards(
    tokens,
    cotangent,
    triple_weight,
    output_weight,
    expand_weight,
    shrink_weight,
    norm_gains,
    shift_biases,
    head_biases,
    expand_biases,
    triple_first,
    output_first,
    expand_first,
    shrink_first,
    gains_first,
    shifts_first,
    heads_first,
    widen_first,
    triple_second,
    output_second,
    expand_second,
    shrink_second,
    gains_second,
    shifts_second,
    heads_second,
    widen_second,
    *,
    wide,
    narrow,
):
    rows = tokens.shape[0]
    local = head_biases.shape[1]
    hidden = expand_biases.shape[0]
    depth = triple_weight.shape[0]
    place = lax.axis_index("wide")
    at_narrow = lax.axis_index("narrow")
    if wide == 8:
        order = jnp.bitwise_xor(place, jnp.array([0, 2, 4, 6, 1, 3, 5, 7], jnp.int32)).astype(jnp.int32)
    else:
        order = jnp.arange(BLOCKS, dtype=jnp.int32)

    triple_block = triple_weight.reshape(depth, 3 * local).astype(low)
    biases = lax.all_gather(
        jnp.concatenate([head_biases[0], head_biases[1], expand_biases]), "narrow", axis=0, tiled=False
    )
    triple_own, triple_twin = gather_weight(triple_block, wide)
    output_own, output_twin = gather_weight(output_weight.astype(low).T, wide)
    expand_own, expand_twin = gather_weight(expand_weight.astype(low), wide)
    shrink_own, shrink_twin = gather_weight(shrink_weight.astype(low).T, wide)
    triple_bias = jnp.concatenate(
        [biases[:, :local], jnp.zeros((narrow, local), full), biases[:, local : 2 * local]], axis=1
    )[:, None]
    widen_bias = biases[:, 2 * local :][:, None]

    whole = pl.BlockSpec((rows, D), lambda: (0, 0))
    wide_full = jax.ShapeDtypeStruct((rows, D), full)
    wide_low = jax.ShapeDtypeStruct((rows, D), low)
    tok, normed, cot, cot_low, gains, shifts, cot_sum = pl.pallas_call(
        start_kernel,
        in_specs=[pl.BlockSpec(memory_space=pltpu.SMEM)] + [pl.BlockSpec(memory_space=pltpu.VMEM)] * 4,
        out_shape=[
            wide_full,
            wide_low,
            wide_full,
            wide_low,
            jax.ShapeDtypeStruct((2, D), full),
            jax.ShapeDtypeStruct((4, D), full),
            jax.ShapeDtypeStruct((1, D), full),
        ],
        compiler_params=big,
    )(order, tokens, cotangent, norm_gains, shift_biases)

    packed, mixed, logs = attend(normed, triple_own, triple_twin, triple_bias)
    middle, normed_two = pl.pallas_call(
        middle_kernel,
        out_shape=[wide_full, wide_low],
        compiler_params=big,
    )(mixed, output_own, output_twin, tok, gains, shifts)
    active, slope = expand(normed_two, expand_own, expand_twin, widen_bias)
    shrink_grads = outer(cot_low, active)
    expanded_low, widen_sum = expand_back(cot_low, shrink_own, shrink_twin, slope)
    expand_grads = outer(normed_two, expanded_low)
    layer_output = shrink(order, active, shrink_own, shrink_twin, middle, shifts)
    middle_grad, middle_low, two_sums = norm_call(
        norm_two_kernel, order, expanded_low, expand_own, expand_twin, middle, cot, gains, True
    )
    output_grads = outer(middle_low, mixed)
    triple_low, head_sums = attend_back(middle_low, output_own, output_twin, packed, logs)
    triple_grads = outer(normed, triple_low)
    input_gradient, one_sums = norm_call(
        norm_one_kernel, order, triple_low, triple_own, triple_twin, tok, middle_grad, gains, False
    )

    shrink_gradient = scatter_grad(*shrink_grads, wide).T
    expand_gradient = scatter_grad(*expand_grads, wide)
    output_gradient = scatter_grad(*output_grads, wide).T
    triple_gradient = scatter_grad(*triple_grads, wide).reshape(depth, 3, local)

    small = jnp.concatenate(
        [
            one_sums[0:1],
            two_sums[0:1],
            one_sums[1:2],
            two_sums[1:3],
            cot_sum,
            head_sums.transpose(1, 0, 2).reshape(2, D),
            widen_sum.reshape(-1, D),
        ],
        axis=0,
    )
    small = lax.psum(small, ("wide", "narrow"))
    gains_gradient = small[0:2]
    shifts_gradient = small[2:6]
    heads_gradient = lax.dynamic_slice_in_dim(small[6:8], at_narrow * local, local, 1)
    widen_gradient = lax.dynamic_slice_in_dim(small[8:].reshape(-1), at_narrow * hidden, hidden, 0)

    params = (
        triple_weight,
        output_weight,
        expand_weight,
        shrink_weight,
        norm_gains,
        shift_biases,
        head_biases,
        expand_biases,
    )
    gradients = (
        triple_gradient,
        output_gradient,
        expand_gradient,
        shrink_gradient,
        gains_gradient,
        shifts_gradient,
        heads_gradient,
        widen_gradient,
    )
    firsts = (
        triple_first,
        output_first,
        expand_first,
        shrink_first,
        gains_first,
        shifts_first,
        heads_first,
        widen_first,
    )
    seconds = (
        triple_second,
        output_second,
        expand_second,
        shrink_second,
        gains_second,
        shifts_second,
        heads_second,
        widen_second,
    )
    rates = (0.1, 1.0, 0.1, 0.05, 1.0, 0.3, 0.2, 0.3)
    decays = (decay_rate, decay_rate, decay_rate, decay_rate, 0.0, 0.0, 0.0, 0.0)
    results = [layer_output, input_gradient]
    for index in range(8):
        renewed, updated = adam_step(
            params[index],
            gradients[index],
            firsts[index],
            seconds[index],
            rates[index],
            decays[index],
        )
        if index == 5:
            results.extend([gradients[index], renewed[1:], renewed[0], updated])
        else:
            results.extend([gradients[index], renewed, updated])
    return tuple(results)


def solution(mesh):
    placed = (
        P(("wide", "narrow"), None),
        P(("wide", "narrow"), None),
        P("wide", None, "narrow"),
        P("narrow", "wide"),
        P("wide", "narrow"),
        P("narrow", "wide"),
        P(),
        P(),
        P(None, "narrow"),
        P("narrow"),
        P("wide", None, "narrow"),
        P("narrow", "wide"),
        P("wide", "narrow"),
        P("narrow", "wide"),
        P(),
        P(),
        P(None, "narrow"),
        P("narrow"),
        P("wide", None, "narrow"),
        P("narrow", "wide"),
        P("wide", "narrow"),
        P("narrow", "wide"),
        P(),
        P(),
        P(None, "narrow"),
        P("narrow"),
    )
    matrices = (P("wide", None, "narrow"), P("narrow", "wide"), P("wide", "narrow"), P("narrow", "wide"))
    outs = [P(("wide", "narrow"), None), P(("wide", "narrow"), None)]
    for spec in matrices:
        outs.extend([spec] * 3)
    outs.extend([P()] * 7)
    outs.extend([P(None, "narrow")] * 3)
    outs.extend([P("narrow")] * 3)
    return jax.shard_map(
        functools.partial(shards, wide=mesh.shape["wide"], narrow=mesh.shape["narrow"]),
        mesh=mesh,
        in_specs=placed,
        out_specs=tuple(outs),
        check_vma=False,
    )
```

```python
import functools
import math

import jax
import jax.numpy as jnp
from jax import lax
from jax.experimental import pallas as pl
from jax.experimental.pallas import tpu as pltpu
from jax.sharding import PartitionSpec as P

D = 1024
H = 16
SEQ = 577
STEP = 10
HEAD = D // H
LANES = 128
BLOCKS = D // LANES
HALF = D // 2


norm_eps = 1e-06
beta_first = 0.9
beta_second = 0.999
adam_eps = 1e-08
decay_rate = 0.05

low = jnp.bfloat16
full = jnp.float32
big = pltpu.CompilerParams(vmem_limit_bytes=56 * 1024 * 1024)


def adam_step(weight, grad, first, second, rate, decay):
    first_new = beta_first * first + (1.0 - beta_first) * grad
    second_new = beta_second * second + (1.0 - beta_second) * grad * grad
    first_hat = first_new / (1.0 - beta_first**STEP)
    second_hat = second_new / (1.0 - beta_second**STEP)
    updated = weight - rate * (first_hat / (jnp.sqrt(second_hat) + adam_eps) + decay * weight)
    return (second_new, updated)


def dot_nn(left, right):
    return lax.dot_general(left, right, (((1,), (0,)), ((), ())), preferred_element_type=full)


def dot_nt(left, right):
    return lax.dot_general(left, right, (((1,), (1,)), ((), ())), preferred_element_type=full)


def dot_tn(left, right):
    return lax.dot_general(left, right, (((0,), (0,)), ((), ())), preferred_element_type=full)


def lane_block(order, at):
    return pl.ds(pl.multiple_of(order[at] * LANES, LANES), LANES)


def stat(values):
    center = values - jnp.mean(values, axis=-1, keepdims=True)
    inverse = lax.rsqrt(jnp.mean(center * center, axis=-1, keepdims=True) + norm_eps)
    return center * inverse, inverse


def norm_back(values, grad, gain):
    unit, inverse = stat(values)
    scaled = grad * gain
    part = inverse * (
        scaled
        - jnp.mean(scaled, axis=-1, keepdims=True)
        - unit * jnp.mean(scaled * unit, axis=-1, keepdims=True)
    )
    gain_sum = jnp.sum(grad * unit, axis=0, keepdims=True)
    shift_sum = jnp.sum(grad, axis=0, keepdims=True)
    return part, gain_sum, shift_sum


def start_kernel(order, tok, cot, gains, shifts, tok_out, normed, cot_out, cot_low, gains_out, shifts_out, cot_sum):
    values = tok[...]
    mean = jnp.mean(values, axis=-1, keepdims=True)
    center = values - mean
    inverse = lax.rsqrt(jnp.mean(center * center, axis=-1, keepdims=True) + norm_eps)
    cot_sum[...] = jnp.sum(cot[...], axis=0, keepdims=True)
    for at in range(BLOCKS):
        source = lane_block(order, at)
        place = slice(at * LANES, (at + 1) * LANES)
        block = tok[:, source]
        tok_out[:, place] = block
        gain = gains[:, source]
        shift = shifts[:, source]
        gains_out[:, place] = gain
        shifts_out[:, place] = shift
        normed[:, place] = ((block - mean) * inverse * gain[0:1] + shift[0:1]).astype(low)
        other = cot[:, source]
        cot_out[:, place] = other
        cot_low[:, place] = other.astype(low)


def piece_specs(pieces, width, lane=0):
    groups = pieces[0].shape[0]
    cut = groups // 2
    shape = (1, pieces[0].shape[1], width)
    same = pl.BlockSpec(shape, lambda n, *s: (n, 0, lane))
    first = pl.BlockSpec(shape, lambda n, *s: (jnp.minimum(n, cut - 1), 0, lane))
    second = pl.BlockSpec(shape, lambda n, *s: (jnp.maximum(n - cut, 0), 0, lane))
    return [same, same, same, first, second]


def assemble(refs, groups):
    near = [ref[0] for ref in refs[:3]]
    far = jnp.where(pl.program_id(0) < groups // 2, refs[3][0], refs[4][0])
    return jnp.concatenate(near + [far], axis=0)


def whole_spec(*shape):
    return pl.BlockSpec(shape, lambda n, *s: (0,) * len(shape))


def group_spec(*shape):
    return pl.BlockSpec((1,) + shape, lambda n, *s: (n,) + (0,) * len(shape))


def grouped(kernel, groups, ins, outs, out_shapes, args, scratch=(), prefetch=0):
    return pl.pallas_call(
        kernel,
        grid_spec=pltpu.PrefetchScalarGridSpec(
            num_scalar_prefetch=prefetch,
            grid=(groups,),
            in_specs=ins,
            out_specs=outs,
            scratch_shapes=list(scratch),
        ),
        out_shape=out_shapes,
        compiler_params=big,
    )(*args)


def struct(shape, dtype):
    return jax.ShapeDtypeStruct(shape, dtype)


def attend_kernel(groups, *refs):
    x, bias = refs[:2]
    own, twin = refs[2:7], refs[7:12]
    packed, mixed, logs = refs[12:]
    value = dot_nn(x[:, :HALF], assemble(own, groups)) + dot_nn(x[:, HALF:], assemble(twin, groups)) + bias[0]
    width = value.shape[1] // 3
    value = value.astype(low)
    packed[0] = value
    lane = lax.broadcasted_iota(jnp.int32, (1, LANES), 1)
    scale = 1.0 / math.sqrt(HEAD)
    rows = value.shape[0]
    log_all = jnp.zeros((rows, LANES), full)
    for pair in range(width // LANES):
        cols = slice(pair * LANES, (pair + 1) * LANES)
        query = value[:, cols]
        key = value[:, width + pair * LANES : width + (pair + 1) * LANES]
        val = value[:, 2 * width + pair * LANES : 2 * width + (pair + 1) * LANES]
        outs = []
        for side in range(2):
            keep = jnp.where(lane // HEAD == side, scale, 0.0).astype(low)
            scores = dot_nt(query * keep, key)
            top = jnp.max(scores, axis=-1, keepdims=True)
            expon = jnp.exp(scores - top)
            total = jnp.sum(expon, axis=-1, keepdims=True)
            outs.append(dot_nn(expon.astype(low), val) / total)
            log_all = jnp.where(lane == 2 * pair + side, top + jnp.log(total), log_all)
        mixed[0, :, cols] = jnp.where(lane < HEAD, outs[0], outs[1]).astype(low)
    logs[0] = log_all.T[:8]


def attend(normed, bias, own, twin):
    groups, _, width = bias.shape
    rows = normed.shape[0]
    return grouped(
        functools.partial(attend_kernel, groups),
        groups,
        [whole_spec(rows, D), group_spec(1, width)] + piece_specs(own, width) + piece_specs(twin, width),
        [group_spec(rows, width), group_spec(rows, width // 3), group_spec(8, rows)],
        [struct((groups, rows, width), low), struct((groups, rows, width // 3), low), struct((groups, 8, rows), full)],
        (normed, bias, *own, *twin),
    )


def attend_back_kernel(groups, *refs):
    grad, packed, logs = refs[:3]
    own, twin = refs[3:8], refs[8:13]
    out, sums = refs[13:]
    upper = (dot_nn(grad[:, :HALF], assemble(own, groups)) + dot_nn(grad[:, HALF:], assemble(twin, groups))).astype(low)
    width = upper.shape[1]
    lane = lax.broadcasted_iota(jnp.int32, (1, LANES), 1)
    scale = 1.0 / math.sqrt(HEAD)
    for pair in range(width // LANES):
        cols = slice(pair * LANES, (pair + 1) * LANES)
        query = packed[0, :, cols]
        key = packed[0, :, width + pair * LANES : width + (pair + 1) * LANES]
        val = packed[0, :, 2 * width + pair * LANES : 2 * width + (pair + 1) * LANES]
        up = upper[:, cols]
        parts = []
        for side in range(2):
            head = 2 * pair + side
            inside = lane // HEAD == side
            scores = dot_nt(key * jnp.where(inside, scale, 0.0).astype(low), query)
            probs = jnp.exp(scores - logs[0, head : head + 1, :])
            val_grad = dot_nn(probs.astype(low), up)
            prob_grad = dot_nt(val * jnp.where(inside, 1.0, 0.0).astype(low), up)
            weighted = probs * prob_grad
            score_grad = (weighted - probs * jnp.sum(weighted, axis=0, keepdims=True)).astype(low)
            key_grad = dot_nn(score_grad, query) * scale
            query_grad = dot_tn(score_grad, key) * scale
            parts.append((query_grad, key_grad, val_grad))
        for kind in range(3):
            both = jnp.where(lane < HEAD, parts[0][kind], parts[1][kind])
            start = kind * width + pair * LANES
            out[0, :, start : start + LANES] = both.astype(low)
            if kind != 1:
                sums[0, kind // 2 : kind // 2 + 1, cols] = jnp.sum(both, axis=0, keepdims=True)


def attend_back(grad, packed, logs, own, twin, lane):
    groups, rows, width = packed.shape
    third = width // 3
    return grouped(
        functools.partial(attend_back_kernel, groups),
        groups,
        [whole_spec(rows, D), group_spec(rows, width), group_spec(8, rows)]
        + piece_specs(own, third, lane)
        + piece_specs(twin, third, lane),
        [group_spec(rows, width), group_spec(2, third)],
        [struct((groups, rows, width), low), struct((groups, 2, third), full)],
        (grad, packed, logs, *own, *twin),
    )


def add_parts(groups, inner, own, twin, total):
    total[:, :HALF] += dot_nt(inner[0], assemble(own, groups))
    total[:, HALF:] += dot_nt(inner[0], assemble(twin, groups))


def middle_kernel(groups, *refs):
    mixed, tok, gains, shifts = refs[:4]
    own, twin = refs[4:9], refs[9:14]
    middle, normed, total = refs[14:]
    n = pl.program_id(0)

    @pl.when(n == 0)
    def _():
        total[...] = tok[...] + shifts[2:3]

    add_parts(groups, mixed, own, twin, total)

    @pl.when(n == groups - 1)
    def _():
        values = total[...]
        middle[...] = values
        unit, _ = stat(values)
        normed[...] = (unit * gains[1:2] + shifts[1:2]).astype(low)


def middle_call(mixed, tok, gains, shifts, own, twin, lane):
    groups, rows, width = mixed.shape
    return grouped(
        functools.partial(middle_kernel, groups),
        groups,
        [group_spec(rows, width), whole_spec(rows, D), whole_spec(2, D), whole_spec(4, D)]
        + piece_specs(own, width, lane)
        + piece_specs(twin, width, lane),
        [whole_spec(rows, D), whole_spec(rows, D)],
        [struct((rows, D), full), struct((rows, D), low)],
        (mixed, tok, gains, shifts, *own, *twin),
        scratch=[pltpu.VMEM((rows, D), full)],
    )


def expand_kernel(groups, *refs):
    x, bias = refs[:2]
    own, twin = refs[2:7], refs[7:12]
    active, slope = refs[12:]
    value = dot_nn(x[:, :HALF], assemble(own, groups)) + dot_nn(x[:, HALF:], assemble(twin, groups)) + bias[0]
    phi = 0.5 * (1.0 + lax.erf(value * math.sqrt(0.5)))
    active[0] = (value * phi).astype(low)
    slope[0] = (phi + value * (jnp.exp(-0.5 * value * value) * (1.0 / math.sqrt(2.0 * math.pi)))).astype(low)


def expand(normed, bias, own, twin):
    groups, rows, width = bias.shape[0], normed.shape[0], bias.shape[2]
    shape = struct((groups, rows, width), low)
    return grouped(
        functools.partial(expand_kernel, groups),
        groups,
        [whole_spec(rows, D), group_spec(1, width)] + piece_specs(own, width) + piece_specs(twin, width),
        [group_spec(rows, width)] * 2,
        [shape, shape],
        (normed, bias, *own, *twin),
    )


def shrink_kernel(groups, order, *refs):
    active, middle, shifts = refs[:3]
    own, twin = refs[3:8], refs[8:13]
    out, total = refs[13:]
    n = pl.program_id(0)

    @pl.when(n == 0)
    def _():
        total[...] = middle[...] + shifts[3:4]

    add_parts(groups, active, own, twin, total)

    @pl.when(n == groups - 1)
    def _():
        for at in range(BLOCKS):
            out[:, lane_block(order, at)] = total[:, at * LANES : (at + 1) * LANES]


def shrink(order, active, middle, shifts, own, twin):
    groups, rows, width = active.shape
    return grouped(
        functools.partial(shrink_kernel, groups),
        groups,
        [group_spec(rows, width), whole_spec(rows, D), whole_spec(4, D)]
        + piece_specs(own, width)
        + piece_specs(twin, width),
        whole_spec(rows, D),
        struct((rows, D), full),
        (order, active, middle, shifts, *own, *twin),
        scratch=[pltpu.VMEM((rows, D), full)],
        prefetch=1,
    )


def expand_back_kernel(groups, *refs):
    grad, slope = refs[:2]
    own, twin = refs[2:7], refs[7:12]
    out, sums = refs[12:]
    value = dot_nn(grad[:, :HALF], assemble(own, groups)) + dot_nn(grad[:, HALF:], assemble(twin, groups))
    value = value * slope[0].astype(full)
    sums[0] = jnp.sum(value, axis=0, keepdims=True)
    out[0] = value.astype(low)


def expand_back(grad, slope, own, twin):
    groups, rows, width = slope.shape
    return grouped(
        functools.partial(expand_back_kernel, groups),
        groups,
        [whole_spec(rows, D), group_spec(rows, width)] + piece_specs(own, width) + piece_specs(twin, width),
        [group_spec(rows, width), group_spec(1, width)],
        [struct((groups, rows, width), low), struct((groups, 1, width), full)],
        (grad, slope, *own, *twin),
    )


def outer_twin_kernel(x, inner, out):
    out[0] = dot_tn(x[...], inner[0]).astype(low)


def outer_twin(x, inner):
    groups, rows, width = inner.shape
    return grouped(
        outer_twin_kernel,
        groups,
        [pl.BlockSpec((rows, HALF), lambda n: (0, 1)), group_spec(rows, width)],
        group_spec(HALF, width),
        struct((groups, HALF, width), low),
        (x, inner),
    )


def outer_own_kernel(groups, x, inner, other, mine, to_x, to_y, far_first, far_second):
    value = (dot_tn(x[...], inner[0]) + other[0].astype(full)).astype(low)
    rows = HALF // 4
    mine[0] = value[:rows]
    to_x[0] = value[rows : 2 * rows]
    to_y[0] = value[2 * rows : 3 * rows]
    n = pl.program_id(0)

    @pl.when(n < groups // 2)
    def _():
        far_first[0] = value[3 * rows :]

    @pl.when(n >= groups // 2)
    def _():
        far_second[0] = value[3 * rows :]


def outer_own(x, inner, other):
    groups, rows, width = inner.shape
    near = struct((groups, HALF // 4, width), low)
    far = struct((groups // 2, HALF // 4, width), low)
    shapes = [near, near, near, far, far]
    return grouped(
        functools.partial(outer_own_kernel, groups),
        groups,
        [pl.BlockSpec((rows, HALF), lambda n: (0, 0)), group_spec(rows, width), group_spec(HALF, width)],
        piece_specs(shapes, width),
        shapes,
        (x, inner, other),
    )


def norm_two_kernel(groups, order, *refs):
    inner, middle, cot, gains = refs[:4]
    own, twin = refs[4:9], refs[9:14]
    out, out_low, sums, total = refs[14:]
    n = pl.program_id(0)

    @pl.when(n == 0)
    def _():
        total[...] = jnp.zeros_like(total)

    add_parts(groups, inner, own, twin, total)

    @pl.when(n == groups - 1)
    def _():
        part, gain_sum, shift_sum = norm_back(middle[...], total[...], gains[1:2])
        grad = cot[...] + part
        out[...] = grad
        out_low[...] = grad.astype(low)
        grad_sum = jnp.sum(grad, axis=0, keepdims=True)
        for at in range(BLOCKS):
            place = lane_block(order, at)
            cols = slice(at * LANES, (at + 1) * LANES)
            sums[0:1, place] = gain_sum[:, cols]
            sums[1:2, place] = shift_sum[:, cols]
            sums[2:3, place] = grad_sum[:, cols]


def norm_one_kernel(groups, order, *refs):
    inner, tok, grad, gains = refs[:4]
    own, twin = refs[4:9], refs[9:14]
    out, sums, total = refs[14:]
    n = pl.program_id(0)

    @pl.when(n == 0)
    def _():
        total[...] = jnp.zeros_like(total)

    add_parts(groups, inner, own, twin, total)

    @pl.when(n == groups - 1)
    def _():
        part, gain_sum, shift_sum = norm_back(tok[...], total[...], gains[0:1])
        result = grad[...] + part
        for at in range(BLOCKS):
            place = lane_block(order, at)
            cols = slice(at * LANES, (at + 1) * LANES)
            out[:, place] = result[:, cols]
            sums[0:1, place] = gain_sum[:, cols]
            sums[1:2, place] = shift_sum[:, cols]


def norm_call(kernel, order, inner, values, grad, gains, own, twin, with_low):
    groups, rows, width = inner.shape
    whole = whole_spec(rows, D)
    count = 3 if with_low else 2
    return grouped(
        functools.partial(kernel, groups),
        groups,
        [group_spec(rows, width), whole, whole, whole_spec(2, D)] + piece_specs(own, width) + piece_specs(twin, width),
        [whole] + ([whole] if with_low else []) + [whole_spec(count, D)],
        [struct((rows, D), full)] + ([struct((rows, D), low)] if with_low else []) + [struct((count, D), full)],
        (order, inner, values, grad, gains, *own, *twin),
        scratch=[pltpu.VMEM((rows, D), full)],
        prefetch=1,
    )


def swap(values, bit):
    return lax.ppermute(values, "wide", [(at, at ^ bit) for at in range(8)])


def turn(values, step):
    return lax.ppermute(values, "narrow", [(at, (at + step) % 4) for at in range(4)])


def cross(values, bit):
    return lax.ppermute(values, "narrow", [(at, at ^ bit) for at in range(4)])


def fence(*values):
    return lax.optimization_barrier(values)


def plain_gather(block):
    groups = lax.all_gather(block, "narrow", axis=0, tiled=False)
    whole = lax.all_gather(groups, "wide", axis=1, tiled=True)
    rows, cut = HALF // 4, whole.shape[0] // 2
    sides = []
    for side in range(2):
        parts = [whole[:, side * HALF + at * rows : side * HALF + (at + 1) * rows] for at in range(4)]
        sides.append((*parts[:3], parts[3][:cut], parts[3][cut:]))
    return tuple(sides)


def plain_scatter(pieces, twin):
    far = jnp.concatenate(pieces[3:], axis=0)
    whole = jnp.concatenate([*pieces[:3], far, twin], axis=1)
    part = lax.psum_scatter(whole, "wide", scatter_dimension=1, tiled=True)
    return lax.psum_scatter(part, "narrow", scatter_dimension=0, tiled=False).astype(full)


def around(block):
    return [turn(block, step) for step in range(1, 4)]


def near_sends(pieces, from_y, from_x):
    cut = from_y.shape[0]
    to_x = jnp.concatenate([(pieces[1][:cut].astype(full) + from_y.astype(full)).astype(low), pieces[1][cut:]], axis=0)
    to_y = jnp.concatenate([pieces[2][:cut], (pieces[2][cut:].astype(full) + from_x.astype(full)).astype(low)], axis=0)
    return to_x, to_y


def last_sends(mine, over_x, over_y):
    part = (mine.astype(full) + over_x.astype(full) + over_y.astype(full)).astype(low)
    return tuple(part[at] for at in range(4))


def last_sum(first, rest):
    total = first.astype(full)
    for part in rest:
        total = total + part.astype(full)
    return total


def shards(
    tokens,
    cotangent,
    triple_weight,
    output_weight,
    expand_weight,
    shrink_weight,
    norm_gains,
    shift_biases,
    head_biases,
    expand_biases,
    triple_first,
    output_first,
    expand_first,
    shrink_first,
    gains_first,
    shifts_first,
    heads_first,
    widen_first,
    triple_second,
    output_second,
    expand_second,
    shrink_second,
    gains_second,
    shifts_second,
    heads_second,
    widen_second,
    *,
    wide,
    narrow,
):
    tuned = wide == 8 and narrow == 4
    rows = tokens.shape[0]
    local = head_biases.shape[1]
    hidden = expand_biases.shape[0]
    place = lax.axis_index("wide")
    at_narrow = lax.axis_index("narrow")
    if tuned:
        order = jnp.bitwise_xor(place, jnp.array([0, 2, 4, 6, 1, 3, 5, 7], jnp.int32)).astype(jnp.int32)
        group_order = (at_narrow - jnp.arange(narrow)) % narrow
    else:
        order = jnp.arange(BLOCKS, dtype=jnp.int32)
        group_order = jnp.arange(narrow)

    triple_block = jnp.concatenate([triple_weight[:, at].astype(low) for at in range(3)] + [output_weight.astype(low).T], axis=1)
    expand_block = expand_weight.astype(low)
    shrink_block = shrink_weight.astype(low).T
    bias_block = jnp.concatenate([head_biases[0], head_biases[1], expand_biases])

    def begin(order, tokens, cotangent):
        return pl.pallas_call(
            start_kernel,
            in_specs=[pl.BlockSpec(memory_space=pltpu.SMEM)] + [pl.BlockSpec(memory_space=pltpu.VMEM)] * 4,
            out_shape=[
                struct((rows, D), full),
                struct((rows, D), low),
                struct((rows, D), full),
                struct((rows, D), low),
                struct((2, D), full),
                struct((4, D), full),
                struct((1, D), full),
            ],
            compiler_params=big,
        )(order, tokens, cotangent, norm_gains, shift_biases)

    def split_bias(biases):
        triple_bias = jnp.concatenate(
            [biases[:, :local], jnp.zeros((narrow, local), full), biases[:, local : 2 * local]], axis=1
        )
        return triple_bias[:, None], biases[:, 2 * local :][:, None]

    if tuned:
        triple_turns = around(triple_block)
        begun = begin(order, tokens, cotangent)
        triple_turns, begun, triple_block, expand_block, shrink_block, bias_block = fence(
            triple_turns, begun, triple_block, expand_block, shrink_block, bias_block
        )
        tok, normed, cot, cot_low, gains, shifts, cot_sum = begun
        t_near = jnp.stack([triple_block, *triple_turns])
        t_x, t_y = swap(t_near, 2), swap(t_near, 4)
        expand_turns = around(expand_block)
        t_near, t_x, t_y, normed, bias_block = fence(t_near, t_x, t_y, normed, bias_block)
        t_f, t_g = swap(t_x[:2], 4), swap(t_y[2:], 2)
        t_near, t_x, t_y, t_f, t_g, expand_turns, expand_block, normed, bias_block = fence(
            t_near, t_x, t_y, t_f, t_g, expand_turns, expand_block, normed, bias_block
        )
        e_near = jnp.stack([expand_block, *expand_turns])
        e_x, e_y = swap(e_near, 2), swap(e_near, 4)
        triple_own = (t_near, t_x, t_y, t_f, t_g)
        triple_twin = tuple(swap(piece, 1) for piece in triple_own)
        bias_turns = around(bias_block)
        triple_twin, bias_turns, normed, shrink_block = fence(triple_twin, bias_turns, normed, shrink_block)
        triple_bias, widen_bias = split_bias(jnp.stack([bias_block, *bias_turns]))
        shrink_turns = around(shrink_block)
        packed, mixed, logs = attend(normed, triple_bias, triple_own, triple_twin)
        e_near, e_x, e_y, mixed, shrink_block, tok = fence(e_near, e_x, e_y, mixed, shrink_block, tok)
        e_f, e_g = swap(e_x[:2], 4), swap(e_y[2:], 2)
        middle, normed_two = middle_call(mixed, tok, gains, shifts, triple_own, triple_twin, 3)
        e_near, e_x, e_y, e_f, e_g, shrink_turns, shrink_block, normed_two = fence(
            e_near, e_x, e_y, e_f, e_g, shrink_turns, shrink_block, normed_two
        )
        s_near = jnp.stack([shrink_block, *shrink_turns])
        s_x, s_y = swap(s_near, 2), swap(s_near, 4)
        expand_own = (e_near, e_x, e_y, e_f, e_g)
        expand_twin = tuple(swap(piece, 1) for piece in expand_own)
    else:
        tok, normed, cot, cot_low, gains, shifts, cot_sum = begin(order, tokens, cotangent)
        triple_bias, widen_bias = split_bias(lax.all_gather(bias_block, "narrow", axis=0, tiled=False))
        triple_own, triple_twin = plain_gather(triple_block)
        expand_own, expand_twin = plain_gather(expand_block)
        shrink_own, shrink_twin = plain_gather(shrink_block)
        packed, mixed, logs = attend(normed, triple_bias, triple_own, triple_twin)
        middle, normed_two = middle_call(mixed, tok, gains, shifts, triple_own, triple_twin, 3)

    active, slope = expand(normed_two, widen_bias, expand_own, expand_twin)
    s_twin = outer_twin(cot_low, active)
    if tuned:
        s_near, s_x, s_y, s_twin, cot_low, active = fence(s_near, s_x, s_y, s_twin, cot_low, active)
        s_f, s_g = swap(s_x[:2], 4), swap(s_y[2:], 2)
        s_other = swap(s_twin, 1)
        s_near_c, s_x_c, s_y_c = swap(s_near, 1), swap(s_x, 1), swap(s_y, 1)
        s_pieces = outer_own(cot_low, active, s_other)
        s_f, s_g, s_pieces, cot_low, slope = fence(s_f, s_g, s_pieces, cot_low, slope)
        s_f_c, s_g_c = swap(s_f, 1), swap(s_g, 1)
        shrink_own = (s_near, s_x, s_y, s_f, s_g)
        shrink_twin = (s_near_c, s_x_c, s_y_c, s_f_c, s_g_c)
        from_y, from_x = swap(s_pieces[3], 4), swap(s_pieces[4], 2)
    else:
        s_pieces = outer_own(cot_low, active, jnp.zeros_like(s_twin))
    expanded_low, widen_sum = expand_back(cot_low, slope, shrink_own, shrink_twin)
    if tuned:
        from_y, from_x, expanded_low, s_pieces = fence(from_y, from_x, expanded_low, s_pieces)
        to_x, to_y = near_sends(s_pieces, from_y, from_x)
        s_over_x, s_over_y = swap(to_x, 2), swap(to_y, 4)
    middle_grad, middle_low, two_sums = norm_call(
        norm_two_kernel, order, expanded_low, middle, cot, gains, expand_own, expand_twin, True
    )
    e_twin = outer_twin(normed_two, expanded_low)
    if tuned:
        s_over_x, s_over_y, e_twin, middle_low, s_pieces, packed = fence(
            s_over_x, s_over_y, e_twin, middle_low, s_pieces, packed
        )
        e_other = swap(e_twin, 1)
        s_last = last_sends(s_pieces[0], s_over_x, s_over_y)
        s_back = [turn(s_last[step], -step) for step in range(1, 4)]
    else:
        e_other = jnp.zeros_like(e_twin)
    triple_low, head_sums = attend_back(middle_low, packed, logs, triple_own, triple_twin, 3)
    if tuned:
        e_other, triple_low, normed = fence(e_other, triple_low, normed)
    e_pieces = outer_own(normed_two, expanded_low, e_other)
    t_twin = outer_twin(normed, triple_low)
    if tuned:
        e_pieces, t_twin, s_back, triple_low, normed = fence(e_pieces, t_twin, s_back, triple_low, normed)
        t_other = swap(t_twin, 1)
        from_y, from_x = swap(e_pieces[3], 4), swap(e_pieces[4], 2)
    else:
        t_other = jnp.zeros_like(t_twin)
    o_twin = outer_twin(middle_low, mixed)
    t_pieces = outer_own(normed, triple_low, t_other)
    if tuned:
        from_y, from_x, e_pieces, t_pieces, o_twin, triple_low = fence(
            from_y, from_x, e_pieces, t_pieces, o_twin, triple_low
        )
        t_from_y, t_from_x = swap(t_pieces[3], 4), swap(t_pieces[4], 2)
        to_x, to_y = near_sends(e_pieces, from_y, from_x)
        e_over_x, e_over_y = swap(to_x, 2), swap(to_y, 4)
        o_other = swap(o_twin, 1)
    else:
        o_other = jnp.zeros_like(o_twin)
    o_pieces = outer_own(middle_low, mixed, o_other)
    input_gradient, one_sums = norm_call(
        norm_one_kernel, order, triple_low, tok, middle_grad, gains, triple_own, triple_twin, False
    )
    small = jnp.concatenate(
        [
            one_sums[0:1],
            two_sums[0:1],
            one_sums[1:2],
            two_sums[1:3],
            cot_sum,
            head_sums[group_order].transpose(1, 0, 2).reshape(2, D),
            widen_sum[group_order].reshape(-1, D),
        ],
        axis=0,
    )
    if tuned:
        t_from_y, t_from_x, o_pieces, small, t_pieces, active, e_over_x, e_over_y = fence(
            t_from_y, t_from_x, o_pieces, small, t_pieces, active, e_over_x, e_over_y
        )
        to_x, to_y = near_sends(t_pieces, t_from_y, t_from_x)
        t_over_x, t_over_y = swap(to_x, 2), swap(to_y, 4)
        from_y, from_x = swap(o_pieces[3], 4), swap(o_pieces[4], 2)
        small = small + swap(small, 1)
        from_y, from_x, small, active = fence(from_y, from_x, small, active)
        to_x, to_y = near_sends(o_pieces, from_y, from_x)
        o_over_x, o_over_y = swap(to_x, 2), swap(to_y, 4)
        small = small + cross(small, 1)
        e_last = last_sends(e_pieces[0], e_over_x, e_over_y)
        e_back = [turn(e_last[step], -step) for step in range(1, 4)]
    layer_output = shrink(order, active, middle, shifts, shrink_own, shrink_twin)
    if tuned:
        t_over_x, t_over_y, o_over_x, o_over_y, small, layer_output = fence(
            t_over_x, t_over_y, o_over_x, o_over_y, small, layer_output
        )
        t_last = last_sends(t_pieces[0], t_over_x, t_over_y)
        t_back = [turn(t_last[step], -step) for step in range(1, 4)]
        small = small + cross(small, 2)
        o_last = last_sends(o_pieces[0], o_over_x, o_over_y)
        o_back = [turn(o_last[step], -step) for step in range(1, 4)]
        small = small + swap(small, 2)
        small = small + swap(small, 4)
        triple_grad = last_sum(t_last[0], t_back)
        output_grad = last_sum(o_last[0], o_back)
        expand_gradient = last_sum(e_last[0], e_back)
        shrink_grad = last_sum(s_last[0], s_back)
    else:
        small = lax.psum(small, ("wide", "narrow"))
        triple_grad = plain_scatter(t_pieces, t_twin)
        output_grad = plain_scatter(o_pieces, o_twin)
        expand_gradient = plain_scatter(e_pieces, e_twin)
        shrink_grad = plain_scatter(s_pieces, s_twin)
    triple_gradient = jnp.stack([triple_grad[:, at * local : (at + 1) * local] for at in range(3)], axis=1)
    output_gradient = output_grad.T
    shrink_gradient = shrink_grad.T
    gains_gradient = small[0:2]
    shifts_gradient = small[2:6]
    heads_gradient = lax.dynamic_slice_in_dim(small[6:8], at_narrow * local, local, 1)
    widen_gradient = lax.dynamic_slice_in_dim(small[8:].reshape(-1), at_narrow * hidden, hidden, 0)

    params = (
        triple_weight,
        output_weight,
        expand_weight,
        shrink_weight,
        norm_gains,
        shift_biases,
        head_biases,
        expand_biases,
    )
    gradients = (
        triple_gradient,
        output_gradient,
        expand_gradient,
        shrink_gradient,
        gains_gradient,
        shifts_gradient,
        heads_gradient,
        widen_gradient,
    )
    firsts = (
        triple_first,
        output_first,
        expand_first,
        shrink_first,
        gains_first,
        shifts_first,
        heads_first,
        widen_first,
    )
    seconds = (
        triple_second,
        output_second,
        expand_second,
        shrink_second,
        gains_second,
        shifts_second,
        heads_second,
        widen_second,
    )
    rates = (0.1, 1.0, 0.1, 0.05, 1.0, 0.3, 0.2, 0.3)
    decays = (decay_rate, decay_rate, decay_rate, decay_rate, 0.0, 0.0, 0.0, 0.0)
    results = [layer_output, input_gradient]
    for index in range(8):
        renewed, updated = adam_step(
            params[index],
            gradients[index],
            firsts[index],
            seconds[index],
            rates[index],
            decays[index],
        )
        if index == 5:
            results.extend([gradients[index], renewed[1:], renewed[0], updated])
        else:
            results.extend([gradients[index], renewed, updated])
    return tuple(results)


def solution(mesh):
    placed = (
        P(("wide", "narrow"), None),
        P(("wide", "narrow"), None),
        P("wide", None, "narrow"),
        P("narrow", "wide"),
        P("wide", "narrow"),
        P("narrow", "wide"),
        P(),
        P(),
        P(None, "narrow"),
        P("narrow"),
        P("wide", None, "narrow"),
        P("narrow", "wide"),
        P("wide", "narrow"),
        P("narrow", "wide"),
        P(),
        P(),
        P(None, "narrow"),
        P("narrow"),
        P("wide", None, "narrow"),
        P("narrow", "wide"),
        P("wide", "narrow"),
        P("narrow", "wide"),
        P(),
        P(),
        P(None, "narrow"),
        P("narrow"),
    )
    matrices = (P("wide", None, "narrow"), P("narrow", "wide"), P("wide", "narrow"), P("narrow", "wide"))
    outs = [P(("wide", "narrow"), None), P(("wide", "narrow"), None)]
    for spec in matrices:
        outs.extend([spec] * 3)
    outs.extend([P()] * 7)
    outs.extend([P(None, "narrow")] * 3)
    outs.extend([P("narrow")] * 3)
    return jax.shard_map(
        functools.partial(shards, wide=mesh.shape["wide"], narrow=mesh.shape["narrow"]),
        mesh=mesh,
        in_specs=placed,
        out_specs=tuple(outs),
        check_vma=False,
    )
```

```python
import functools
import math

import jax
import jax.numpy as jnp
from jax import lax
from jax.experimental import pallas as pl
from jax.experimental.pallas import tpu as pltpu
from jax.sharding import PartitionSpec as P

D = 1024
H = 16
SEQ = 577
STEP = 10
HEAD = D // H
LANES = 128
BLOCKS = D // LANES
HALF = D // 2


norm_eps = 1e-06
beta_first = 0.9
beta_second = 0.999
adam_eps = 1e-08
decay_rate = 0.05

low = jnp.bfloat16
full = jnp.float32
big = pltpu.CompilerParams(vmem_limit_bytes=56 * 1024 * 1024)


def adam_step(weight, grad, first, second, rate, decay):
    first_new = beta_first * first + (1.0 - beta_first) * grad
    second_new = beta_second * second + (1.0 - beta_second) * grad * grad
    first_hat = first_new / (1.0 - beta_first**STEP)
    second_hat = second_new / (1.0 - beta_second**STEP)
    updated = weight - rate * (first_hat / (jnp.sqrt(second_hat) + adam_eps) + decay * weight)
    return (second_new, updated)


def dot_nn(left, right):
    return lax.dot_general(left, right, (((1,), (0,)), ((), ())), preferred_element_type=full)


def dot_nt(left, right):
    return lax.dot_general(left, right, (((1,), (1,)), ((), ())), preferred_element_type=full)


def dot_tn(left, right):
    return lax.dot_general(left, right, (((0,), (0,)), ((), ())), preferred_element_type=full)


def lane_block(order, at):
    return pl.ds(pl.multiple_of(order[at] * LANES, LANES), LANES)


def stat(values):
    center = values - jnp.mean(values, axis=-1, keepdims=True)
    inverse = lax.rsqrt(jnp.mean(center * center, axis=-1, keepdims=True) + norm_eps)
    return center * inverse, inverse


def norm_back(values, grad, gain):
    unit, inverse = stat(values)
    scaled = grad * gain
    part = inverse * (
        scaled
        - jnp.mean(scaled, axis=-1, keepdims=True)
        - unit * jnp.mean(scaled * unit, axis=-1, keepdims=True)
    )
    gain_sum = jnp.sum(grad * unit, axis=0, keepdims=True)
    shift_sum = jnp.sum(grad, axis=0, keepdims=True)
    return part, gain_sum, shift_sum


def start_kernel(order, tok, cot, gains, shifts, tok_out, normed, cot_out, cot_low, gains_out, shifts_out, cot_sum):
    values = tok[...]
    mean = jnp.mean(values, axis=-1, keepdims=True)
    center = values - mean
    inverse = lax.rsqrt(jnp.mean(center * center, axis=-1, keepdims=True) + norm_eps)
    cot_sum[...] = jnp.sum(cot[...], axis=0, keepdims=True)
    for at in range(BLOCKS):
        source = lane_block(order, at)
        place = slice(at * LANES, (at + 1) * LANES)
        block = tok[:, source]
        tok_out[:, place] = block
        gain = gains[:, source]
        shift = shifts[:, source]
        gains_out[:, place] = gain
        shifts_out[:, place] = shift
        normed[:, place] = ((block - mean) * inverse * gain[0:1] + shift[0:1]).astype(low)
        other = cot[:, source]
        cot_out[:, place] = other
        cot_low[:, place] = other.astype(low)


def piece_specs(pieces, width, lane=0):
    groups = pieces[0].shape[0]
    cut = groups // 2
    shape = (1, pieces[0].shape[1], width)
    same = pl.BlockSpec(shape, lambda n, *s: (n, 0, lane))
    first = pl.BlockSpec(shape, lambda n, *s: (jnp.minimum(n, cut - 1), 0, lane))
    second = pl.BlockSpec(shape, lambda n, *s: (jnp.maximum(n - cut, 0), 0, lane))
    return [same, same, same, first, second]


def assemble(refs, groups):
    near = [ref[0] for ref in refs[:3]]
    far = jnp.where(pl.program_id(0) < groups // 2, refs[3][0], refs[4][0])
    return jnp.concatenate(near + [far], axis=0)


def whole_spec(*shape):
    return pl.BlockSpec(shape, lambda n, *s: (0,) * len(shape))


def once_spec(*shape):
    return pl.BlockSpec(shape, lambda n, *s: (0,) * len(shape), pipeline_mode=pl.Buffered(1))


def twin_half(rows):
    return pl.BlockSpec((rows, HALF), lambda n, *s: (0, 1), pipeline_mode=pl.Buffered(1))


def group_spec(*shape):
    return pl.BlockSpec((1,) + shape, lambda n, *s: (n,) + (0,) * len(shape))


def grouped(kernel, groups, ins, outs, out_shapes, args, scratch=(), prefetch=0):
    return pl.pallas_call(
        kernel,
        grid_spec=pltpu.PrefetchScalarGridSpec(
            num_scalar_prefetch=prefetch,
            grid=(groups,),
            in_specs=ins,
            out_specs=outs,
            scratch_shapes=list(scratch),
        ),
        out_shape=out_shapes,
        compiler_params=big,
    )(*args)


def struct(shape, dtype):
    return jax.ShapeDtypeStruct(shape, dtype)


def attend_kernel(groups, *refs):
    x, bias = refs[:2]
    own, twin = refs[2:7], refs[7:12]
    packed, mixed, logs = refs[12:]
    value = dot_nn(x[:, :HALF], assemble(own, groups)) + dot_nn(x[:, HALF:], assemble(twin, groups)) + bias[0]
    width = value.shape[1] // 3
    value = value.astype(low)
    packed[0] = value
    lane = lax.broadcasted_iota(jnp.int32, (1, LANES), 1)
    scale = 1.0 / math.sqrt(HEAD)
    rows = value.shape[0]
    log_all = jnp.zeros((rows, LANES), full)
    for pair in range(width // LANES):
        cols = slice(pair * LANES, (pair + 1) * LANES)
        query = value[:, cols]
        key = value[:, width + pair * LANES : width + (pair + 1) * LANES]
        val = value[:, 2 * width + pair * LANES : 2 * width + (pair + 1) * LANES]
        outs = []
        for side in range(2):
            keep = jnp.where(lane // HEAD == side, scale, 0.0).astype(low)
            scores = dot_nt(query * keep, key)
            top = jnp.max(scores, axis=-1, keepdims=True)
            expon = jnp.exp(scores - top)
            total = jnp.sum(expon, axis=-1, keepdims=True)
            outs.append(dot_nn(expon.astype(low), val) / total)
            log_all = jnp.where(lane == 2 * pair + side, top + jnp.log(total), log_all)
        mixed[0, :, cols] = jnp.where(lane < HEAD, outs[0], outs[1]).astype(low)
    logs[0] = log_all.T[:8]


def attend(normed, bias, own, twin):
    groups, _, width = bias.shape
    rows = normed.shape[0]
    return grouped(
        functools.partial(attend_kernel, groups),
        groups,
        [whole_spec(rows, D), group_spec(1, width)] + piece_specs(own, width) + piece_specs(twin, width),
        [group_spec(rows, width), group_spec(rows, width // 3), group_spec(8, rows)],
        [struct((groups, rows, width), low), struct((groups, rows, width // 3), low), struct((groups, 8, rows), full)],
        (normed, bias, *own, *twin),
    )


def attend_back_kernel(groups, *refs):
    grad, packed, logs, normed = refs[:4]
    own, twin = refs[4:9], refs[9:14]
    out, sums, outer = refs[14:]
    upper = (dot_nn(grad[:, :HALF], assemble(own, groups)) + dot_nn(grad[:, HALF:], assemble(twin, groups))).astype(low)
    width = upper.shape[1]
    lane = lax.broadcasted_iota(jnp.int32, (1, LANES), 1)
    scale = 1.0 / math.sqrt(HEAD)
    for pair in range(width // LANES):
        cols = slice(pair * LANES, (pair + 1) * LANES)
        query = packed[0, :, cols]
        key = packed[0, :, width + pair * LANES : width + (pair + 1) * LANES]
        val = packed[0, :, 2 * width + pair * LANES : 2 * width + (pair + 1) * LANES]
        up = upper[:, cols]
        parts = []
        for side in range(2):
            head = 2 * pair + side
            inside = lane // HEAD == side
            scores = dot_nt(key * jnp.where(inside, scale, 0.0).astype(low), query)
            probs = jnp.exp(scores - logs[0, head : head + 1, :])
            val_grad = dot_nn(probs.astype(low), up)
            prob_grad = dot_nt(val * jnp.where(inside, 1.0, 0.0).astype(low), up)
            weighted = probs * prob_grad
            score_grad = (weighted - probs * jnp.sum(weighted, axis=0, keepdims=True)).astype(low)
            key_grad = dot_nn(score_grad, query) * scale
            query_grad = dot_tn(score_grad, key) * scale
            parts.append((query_grad, key_grad, val_grad))
        for kind in range(3):
            both = jnp.where(lane < HEAD, parts[0][kind], parts[1][kind])
            start = kind * width + pair * LANES
            out[0, :, start : start + LANES] = both.astype(low)
            if kind != 1:
                sums[0, kind // 2 : kind // 2 + 1, cols] = jnp.sum(both, axis=0, keepdims=True)
    outer[0] = dot_tn(normed[...], out[0]).astype(low)


def attend_back(grad, packed, logs, normed, own, twin, lane):
    groups, rows, width = packed.shape
    third = width // 3
    return grouped(
        functools.partial(attend_back_kernel, groups),
        groups,
        [whole_spec(rows, D), group_spec(rows, width), group_spec(8, rows), twin_half(rows)]
        + piece_specs(own, third, lane)
        + piece_specs(twin, third, lane),
        [group_spec(rows, width), group_spec(2, third), group_spec(HALF, width)],
        [
            struct((groups, rows, width), low),
            struct((groups, 2, third), full),
            struct((groups, HALF, width), low),
        ],
        (grad, packed, logs, normed, *own, *twin),
    )


def add_parts(groups, inner, own, twin, total):
    total[:, :HALF] += dot_nt(inner[0], assemble(own, groups))
    total[:, HALF:] += dot_nt(inner[0], assemble(twin, groups))


def middle_kernel(groups, *refs):
    mixed, tok, gains, shifts = refs[:4]
    own, twin = refs[4:9], refs[9:14]
    middle, normed, total = refs[14:]
    n = pl.program_id(0)

    @pl.when(n == 0)
    def _():
        total[...] = tok[...] + shifts[2:3]

    add_parts(groups, mixed, own, twin, total)

    @pl.when(n == groups - 1)
    def _():
        values = total[...]
        middle[...] = values
        unit, _ = stat(values)
        normed[...] = (unit * gains[1:2] + shifts[1:2]).astype(low)


def middle_call(mixed, tok, gains, shifts, own, twin, lane):
    groups, rows, width = mixed.shape
    return grouped(
        functools.partial(middle_kernel, groups),
        groups,
        [group_spec(rows, width), whole_spec(rows, D), whole_spec(2, D), whole_spec(4, D)]
        + piece_specs(own, width, lane)
        + piece_specs(twin, width, lane),
        [whole_spec(rows, D), whole_spec(rows, D)],
        [struct((rows, D), full), struct((rows, D), low)],
        (mixed, tok, gains, shifts, *own, *twin),
        scratch=[pltpu.VMEM((rows, D), full)],
    )


def expand_kernel(groups, *refs):
    x, bias, cot = refs[:3]
    own, twin = refs[3:8], refs[8:13]
    active, slope, outer = refs[13:]
    value = dot_nn(x[:, :HALF], assemble(own, groups)) + dot_nn(x[:, HALF:], assemble(twin, groups)) + bias[0]
    phi = 0.5 * (1.0 + lax.erf(value * math.sqrt(0.5)))
    low_active = (value * phi).astype(low)
    active[0] = low_active
    outer[0] = dot_tn(cot[...], low_active).astype(low)
    slope[0] = (phi + value * (jnp.exp(-0.5 * value * value) * (1.0 / math.sqrt(2.0 * math.pi)))).astype(low)


def expand(normed, bias, cot, own, twin):
    groups, rows, width = bias.shape[0], normed.shape[0], bias.shape[2]
    shape = struct((groups, rows, width), low)
    return grouped(
        functools.partial(expand_kernel, groups),
        groups,
        [whole_spec(rows, D), group_spec(1, width), twin_half(rows)]
        + piece_specs(own, width)
        + piece_specs(twin, width),
        [group_spec(rows, width)] * 2 + [group_spec(HALF, width)],
        [shape, shape, struct((groups, HALF, width), low)],
        (normed, bias, cot, *own, *twin),
    )


def hidden_back_kernel(groups, order, *refs):
    grad, slope, active, middle, cot, gains, shifts, normed = refs[:8]
    shrink_own, shrink_twin = refs[8:13], refs[13:18]
    expand_own, expand_twin = refs[18:23], refs[23:28]
    inner, sums, outer, layer, out, out_low, two_sums, total, result = refs[28:]
    n = pl.program_id(0)

    @pl.when(n == 0)
    def _():
        total[...] = jnp.zeros_like(total)
        result[...] = middle[...] + shifts[3:4]

    own, twin = assemble(shrink_own, groups), assemble(shrink_twin, groups)
    value = (dot_nn(grad[:, :HALF], own) + dot_nn(grad[:, HALF:], twin)) * slope[0].astype(full)
    sums[0] = jnp.sum(value, axis=0, keepdims=True)
    low_value = value.astype(low)
    inner[0] = low_value
    result[:, :HALF] += dot_nt(active[0], own)
    result[:, HALF:] += dot_nt(active[0], twin)
    outer[0] = dot_tn(normed[...], low_value).astype(low)
    add_parts(groups, inner, expand_own, expand_twin, total)

    @pl.when(n == groups - 1)
    def _():
        part, gain_sum, shift_sum = norm_back(middle[...], total[...], gains[1:2])
        grad_out = cot[...] + part
        out[...] = grad_out
        out_low[...] = grad_out.astype(low)
        grad_sum = jnp.sum(grad_out, axis=0, keepdims=True)
        for at in range(BLOCKS):
            place = lane_block(order, at)
            cols = slice(at * LANES, (at + 1) * LANES)
            layer[:, place] = result[:, cols]
            two_sums[0:1, place] = gain_sum[:, cols]
            two_sums[1:2, place] = shift_sum[:, cols]
            two_sums[2:3, place] = grad_sum[:, cols]


def hidden_back(order, grad, slope, active, middle, cot, gains, shifts, normed, shrink_own, shrink_twin, own, twin):
    groups, rows, width = slope.shape
    group = group_spec(rows, width)
    pieces = piece_specs(own, width)
    once = once_spec(rows, D)
    return grouped(
        functools.partial(hidden_back_kernel, groups),
        groups,
        [once, group, group, once, once, whole_spec(2, D), whole_spec(4, D), twin_half(rows)] + pieces * 4,
        [group, group_spec(1, width), group_spec(HALF, width), once, once, once, whole_spec(3, D)],
        [
            struct((groups, rows, width), low),
            struct((groups, 1, width), full),
            struct((groups, HALF, width), low),
            struct((rows, D), full),
            struct((rows, D), full),
            struct((rows, D), low),
            struct((3, D), full),
        ],
        (
            order,
            grad,
            slope,
            active,
            middle,
            cot,
            gains,
            shifts,
            normed,
            *shrink_own,
            *shrink_twin,
            *own,
            *twin,
        ),
        scratch=[pltpu.VMEM((rows, D), full), pltpu.VMEM((rows, D), full)],
        prefetch=1,
    )


def outer_twin_kernel(x, inner, out):
    out[0] = dot_tn(x[...], inner[0]).astype(low)


def outer_twin(x, inner):
    groups, rows, width = inner.shape
    return grouped(
        outer_twin_kernel,
        groups,
        [pl.BlockSpec((rows, HALF), lambda n: (0, 1)), group_spec(rows, width)],
        group_spec(HALF, width),
        struct((groups, HALF, width), low),
        (x, inner),
    )


def outer_own_kernel(groups, x, inner, other, mine, to_x, to_y, far_first, far_second):
    value = (dot_tn(x[...], inner[0]) + other[0].astype(full)).astype(low)
    rows = HALF // 4
    mine[0] = value[:rows]
    to_x[0] = value[rows : 2 * rows]
    to_y[0] = value[2 * rows : 3 * rows]
    n = pl.program_id(0)

    @pl.when(n < groups // 2)
    def _():
        far_first[0] = value[3 * rows :]

    @pl.when(n >= groups // 2)
    def _():
        far_second[0] = value[3 * rows :]


def outer_own(x, inner, other):
    groups, rows, width = inner.shape
    near = struct((groups, HALF // 4, width), low)
    far = struct((groups // 2, HALF // 4, width), low)
    shapes = [near, near, near, far, far]
    return grouped(
        functools.partial(outer_own_kernel, groups),
        groups,
        [pl.BlockSpec((rows, HALF), lambda n: (0, 0)), group_spec(rows, width), group_spec(HALF, width)],
        piece_specs(shapes, width),
        shapes,
        (x, inner, other),
    )


def norm_one_kernel(groups, order, *refs):
    inner, tok, grad, gains = refs[:4]
    own, twin = refs[4:9], refs[9:14]
    out, sums, total = refs[14:]
    n = pl.program_id(0)

    @pl.when(n == 0)
    def _():
        total[...] = jnp.zeros_like(total)

    add_parts(groups, inner, own, twin, total)

    @pl.when(n == groups - 1)
    def _():
        part, gain_sum, shift_sum = norm_back(tok[...], total[...], gains[0:1])
        result = grad[...] + part
        for at in range(BLOCKS):
            place = lane_block(order, at)
            cols = slice(at * LANES, (at + 1) * LANES)
            out[:, place] = result[:, cols]
            sums[0:1, place] = gain_sum[:, cols]
            sums[1:2, place] = shift_sum[:, cols]


def norm_one(order, inner, values, grad, gains, own, twin):
    groups, rows, width = inner.shape
    whole = whole_spec(rows, D)
    return grouped(
        functools.partial(norm_one_kernel, groups),
        groups,
        [group_spec(rows, width), whole, whole, whole_spec(2, D)] + piece_specs(own, width) + piece_specs(twin, width),
        [whole, whole_spec(2, D)],
        [struct((rows, D), full), struct((2, D), full)],
        (order, inner, values, grad, gains, *own, *twin),
        scratch=[pltpu.VMEM((rows, D), full)],
        prefetch=1,
    )


def swap(values, bit):
    return lax.ppermute(values, "wide", [(at, at ^ bit) for at in range(8)])


def turn(values, step):
    return lax.ppermute(values, "narrow", [(at, (at + step) % 4) for at in range(4)])


def cross(values, bit):
    return lax.ppermute(values, "narrow", [(at, at ^ bit) for at in range(4)])


def fence(*values):
    return lax.optimization_barrier(values)


def plain_gather(block):
    groups = lax.all_gather(block, "narrow", axis=0, tiled=False)
    whole = lax.all_gather(groups, "wide", axis=1, tiled=True)
    rows, cut = HALF // 4, whole.shape[0] // 2
    sides = []
    for side in range(2):
        parts = [whole[:, side * HALF + at * rows : side * HALF + (at + 1) * rows] for at in range(4)]
        sides.append((*parts[:3], parts[3][:cut], parts[3][cut:]))
    return tuple(sides)


def plain_scatter(pieces, twin):
    far = jnp.concatenate(pieces[3:], axis=0)
    whole = jnp.concatenate([*pieces[:3], far, twin], axis=1)
    part = lax.psum_scatter(whole, "wide", scatter_dimension=1, tiled=True)
    return lax.psum_scatter(part, "narrow", scatter_dimension=0, tiled=False).astype(full)


def around(block):
    return [turn(block, step) for step in range(1, 4)]


def near_sends(pieces, from_y, from_x):
    cut = from_y.shape[0]
    to_x = jnp.concatenate([(pieces[1][:cut].astype(full) + from_y.astype(full)).astype(low), pieces[1][cut:]], axis=0)
    to_y = jnp.concatenate([pieces[2][:cut], (pieces[2][cut:].astype(full) + from_x.astype(full)).astype(low)], axis=0)
    return to_x, to_y


def last_sends(mine, over_x, over_y):
    part = (mine.astype(full) + over_x.astype(full) + over_y.astype(full)).astype(low)
    return tuple(part[at] for at in range(4))


def narrow_scatter(mine, over_x, over_y, places):
    part = (mine.astype(full) + over_x.astype(full) + over_y.astype(full)).astype(low)
    parts = [lax.dynamic_index_in_dim(part, places[at], 0, keepdims=False) for at in range(4)]
    return lax.psum_scatter(jnp.stack(parts), "narrow", scatter_dimension=0, tiled=False).astype(full)


def last_sum(first, rest):
    total = first.astype(full)
    for part in rest:
        total = total + part.astype(full)
    return total


def shards(
    tokens,
    cotangent,
    triple_weight,
    output_weight,
    expand_weight,
    shrink_weight,
    norm_gains,
    shift_biases,
    head_biases,
    expand_biases,
    triple_first,
    output_first,
    expand_first,
    shrink_first,
    gains_first,
    shifts_first,
    heads_first,
    widen_first,
    triple_second,
    output_second,
    expand_second,
    shrink_second,
    gains_second,
    shifts_second,
    heads_second,
    widen_second,
    *,
    wide,
    narrow,
):
    tuned = wide == 8 and narrow == 4
    rows = tokens.shape[0]
    local = head_biases.shape[1]
    hidden = expand_biases.shape[0]
    place = lax.axis_index("wide")
    at_narrow = lax.axis_index("narrow")
    if tuned:
        order = jnp.bitwise_xor(place, jnp.array([0, 2, 4, 6, 1, 3, 5, 7], jnp.int32)).astype(jnp.int32)
        group_order = (at_narrow - jnp.arange(narrow)) % narrow
    else:
        order = jnp.arange(BLOCKS, dtype=jnp.int32)
        group_order = jnp.arange(narrow)

    triple_block = jnp.concatenate([triple_weight[:, at].astype(low) for at in range(3)] + [output_weight.astype(low).T], axis=1)
    expand_block = expand_weight.astype(low)
    shrink_block = shrink_weight.astype(low).T
    bias_block = jnp.concatenate([head_biases[0], head_biases[1], expand_biases])

    def begin(order, tokens, cotangent):
        return pl.pallas_call(
            start_kernel,
            in_specs=[pl.BlockSpec(memory_space=pltpu.SMEM)] + [pl.BlockSpec(memory_space=pltpu.VMEM)] * 4,
            out_shape=[
                struct((rows, D), full),
                struct((rows, D), low),
                struct((rows, D), full),
                struct((rows, D), low),
                struct((2, D), full),
                struct((4, D), full),
                struct((1, D), full),
            ],
            compiler_params=big,
        )(order, tokens, cotangent, norm_gains, shift_biases)

    def split_bias(biases):
        triple_bias = jnp.concatenate(
            [biases[:, :local], jnp.zeros((narrow, local), full), biases[:, local : 2 * local]], axis=1
        )
        return triple_bias[:, None], biases[:, 2 * local :][:, None]

    if tuned:
        triple_turns = around(triple_block)
        begun = begin(order, tokens, cotangent)
        triple_turns, begun, triple_block, expand_block, shrink_block, bias_block = fence(
            triple_turns, begun, triple_block, expand_block, shrink_block, bias_block
        )
        tok, normed, cot, cot_low, gains, shifts, cot_sum = begun
        t_near = jnp.stack([triple_block, *triple_turns])
        t_x, t_y = swap(t_near, 2), swap(t_near, 4)
        expand_turns = around(expand_block)
        t_near, t_x, t_y, expand_turns, expand_block, normed, bias_block = fence(
            t_near, t_x, t_y, expand_turns, expand_block, normed, bias_block
        )
        t_f, t_g = swap(t_x[:2], 4), swap(t_y[2:], 2)
        t_near_c, t_x_c, t_y_c = swap(t_near, 1), swap(t_x, 1), swap(t_y, 1)
        e_near = jnp.stack([expand_block, *expand_turns])
        t_f, t_g, t_near_c, t_x_c, t_y_c, e_near, normed, bias_block, shrink_block = fence(
            t_f, t_g, t_near_c, t_x_c, t_y_c, e_near, normed, bias_block, shrink_block
        )
        e_x, e_y = swap(e_near, 2), swap(e_near, 4)
        t_f_c, t_g_c = swap(t_f, 1), swap(t_g, 1)
        triple_own = (t_near, t_x, t_y, t_f, t_g)
        triple_twin = (t_near_c, t_x_c, t_y_c, t_f_c, t_g_c)
        bias_turns = around(bias_block)
        triple_twin, bias_turns, normed, shrink_block = fence(triple_twin, bias_turns, normed, shrink_block)
        triple_bias, widen_bias = split_bias(jnp.stack([bias_block, *bias_turns]))
        shrink_turns = around(shrink_block)
        packed, mixed, logs = attend(normed, triple_bias, triple_own, triple_twin)
        e_near, e_x, e_y, mixed, shrink_turns, shrink_block, tok = fence(
            e_near, e_x, e_y, mixed, shrink_turns, shrink_block, tok
        )
        e_f, e_g = swap(e_x[:2], 4), swap(e_y[2:], 2)
        e_near_c, e_x_c, e_y_c = swap(e_near, 1), swap(e_x, 1), swap(e_y, 1)
        middle, normed_two = middle_call(mixed, tok, gains, shifts, triple_own, triple_twin, 3)
        s_near = jnp.stack([shrink_block, *shrink_turns])
        e_f, e_g, e_near_c, e_x_c, e_y_c, s_near, normed_two = fence(
            e_f, e_g, e_near_c, e_x_c, e_y_c, s_near, normed_two
        )
        s_x, s_y = swap(s_near, 2), swap(s_near, 4)
        expand_own = (e_near, e_x, e_y, e_f, e_g)
        expand_twin = (e_near_c, e_x_c, e_y_c, swap(e_f, 1), swap(e_g, 1))
    else:
        tok, normed, cot, cot_low, gains, shifts, cot_sum = begin(order, tokens, cotangent)
        triple_bias, widen_bias = split_bias(lax.all_gather(bias_block, "narrow", axis=0, tiled=False))
        triple_own, triple_twin = plain_gather(triple_block)
        expand_own, expand_twin = plain_gather(expand_block)
        shrink_own, shrink_twin = plain_gather(shrink_block)
        packed, mixed, logs = attend(normed, triple_bias, triple_own, triple_twin)
        middle, normed_two = middle_call(mixed, tok, gains, shifts, triple_own, triple_twin, 3)

    active, slope, s_twin = expand(normed_two, widen_bias, cot_low, expand_own, expand_twin)
    if tuned:
        s_near, s_x, s_y, s_twin, cot_low, active = fence(s_near, s_x, s_y, s_twin, cot_low, active)
        s_f, s_g = swap(s_x[:2], 4), swap(s_y[2:], 2)
        s_other = swap(s_twin, 1)
        s_near_c, s_x_c = swap(s_near, 1), swap(s_x, 1)
        s_pieces = outer_own(cot_low, active, s_other)
        s_f, s_g, s_pieces, s_near_c, s_x_c, cot_low, slope = fence(
            s_f, s_g, s_pieces, s_near_c, s_x_c, cot_low, slope
        )
        from_y, from_x = swap(s_pieces[3], 4), swap(s_pieces[4], 2)
        shrink_own = (s_near, s_x, s_y, s_f, s_g)
        shrink_twin = (s_near_c, s_x_c, swap(s_y, 1), swap(s_f, 1), swap(s_g, 1))
    else:
        s_pieces = outer_own(cot_low, active, jnp.zeros_like(s_twin))
    expanded_low, widen_sum, e_twin, layer_output, middle_grad, middle_low, two_sums = hidden_back(
        order,
        cot_low,
        slope,
        active,
        middle,
        cot,
        gains,
        shifts,
        normed_two,
        shrink_own,
        shrink_twin,
        expand_own,
        expand_twin,
    )
    if tuned:
        from_y, from_x, expanded_low, e_twin, s_pieces = fence(from_y, from_x, expanded_low, e_twin, s_pieces)
        e_other = swap(e_twin, 1)
        to_x, to_y = near_sends(s_pieces, from_y, from_x)
        s_over_x, s_over_y = swap(to_x, 2), swap(to_y, 4)
    else:
        e_other = jnp.zeros_like(e_twin)
    e_pieces = outer_own(normed_two, expanded_low, e_other)
    if tuned:
        e_pieces, middle_low, packed = fence(e_pieces, middle_low, packed)
        from_y, from_x = swap(e_pieces[3], 4), swap(e_pieces[4], 2)
    triple_low, head_sums, t_twin = attend_back(middle_low, packed, logs, normed, triple_own, triple_twin, 3)
    if tuned:
        from_y, from_x, s_over_x, s_over_y, t_twin, triple_low, e_pieces, s_pieces, mixed = fence(
            from_y, from_x, s_over_x, s_over_y, t_twin, triple_low, e_pieces, s_pieces, mixed
        )
        t_other = swap(t_twin, 1)
        to_x, to_y = near_sends(e_pieces, from_y, from_x)
        e_over_x, e_over_y = swap(to_x, 2), swap(to_y, 4)
        o_twin = outer_twin(middle_low, mixed)
        t_other, o_twin, triple_low, normed = fence(t_other, o_twin, triple_low, normed)
    else:
        t_other = jnp.zeros_like(t_twin)
        o_twin = outer_twin(middle_low, mixed)
    t_pieces = outer_own(normed, triple_low, t_other)
    if tuned:
        t_pieces, o_twin, triple_low = fence(t_pieces, o_twin, triple_low)
        t_from_y, t_from_x = swap(t_pieces[3], 4), swap(t_pieces[4], 2)
        o_other = swap(o_twin, 1)
        shrink_grad = narrow_scatter(s_pieces[0], s_over_x, s_over_y, group_order)
    else:
        o_other = jnp.zeros_like(o_twin)
    input_gradient, one_sums = norm_one(
        order, triple_low, tok, middle_grad, gains, triple_own, triple_twin
    )
    small = jnp.concatenate(
        [
            one_sums[0:1],
            two_sums[0:1],
            one_sums[1:2],
            two_sums[1:3],
            cot_sum,
            head_sums[group_order].transpose(1, 0, 2).reshape(2, D),
            widen_sum[group_order].reshape(-1, D),
        ],
        axis=0,
    )
    o_pieces = outer_own(middle_low, mixed, o_other)
    if tuned:
        t_from_y, t_from_x, small, t_pieces, e_over_x, e_over_y, o_pieces, shrink_grad = fence(
            t_from_y, t_from_x, small, t_pieces, e_over_x, e_over_y, o_pieces, shrink_grad
        )
        to_x, to_y = near_sends(t_pieces, t_from_y, t_from_x)
        t_over_x, t_over_y = swap(to_x, 2), swap(to_y, 4)
        expand_gradient = narrow_scatter(e_pieces[0], e_over_x, e_over_y, group_order)
        from_y, from_x = swap(o_pieces[3], 4), swap(o_pieces[4], 2)
        to_x, to_y = near_sends(o_pieces, from_y, from_x)
        o_over_x, o_over_y = swap(to_x, 2), swap(to_y, 4)
        small = small + swap(small, 1)
        small = small + cross(small, 1)
        small = small + cross(small, 2)
        small = small + swap(small, 2)
        small = small + swap(small, 4)
        t_over_x, t_over_y, o_over_x, o_over_y, small, expand_gradient = fence(
            t_over_x, t_over_y, o_over_x, o_over_y, small, expand_gradient
        )
        t_last = last_sends(t_pieces[0], t_over_x, t_over_y)
        t_back = [turn(t_last[step], -step) for step in range(1, 4)]
        output_grad = narrow_scatter(o_pieces[0], o_over_x, o_over_y, group_order)
        triple_grad = last_sum(t_last[0], t_back)
    else:
        small = lax.psum(small, ("wide", "narrow"))
        triple_grad = plain_scatter(t_pieces, t_twin)
        output_grad = plain_scatter(o_pieces, o_twin)
        expand_gradient = plain_scatter(e_pieces, e_twin)
        shrink_grad = plain_scatter(s_pieces, s_twin)
    triple_gradient = jnp.stack([triple_grad[:, at * local : (at + 1) * local] for at in range(3)], axis=1)
    output_gradient = output_grad.T
    shrink_gradient = shrink_grad.T
    gains_gradient = small[0:2]
    shifts_gradient = small[2:6]
    heads_gradient = lax.dynamic_slice_in_dim(small[6:8], at_narrow * local, local, 1)
    widen_gradient = lax.dynamic_slice_in_dim(small[8:].reshape(-1), at_narrow * hidden, hidden, 0)

    params = (
        triple_weight,
        output_weight,
        expand_weight,
        shrink_weight,
        norm_gains,
        shift_biases,
        head_biases,
        expand_biases,
    )
    gradients = (
        triple_gradient,
        output_gradient,
        expand_gradient,
        shrink_gradient,
        gains_gradient,
        shifts_gradient,
        heads_gradient,
        widen_gradient,
    )
    firsts = (
        triple_first,
        output_first,
        expand_first,
        shrink_first,
        gains_first,
        shifts_first,
        heads_first,
        widen_first,
    )
    seconds = (
        triple_second,
        output_second,
        expand_second,
        shrink_second,
        gains_second,
        shifts_second,
        heads_second,
        widen_second,
    )
    rates = (0.1, 1.0, 0.1, 0.05, 1.0, 0.3, 0.2, 0.3)
    decays = (decay_rate, decay_rate, decay_rate, decay_rate, 0.0, 0.0, 0.0, 0.0)
    results = [layer_output, input_gradient]
    for index in range(8):
        renewed, updated = adam_step(
            params[index],
            gradients[index],
            firsts[index],
            seconds[index],
            rates[index],
            decays[index],
        )
        if index == 5:
            results.extend([gradients[index], renewed[1:], renewed[0], updated])
        else:
            results.extend([gradients[index], renewed, updated])
    return tuple(results)


def solution(mesh):
    placed = (
        P(("wide", "narrow"), None),
        P(("wide", "narrow"), None),
        P("wide", None, "narrow"),
        P("narrow", "wide"),
        P("wide", "narrow"),
        P("narrow", "wide"),
        P(),
        P(),
        P(None, "narrow"),
        P("narrow"),
        P("wide", None, "narrow"),
        P("narrow", "wide"),
        P("wide", "narrow"),
        P("narrow", "wide"),
        P(),
        P(),
        P(None, "narrow"),
        P("narrow"),
        P("wide", None, "narrow"),
        P("narrow", "wide"),
        P("wide", "narrow"),
        P("narrow", "wide"),
        P(),
        P(),
        P(None, "narrow"),
        P("narrow"),
    )
    matrices = (P("wide", None, "narrow"), P("narrow", "wide"), P("wide", "narrow"), P("narrow", "wide"))
    outs = [P(("wide", "narrow"), None), P(("wide", "narrow"), None)]
    for spec in matrices:
        outs.extend([spec] * 3)
    outs.extend([P()] * 7)
    outs.extend([P(None, "narrow")] * 3)
    outs.extend([P("narrow")] * 3)
    return jax.shard_map(
        functools.partial(shards, wide=mesh.shape["wide"], narrow=mesh.shape["narrow"]),
        mesh=mesh,
        in_specs=placed,
        out_specs=tuple(outs),
        check_vma=False,
    )
```

```python
import functools
import math

import jax
import jax.numpy as jnp
from jax import lax
from jax.experimental import pallas as pl
from jax.experimental.pallas import tpu as pltpu
from jax.sharding import PartitionSpec as P

D = 1024
H = 16
SEQ = 577
STEP = 10
HEAD = D // H
LANES = 128
BLOCKS = D // LANES
HALF = D // 2


norm_eps = 1e-06
beta_first = 0.9
beta_second = 0.999
adam_eps = 1e-08
decay_rate = 0.05

low = jnp.bfloat16
full = jnp.float32
big = pltpu.CompilerParams(vmem_limit_bytes=56 * 1024 * 1024)


def adam_step(weight, grad, first, second, rate, decay):
    first_new = beta_first * first + (1.0 - beta_first) * grad
    second_new = beta_second * second + (1.0 - beta_second) * grad * grad
    first_hat = first_new / (1.0 - beta_first**STEP)
    second_hat = second_new / (1.0 - beta_second**STEP)
    updated = weight - rate * (first_hat / (jnp.sqrt(second_hat) + adam_eps) + decay * weight)
    return (second_new, updated)


def dot_nn(left, right):
    return lax.dot_general(left, right, (((1,), (0,)), ((), ())), preferred_element_type=full)


def dot_nt(left, right):
    return lax.dot_general(left, right, (((1,), (1,)), ((), ())), preferred_element_type=full)


def dot_tn(left, right):
    return lax.dot_general(left, right, (((0,), (0,)), ((), ())), preferred_element_type=full)


def lane_block(order, at):
    return pl.ds(pl.multiple_of(order[at] * LANES, LANES), LANES)


def stat(values):
    center = values - jnp.mean(values, axis=-1, keepdims=True)
    inverse = lax.rsqrt(jnp.mean(center * center, axis=-1, keepdims=True) + norm_eps)
    return center * inverse, inverse


def norm_back(values, grad, gain):
    unit, inverse = stat(values)
    scaled = grad * gain
    part = inverse * (
        scaled
        - jnp.mean(scaled, axis=-1, keepdims=True)
        - unit * jnp.mean(scaled * unit, axis=-1, keepdims=True)
    )
    gain_sum = jnp.sum(grad * unit, axis=0, keepdims=True)
    shift_sum = jnp.sum(grad, axis=0, keepdims=True)
    return part, gain_sum, shift_sum


def start_kernel(order, tok, cot, gains, shifts, tok_out, normed, cot_out, cot_low, gains_out, shifts_out, cot_sum):
    values = tok[...]
    mean = jnp.mean(values, axis=-1, keepdims=True)
    center = values - mean
    inverse = lax.rsqrt(jnp.mean(center * center, axis=-1, keepdims=True) + norm_eps)
    cot_sum[...] = jnp.sum(cot[...], axis=0, keepdims=True)
    for at in range(BLOCKS):
        source = lane_block(order, at)
        place = slice(at * LANES, (at + 1) * LANES)
        block = tok[:, source]
        tok_out[:, place] = block
        gain = gains[:, source]
        shift = shifts[:, source]
        gains_out[:, place] = gain
        shifts_out[:, place] = shift
        normed[:, place] = ((block - mean) * inverse * gain[0:1] + shift[0:1]).astype(low)
        other = cot[:, source]
        cot_out[:, place] = other
        cot_low[:, place] = other.astype(low)


def piece_specs(pieces, width, lane=0):
    groups = pieces[0].shape[0]
    cut = groups // 2
    shape = (1, pieces[0].shape[1], width)
    same = pl.BlockSpec(shape, lambda n, *s: (n, 0, lane))
    first = pl.BlockSpec(shape, lambda n, *s: (jnp.minimum(n, cut - 1), 0, lane))
    second = pl.BlockSpec(shape, lambda n, *s: (jnp.maximum(n - cut, 0), 0, lane))
    return [same, same, same, first, second]


def assemble(refs, groups):
    near = [ref[0] for ref in refs[:3]]
    far = jnp.where(pl.program_id(0) < groups // 2, refs[3][0], refs[4][0])
    return jnp.concatenate(near + [far], axis=0)


def whole_spec(*shape):
    return pl.BlockSpec(shape, lambda n, *s: (0,) * len(shape))


def once_spec(*shape):
    return pl.BlockSpec(shape, lambda n, *s: (0,) * len(shape), pipeline_mode=pl.Buffered(1))


def twin_half(rows):
    return pl.BlockSpec((rows, HALF), lambda n, *s: (0, 1), pipeline_mode=pl.Buffered(1))


def group_spec(*shape):
    return pl.BlockSpec((1,) + shape, lambda n, *s: (n,) + (0,) * len(shape))


def grouped(kernel, groups, ins, outs, out_shapes, args, scratch=(), prefetch=0):
    return pl.pallas_call(
        kernel,
        grid_spec=pltpu.PrefetchScalarGridSpec(
            num_scalar_prefetch=prefetch,
            grid=(groups,),
            in_specs=ins,
            out_specs=outs,
            scratch_shapes=list(scratch),
        ),
        out_shape=out_shapes,
        compiler_params=big,
    )(*args)


def struct(shape, dtype):
    return jax.ShapeDtypeStruct(shape, dtype)


def attend_kernel(groups, *refs):
    x, bias = refs[:2]
    own, twin = refs[2:7], refs[7:12]
    packed, mixed, logs = refs[12:]
    value = dot_nn(x[:, :HALF], assemble(own, groups)) + dot_nn(x[:, HALF:], assemble(twin, groups)) + bias[0]
    width = value.shape[1] // 3
    value = value.astype(low)
    packed[0] = value
    lane = lax.broadcasted_iota(jnp.int32, (1, LANES), 1)
    scale = 1.0 / math.sqrt(HEAD)
    rows = value.shape[0]
    log_all = jnp.zeros((rows, LANES), full)
    for pair in range(width // LANES):
        cols = slice(pair * LANES, (pair + 1) * LANES)
        query = value[:, cols]
        key = value[:, width + pair * LANES : width + (pair + 1) * LANES]
        val = value[:, 2 * width + pair * LANES : 2 * width + (pair + 1) * LANES]
        outs = []
        for side in range(2):
            keep = jnp.where(lane // HEAD == side, scale, 0.0).astype(low)
            scores = dot_nt(query * keep, key)
            top = jnp.max(scores, axis=-1, keepdims=True)
            expon = jnp.exp(scores - top)
            total = jnp.sum(expon, axis=-1, keepdims=True)
            outs.append(dot_nn(expon.astype(low), val) / total)
            log_all = jnp.where(lane == 2 * pair + side, top + jnp.log(total), log_all)
        mixed[0, :, cols] = jnp.where(lane < HEAD, outs[0], outs[1]).astype(low)
    logs[0] = log_all.T[:8]


def attend(normed, bias, own, twin):
    groups, _, width = bias.shape
    rows = normed.shape[0]
    return grouped(
        functools.partial(attend_kernel, groups),
        groups,
        [whole_spec(rows, D), group_spec(1, width)] + piece_specs(own, width) + piece_specs(twin, width),
        [group_spec(rows, width), group_spec(rows, width // 3), group_spec(8, rows)],
        [struct((groups, rows, width), low), struct((groups, rows, width // 3), low), struct((groups, 8, rows), full)],
        (normed, bias, *own, *twin),
    )


def attend_back_kernel(groups, *refs):
    grad, packed, logs, normed = refs[:4]
    own, twin = refs[4:9], refs[9:14]
    out, sums, outer = refs[14:]
    upper = (dot_nn(grad[:, :HALF], assemble(own, groups)) + dot_nn(grad[:, HALF:], assemble(twin, groups))).astype(low)
    width = upper.shape[1]
    lane = lax.broadcasted_iota(jnp.int32, (1, LANES), 1)
    scale = 1.0 / math.sqrt(HEAD)
    for pair in range(width // LANES):
        cols = slice(pair * LANES, (pair + 1) * LANES)
        query = packed[0, :, cols]
        key = packed[0, :, width + pair * LANES : width + (pair + 1) * LANES]
        val = packed[0, :, 2 * width + pair * LANES : 2 * width + (pair + 1) * LANES]
        up = upper[:, cols]
        parts = []
        for side in range(2):
            head = 2 * pair + side
            inside = lane // HEAD == side
            scores = dot_nt(key * jnp.where(inside, scale, 0.0).astype(low), query)
            probs = jnp.exp(scores - logs[0, head : head + 1, :])
            val_grad = dot_nn(probs.astype(low), up)
            prob_grad = dot_nt(val * jnp.where(inside, 1.0, 0.0).astype(low), up)
            weighted = probs * prob_grad
            score_grad = (weighted - probs * jnp.sum(weighted, axis=0, keepdims=True)).astype(low)
            key_grad = dot_nn(score_grad, query) * scale
            query_grad = dot_tn(score_grad, key) * scale
            parts.append((query_grad, key_grad, val_grad))
        for kind in range(3):
            both = jnp.where(lane < HEAD, parts[0][kind], parts[1][kind])
            start = kind * width + pair * LANES
            out[0, :, start : start + LANES] = both.astype(low)
            if kind != 1:
                sums[0, kind // 2 : kind // 2 + 1, cols] = jnp.sum(both, axis=0, keepdims=True)
    outer[0] = dot_tn(normed[...], out[0]).astype(low)


def attend_back(grad, packed, logs, normed, own, twin, lane):
    groups, rows, width = packed.shape
    third = width // 3
    return grouped(
        functools.partial(attend_back_kernel, groups),
        groups,
        [whole_spec(rows, D), group_spec(rows, width), group_spec(8, rows), twin_half(rows)]
        + piece_specs(own, third, lane)
        + piece_specs(twin, third, lane),
        [group_spec(rows, width), group_spec(2, third), group_spec(HALF, width)],
        [
            struct((groups, rows, width), low),
            struct((groups, 2, third), full),
            struct((groups, HALF, width), low),
        ],
        (grad, packed, logs, normed, *own, *twin),
    )


def add_parts(groups, inner, own, twin, total):
    total[:, :HALF] += dot_nt(inner[0], assemble(own, groups))
    total[:, HALF:] += dot_nt(inner[0], assemble(twin, groups))


def middle_kernel(groups, *refs):
    mixed, tok, gains, shifts = refs[:4]
    own, twin = refs[4:9], refs[9:14]
    middle, normed, total = refs[14:]
    n = pl.program_id(0)

    @pl.when(n == 0)
    def _():
        total[...] = tok[...] + shifts[2:3]

    add_parts(groups, mixed, own, twin, total)

    @pl.when(n == groups - 1)
    def _():
        values = total[...]
        middle[...] = values
        unit, _ = stat(values)
        normed[...] = (unit * gains[1:2] + shifts[1:2]).astype(low)


def middle_call(mixed, tok, gains, shifts, own, twin, lane):
    groups, rows, width = mixed.shape
    return grouped(
        functools.partial(middle_kernel, groups),
        groups,
        [group_spec(rows, width), whole_spec(rows, D), whole_spec(2, D), whole_spec(4, D)]
        + piece_specs(own, width, lane)
        + piece_specs(twin, width, lane),
        [whole_spec(rows, D), whole_spec(rows, D)],
        [struct((rows, D), full), struct((rows, D), low)],
        (mixed, tok, gains, shifts, *own, *twin),
        scratch=[pltpu.VMEM((rows, D), full)],
    )


def expand_kernel(groups, *refs):
    x, bias, cot = refs[:3]
    own, twin = refs[3:8], refs[8:13]
    active, slope, outer = refs[13:]
    value = dot_nn(x[:, :HALF], assemble(own, groups)) + dot_nn(x[:, HALF:], assemble(twin, groups)) + bias[0]
    phi = 0.5 * (1.0 + lax.erf(value * math.sqrt(0.5)))
    low_active = (value * phi).astype(low)
    active[0] = low_active
    outer[0] = dot_tn(cot[...], low_active).astype(low)
    slope[0] = (phi + value * (jnp.exp(-0.5 * value * value) * (1.0 / math.sqrt(2.0 * math.pi)))).astype(low)


def expand(normed, bias, cot, own, twin):
    groups, rows, width = bias.shape[0], normed.shape[0], bias.shape[2]
    shape = struct((groups, rows, width), low)
    return grouped(
        functools.partial(expand_kernel, groups),
        groups,
        [whole_spec(rows, D), group_spec(1, width), twin_half(rows)]
        + piece_specs(own, width)
        + piece_specs(twin, width),
        [group_spec(rows, width)] * 2 + [group_spec(HALF, width)],
        [shape, shape, struct((groups, HALF, width), low)],
        (normed, bias, cot, *own, *twin),
    )


def hidden_back_kernel(groups, order, *refs):
    grad, slope, active, middle, cot, gains, shifts, normed = refs[:8]
    shrink_own, shrink_twin = refs[8:13], refs[13:18]
    expand_own, expand_twin = refs[18:23], refs[23:28]
    inner, sums, outer, layer, out, out_low, two_sums, total, result = refs[28:]
    n = pl.program_id(0)

    @pl.when(n == 0)
    def _():
        total[...] = jnp.zeros_like(total)
        result[...] = middle[...] + shifts[3:4]

    own, twin = assemble(shrink_own, groups), assemble(shrink_twin, groups)
    value = (dot_nn(grad[:, :HALF], own) + dot_nn(grad[:, HALF:], twin)) * slope[0].astype(full)
    sums[0] = jnp.sum(value, axis=0, keepdims=True)
    low_value = value.astype(low)
    inner[0] = low_value
    result[:, :HALF] += dot_nt(active[0], own)
    result[:, HALF:] += dot_nt(active[0], twin)
    outer[0] = dot_tn(normed[...], low_value).astype(low)
    add_parts(groups, inner, expand_own, expand_twin, total)

    @pl.when(n == groups - 1)
    def _():
        part, gain_sum, shift_sum = norm_back(middle[...], total[...], gains[1:2])
        grad_out = cot[...] + part
        out[...] = grad_out
        out_low[...] = grad_out.astype(low)
        grad_sum = jnp.sum(grad_out, axis=0, keepdims=True)
        for at in range(BLOCKS):
            place = lane_block(order, at)
            cols = slice(at * LANES, (at + 1) * LANES)
            layer[:, place] = result[:, cols]
            two_sums[0:1, place] = gain_sum[:, cols]
            two_sums[1:2, place] = shift_sum[:, cols]
            two_sums[2:3, place] = grad_sum[:, cols]


def hidden_back(order, grad, slope, active, middle, cot, gains, shifts, normed, shrink_own, shrink_twin, own, twin):
    groups, rows, width = slope.shape
    group = group_spec(rows, width)
    pieces = piece_specs(own, width)
    once = once_spec(rows, D)
    return grouped(
        functools.partial(hidden_back_kernel, groups),
        groups,
        [once, group, group, once, once, whole_spec(2, D), whole_spec(4, D), twin_half(rows)] + pieces * 4,
        [group, group_spec(1, width), group_spec(HALF, width), once, once, once, whole_spec(3, D)],
        [
            struct((groups, rows, width), low),
            struct((groups, 1, width), full),
            struct((groups, HALF, width), low),
            struct((rows, D), full),
            struct((rows, D), full),
            struct((rows, D), low),
            struct((3, D), full),
        ],
        (
            order,
            grad,
            slope,
            active,
            middle,
            cot,
            gains,
            shifts,
            normed,
            *shrink_own,
            *shrink_twin,
            *own,
            *twin,
        ),
        scratch=[pltpu.VMEM((rows, D), full), pltpu.VMEM((rows, D), full)],
        prefetch=1,
    )


def outer_twin_kernel(x, inner, out):
    out[0] = dot_tn(x[...], inner[0]).astype(low)


def outer_twin(x, inner):
    groups, rows, width = inner.shape
    return grouped(
        outer_twin_kernel,
        groups,
        [pl.BlockSpec((rows, HALF), lambda n: (0, 1)), group_spec(rows, width)],
        group_spec(HALF, width),
        struct((groups, HALF, width), low),
        (x, inner),
    )


def outer_own_kernel(groups, x, inner, other, mine, to_x, to_y, far_first, far_second):
    value = (dot_tn(x[...], inner[0]) + other[0].astype(full)).astype(low)
    rows = HALF // 4
    mine[0] = value[:rows]
    to_x[0] = value[rows : 2 * rows]
    to_y[0] = value[2 * rows : 3 * rows]
    n = pl.program_id(0)

    @pl.when(n < groups // 2)
    def _():
        far_first[0] = value[3 * rows :]

    @pl.when(n >= groups // 2)
    def _():
        far_second[0] = value[3 * rows :]


def outer_own(x, inner, other):
    groups, rows, width = inner.shape
    near = struct((groups, HALF // 4, width), low)
    far = struct((groups // 2, HALF // 4, width), low)
    shapes = [near, near, near, far, far]
    return grouped(
        functools.partial(outer_own_kernel, groups),
        groups,
        [pl.BlockSpec((rows, HALF), lambda n: (0, 0)), group_spec(rows, width), group_spec(HALF, width)],
        piece_specs(shapes, width),
        shapes,
        (x, inner, other),
    )


def norm_one_kernel(groups, order, *refs):
    inner, tok, grad, gains = refs[:4]
    own, twin = refs[4:9], refs[9:14]
    out, sums, total = refs[14:]
    n = pl.program_id(0)

    @pl.when(n == 0)
    def _():
        total[...] = jnp.zeros_like(total)

    add_parts(groups, inner, own, twin, total)

    @pl.when(n == groups - 1)
    def _():
        part, gain_sum, shift_sum = norm_back(tok[...], total[...], gains[0:1])
        result = grad[...] + part
        for at in range(BLOCKS):
            place = lane_block(order, at)
            cols = slice(at * LANES, (at + 1) * LANES)
            out[:, place] = result[:, cols]
            sums[0:1, place] = gain_sum[:, cols]
            sums[1:2, place] = shift_sum[:, cols]


def norm_one(order, inner, values, grad, gains, own, twin):
    groups, rows, width = inner.shape
    whole = whole_spec(rows, D)
    return grouped(
        functools.partial(norm_one_kernel, groups),
        groups,
        [group_spec(rows, width), whole, whole, whole_spec(2, D)] + piece_specs(own, width) + piece_specs(twin, width),
        [whole, whole_spec(2, D)],
        [struct((rows, D), full), struct((2, D), full)],
        (order, inner, values, grad, gains, *own, *twin),
        scratch=[pltpu.VMEM((rows, D), full)],
        prefetch=1,
    )


def turned_adam_kernel(rate, grad, weight, first, second, grad_out, second_out, weight_out):
    turned = grad[...].T
    grad_out[...] = turned
    second_new, updated = adam_step(weight[...], turned, first[...], second[...], rate, decay_rate)
    second_out[...] = second_new
    weight_out[...] = updated


def turned_adam(rate, grad, weight, first, second):
    return pl.pallas_call(
        functools.partial(turned_adam_kernel, rate),
        out_shape=[struct(weight.shape, full)] * 3,
        compiler_params=big,
    )(grad, weight, first, second)


def swap(values, bit):
    return lax.ppermute(values, "wide", [(at, at ^ bit) for at in range(8)])


def turn(values, step):
    return lax.ppermute(values, "narrow", [(at, (at + step) % 4) for at in range(4)])


def cross(values, bit):
    return lax.ppermute(values, "narrow", [(at, at ^ bit) for at in range(4)])


def fence(*values):
    return lax.optimization_barrier(values)


def plain_gather(block):
    groups = lax.all_gather(block, "narrow", axis=0, tiled=False)
    whole = lax.all_gather(groups, "wide", axis=1, tiled=True)
    rows, cut = HALF // 4, whole.shape[0] // 2
    sides = []
    for side in range(2):
        parts = [whole[:, side * HALF + at * rows : side * HALF + (at + 1) * rows] for at in range(4)]
        sides.append((*parts[:3], parts[3][:cut], parts[3][cut:]))
    return tuple(sides)


def plain_scatter(pieces, twin):
    far = jnp.concatenate(pieces[3:], axis=0)
    whole = jnp.concatenate([*pieces[:3], far, twin], axis=1)
    part = lax.psum_scatter(whole, "wide", scatter_dimension=1, tiled=True)
    return lax.psum_scatter(part, "narrow", scatter_dimension=0, tiled=False).astype(full)


def around(block):
    return [turn(block, step) for step in range(1, 4)]


def near_sends(pieces, from_y, from_x):
    cut = from_y.shape[0]
    to_x = jnp.concatenate([(pieces[1][:cut].astype(full) + from_y.astype(full)).astype(low), pieces[1][cut:]], axis=0)
    to_y = jnp.concatenate([pieces[2][:cut], (pieces[2][cut:].astype(full) + from_x.astype(full)).astype(low)], axis=0)
    return to_x, to_y


def last_sends(mine, over_x, over_y):
    part = (mine.astype(full) + over_x.astype(full) + over_y.astype(full)).astype(low)
    return tuple(part[at] for at in range(4))


def narrow_scatter(mine, over_x, over_y, places):
    part = (mine.astype(full) + over_x.astype(full) + over_y.astype(full)).astype(low)
    parts = [lax.dynamic_index_in_dim(part, places[at], 0, keepdims=False) for at in range(4)]
    return lax.psum_scatter(jnp.stack(parts), "narrow", scatter_dimension=0, tiled=False).astype(full)


def last_sum(first, rest):
    total = first.astype(full)
    for part in rest:
        total = total + part.astype(full)
    return total


def shards(
    tokens,
    cotangent,
    triple_weight,
    output_weight,
    expand_weight,
    shrink_weight,
    norm_gains,
    shift_biases,
    head_biases,
    expand_biases,
    triple_first,
    output_first,
    expand_first,
    shrink_first,
    gains_first,
    shifts_first,
    heads_first,
    widen_first,
    triple_second,
    output_second,
    expand_second,
    shrink_second,
    gains_second,
    shifts_second,
    heads_second,
    widen_second,
    *,
    wide,
    narrow,
):
    tuned = wide == 8 and narrow == 4
    rows = tokens.shape[0]
    local = head_biases.shape[1]
    hidden = expand_biases.shape[0]
    place = lax.axis_index("wide")
    at_narrow = lax.axis_index("narrow")
    if tuned:
        order = jnp.bitwise_xor(place, jnp.array([0, 2, 4, 6, 1, 3, 5, 7], jnp.int32)).astype(jnp.int32)
        steps = [lax.rem(at_narrow + (narrow - at), narrow) for at in range(narrow)]
    else:
        order = jnp.arange(BLOCKS, dtype=jnp.int32)
        steps = list(range(narrow))

    triple_block = jnp.concatenate([triple_weight[:, at].astype(low) for at in range(3)] + [output_weight.astype(low).T], axis=1)
    expand_block = expand_weight.astype(low)
    shrink_block = shrink_weight.astype(low).T
    zeros = jnp.zeros((local,), full)
    bias_rows = jnp.stack([jnp.concatenate([head_biases[0], zeros, head_biases[1], zeros]), expand_biases])

    def begin(order, tokens, cotangent):
        return pl.pallas_call(
            start_kernel,
            in_specs=[pl.BlockSpec(memory_space=pltpu.SMEM)] + [pl.BlockSpec(memory_space=pltpu.VMEM)] * 4,
            out_shape=[
                struct((rows, D), full),
                struct((rows, D), low),
                struct((rows, D), full),
                struct((rows, D), low),
                struct((2, D), full),
                struct((4, D), full),
                struct((1, D), full),
            ],
            compiler_params=big,
        )(order, tokens, cotangent, norm_gains, shift_biases)

    def split_bias(biases):
        return biases[:, 0:1, : 3 * local], biases[:, 1:2]

    if tuned:
        high = lax.reduce_precision(bias_rows, 8, 7)
        rest = bias_rows - high
        mid = lax.reduce_precision(rest, 8, 7)
        parts = jnp.concatenate([high, mid, rest - mid, jnp.zeros((10, hidden), full)]).astype(low)
        ridden = jnp.concatenate([triple_block, parts], axis=0)
        triple_turns = around(ridden)
        begun = begin(order, tokens, cotangent)
        triple_turns, begun, ridden, expand_block, shrink_block = fence(
            triple_turns, begun, ridden, expand_block, shrink_block
        )
        tok, normed, cot, cot_low, gains, shifts, cot_sum = begun
        depth = triple_block.shape[0]
        arrived = [ridden, *triple_turns]
        t_near = jnp.stack([block[:depth] for block in arrived])
        biases = jnp.stack([block[depth:] for block in arrived])
        t_x, t_y = swap(t_near, 2), swap(t_near, 4)
        expand_turns = around(expand_block)
        t_near, t_x, t_y, expand_turns, expand_block, normed, biases = fence(
            t_near, t_x, t_y, expand_turns, expand_block, normed, biases
        )
        t_f, t_g = swap(t_x[:2], 4), swap(t_y[2:], 2)
        t_near_c, t_x_c, t_y_c = swap(t_near, 1), swap(t_x, 1), swap(t_y, 1)
        e_near = jnp.stack([expand_block, *expand_turns])
        biases = biases.astype(full)
        triple_bias, widen_bias = split_bias(biases[:, 0:2] + biases[:, 2:4] + biases[:, 4:6])
        t_f, t_g, t_near_c, t_x_c, t_y_c, e_near, normed, triple_bias, shrink_block = fence(
            t_f, t_g, t_near_c, t_x_c, t_y_c, e_near, normed, triple_bias, shrink_block
        )
        e_x, e_y = swap(e_near, 2), swap(e_near, 4)
        t_f_c, t_g_c = swap(t_f, 1), swap(t_g, 1)
        triple_own = (t_near, t_x, t_y, t_f, t_g)
        triple_twin = (t_near_c, t_x_c, t_y_c, t_f_c, t_g_c)
        triple_twin, normed, shrink_block = fence(triple_twin, normed, shrink_block)
        shrink_turns = around(shrink_block)
        packed, mixed, logs = attend(normed, triple_bias, triple_own, triple_twin)
        e_near, e_x, e_y, mixed, shrink_turns, shrink_block, tok = fence(
            e_near, e_x, e_y, mixed, shrink_turns, shrink_block, tok
        )
        e_f, e_g = swap(e_x[:2], 4), swap(e_y[2:], 2)
        e_near_c, e_x_c, e_y_c = swap(e_near, 1), swap(e_x, 1), swap(e_y, 1)
        middle, normed_two = middle_call(mixed, tok, gains, shifts, triple_own, triple_twin, 3)
        s_near = jnp.stack([shrink_block, *shrink_turns])
        e_f, e_g, e_near_c, e_x_c, e_y_c, s_near, normed_two = fence(
            e_f, e_g, e_near_c, e_x_c, e_y_c, s_near, normed_two
        )
        s_x, s_y = swap(s_near, 2), swap(s_near, 4)
        expand_own = (e_near, e_x, e_y, e_f, e_g)
        expand_twin = (e_near_c, e_x_c, e_y_c, swap(e_f, 1), swap(e_g, 1))
    else:
        tok, normed, cot, cot_low, gains, shifts, cot_sum = begin(order, tokens, cotangent)
        triple_bias, widen_bias = split_bias(lax.all_gather(bias_rows, "narrow", axis=0, tiled=False))
        triple_own, triple_twin = plain_gather(triple_block)
        expand_own, expand_twin = plain_gather(expand_block)
        shrink_own, shrink_twin = plain_gather(shrink_block)
        packed, mixed, logs = attend(normed, triple_bias, triple_own, triple_twin)
        middle, normed_two = middle_call(mixed, tok, gains, shifts, triple_own, triple_twin, 3)

    active, slope, s_twin = expand(normed_two, widen_bias, cot_low, expand_own, expand_twin)
    if tuned:
        s_near, s_x, s_y, s_twin, cot_low, active = fence(s_near, s_x, s_y, s_twin, cot_low, active)
        s_f, s_g = swap(s_x[:2], 4), swap(s_y[2:], 2)
        s_other = swap(s_twin, 1)
        s_near_c, s_x_c = swap(s_near, 1), swap(s_x, 1)
        s_pieces = outer_own(cot_low, active, s_other)
        s_f, s_g, s_pieces, s_near_c, s_x_c, cot_low, slope = fence(
            s_f, s_g, s_pieces, s_near_c, s_x_c, cot_low, slope
        )
        from_y, from_x = swap(s_pieces[3], 4), swap(s_pieces[4], 2)
        shrink_own = (s_near, s_x, s_y, s_f, s_g)
        shrink_twin = (s_near_c, s_x_c, swap(s_y, 1), swap(s_f, 1), swap(s_g, 1))
    else:
        s_pieces = outer_own(cot_low, active, jnp.zeros_like(s_twin))
    expanded_low, widen_sum, e_twin, layer_output, middle_grad, middle_low, two_sums = hidden_back(
        order,
        cot_low,
        slope,
        active,
        middle,
        cot,
        gains,
        shifts,
        normed_two,
        shrink_own,
        shrink_twin,
        expand_own,
        expand_twin,
    )
    if tuned:
        from_y, from_x, expanded_low, e_twin, s_pieces = fence(from_y, from_x, expanded_low, e_twin, s_pieces)
        e_other = swap(e_twin, 1)
        to_x, to_y = near_sends(s_pieces, from_y, from_x)
        s_over_x, s_over_y = swap(to_x, 2), swap(to_y, 4)
    else:
        e_other = jnp.zeros_like(e_twin)
    o_twin = outer_twin(middle_low, mixed)
    if tuned:
        e_other, o_twin, expanded_low = fence(e_other, o_twin, expanded_low)
    e_pieces = outer_own(normed_two, expanded_low, e_other)
    if tuned:
        e_pieces, middle_low, packed, o_twin = fence(e_pieces, middle_low, packed, o_twin)
        from_y, from_x = swap(e_pieces[3], 4), swap(e_pieces[4], 2)
        o_other = swap(o_twin, 1)
    else:
        o_other = jnp.zeros_like(o_twin)
    triple_low, head_sums, t_twin = attend_back(middle_low, packed, logs, normed, triple_own, triple_twin, 3)
    if tuned:
        from_y, from_x, s_over_x, s_over_y, t_twin, triple_low, e_pieces, s_pieces, mixed, o_other = fence(
            from_y, from_x, s_over_x, s_over_y, t_twin, triple_low, e_pieces, s_pieces, mixed, o_other
        )
        t_other = swap(t_twin, 1)
        to_x, to_y = near_sends(e_pieces, from_y, from_x)
        e_over_x, e_over_y = swap(to_x, 2), swap(to_y, 4)
        shrink_grad = narrow_scatter(s_pieces[0], s_over_x, s_over_y, steps)
    else:
        t_other = jnp.zeros_like(t_twin)
    o_pieces = outer_own(middle_low, mixed, o_other)
    if tuned:
        t_other, o_pieces, triple_low, normed = fence(t_other, o_pieces, triple_low, normed)
    t_pieces = outer_own(normed, triple_low, t_other)
    if tuned:
        t_pieces, triple_low = fence(t_pieces, triple_low)
        t_from_y, t_from_x = swap(t_pieces[3], 4), swap(t_pieces[4], 2)
    input_gradient, one_sums = norm_one(
        order, triple_low, tok, middle_grad, gains, triple_own, triple_twin
    )
    turned_heads = jnp.stack([lax.dynamic_index_in_dim(head_sums, step, 0, keepdims=False) for step in steps], axis=1)
    turned_widen = jnp.concatenate([lax.dynamic_index_in_dim(widen_sum, step, 0, keepdims=False) for step in steps])
    small = jnp.concatenate(
        [
            one_sums[0:1],
            two_sums[0:1],
            one_sums[1:2],
            two_sums[1:3],
            cot_sum,
            turned_heads.reshape(2, D),
            turned_widen.reshape(-1, D),
        ],
        axis=0,
    )
    if tuned:
        t_from_y, t_from_x, small, t_pieces, e_over_x, e_over_y, o_pieces = fence(
            t_from_y, t_from_x, small, t_pieces, e_over_x, e_over_y, o_pieces
        )
        to_x, to_y = near_sends(t_pieces, t_from_y, t_from_x)
        to_x, to_y, small, e_over_x, e_over_y, o_pieces = fence(to_x, to_y, small, e_over_x, e_over_y, o_pieces)
        t_over_x, t_over_y = swap(to_x, 2), swap(to_y, 4)
        expand_gradient = narrow_scatter(e_pieces[0], e_over_x, e_over_y, steps)
        from_y, from_x = swap(o_pieces[3], 4), swap(o_pieces[4], 2)
        to_x, to_y = near_sends(o_pieces, from_y, from_x)
        o_over_x, o_over_y = swap(to_x, 2), swap(to_y, 4)
        small = small + swap(small, 1)
        small = small + cross(small, 1)
        shrink_done = turned_adam(0.05, shrink_grad, shrink_weight, shrink_first, shrink_second)
        t_over_x, t_over_y, o_over_x, o_over_y, small, expand_gradient, shrink_done = fence(
            t_over_x, t_over_y, o_over_x, o_over_y, small, expand_gradient, shrink_done
        )
        t_last = last_sends(t_pieces[0], t_over_x, t_over_y)
        t_last, small, expand_gradient, o_over_x, o_over_y = fence(t_last, small, expand_gradient, o_over_x, o_over_y)
        small = small + cross(small, 2)
        small = small + swap(small, 2)
        small = small + swap(small, 4)
        t_back = [turn(t_last[step], -step) for step in range(1, 4)]
        output_grad = narrow_scatter(o_pieces[0], o_over_x, o_over_y, steps)
        triple_grad = last_sum(t_last[0], t_back)
    else:
        small = lax.psum(small, ("wide", "narrow"))
        triple_grad = plain_scatter(t_pieces, t_twin)
        output_grad = plain_scatter(o_pieces, o_twin)
        expand_gradient = plain_scatter(e_pieces, e_twin)
        shrink_grad = plain_scatter(s_pieces, s_twin)
    triple_gradient = jnp.stack([triple_grad[:, at * local : (at + 1) * local] for at in range(3)], axis=1)
    if not tuned:
        shrink_done = turned_adam(0.05, shrink_grad, shrink_weight, shrink_first, shrink_second)
    output_done = turned_adam(1.0, output_grad, output_weight, output_first, output_second)
    gains_gradient = small[0:2]
    shifts_gradient = small[2:6]
    heads_gradient = lax.dynamic_slice_in_dim(small[6:8], at_narrow * local, local, 1)
    widen_gradient = lax.dynamic_slice_in_dim(small[8:].reshape(-1), at_narrow * hidden, hidden, 0)

    params = (
        triple_weight,
        output_weight,
        expand_weight,
        shrink_weight,
        norm_gains,
        shift_biases,
        head_biases,
        expand_biases,
    )
    gradients = (
        triple_gradient,
        output_done[0],
        expand_gradient,
        shrink_done[0],
        gains_gradient,
        shifts_gradient,
        heads_gradient,
        widen_gradient,
    )
    firsts = (
        triple_first,
        output_first,
        expand_first,
        shrink_first,
        gains_first,
        shifts_first,
        heads_first,
        widen_first,
    )
    seconds = (
        triple_second,
        output_second,
        expand_second,
        shrink_second,
        gains_second,
        shifts_second,
        heads_second,
        widen_second,
    )
    rates = (0.1, 1.0, 0.1, 0.05, 1.0, 0.3, 0.2, 0.3)
    decays = (decay_rate, decay_rate, decay_rate, decay_rate, 0.0, 0.0, 0.0, 0.0)
    results = [layer_output, input_gradient]
    for index in range(8):
        if index in (1, 3):
            results.extend(output_done if index == 1 else shrink_done)
            continue
        renewed, updated = adam_step(
            params[index],
            gradients[index],
            firsts[index],
            seconds[index],
            rates[index],
            decays[index],
        )
        if index == 5:
            results.extend([gradients[index], renewed[1:], renewed[0], updated])
        else:
            results.extend([gradients[index], renewed, updated])
    return tuple(results)


def solution(mesh):
    placed = (
        P(("wide", "narrow"), None),
        P(("wide", "narrow"), None),
        P("wide", None, "narrow"),
        P("narrow", "wide"),
        P("wide", "narrow"),
        P("narrow", "wide"),
        P(),
        P(),
        P(None, "narrow"),
        P("narrow"),
        P("wide", None, "narrow"),
        P("narrow", "wide"),
        P("wide", "narrow"),
        P("narrow", "wide"),
        P(),
        P(),
        P(None, "narrow"),
        P("narrow"),
        P("wide", None, "narrow"),
        P("narrow", "wide"),
        P("wide", "narrow"),
        P("narrow", "wide"),
        P(),
        P(),
        P(None, "narrow"),
        P("narrow"),
    )
    matrices = (P("wide", None, "narrow"), P("narrow", "wide"), P("wide", "narrow"), P("narrow", "wide"))
    outs = [P(("wide", "narrow"), None), P(("wide", "narrow"), None)]
    for spec in matrices:
        outs.extend([spec] * 3)
    outs.extend([P()] * 7)
    outs.extend([P(None, "narrow")] * 3)
    outs.extend([P("narrow")] * 3)
    return jax.shard_map(
        functools.partial(shards, wide=mesh.shape["wide"], narrow=mesh.shape["narrow"]),
        mesh=mesh,
        in_specs=placed,
        out_specs=tuple(outs),
        check_vma=False,
    )
```

```python
import functools
import math

import jax
import jax.numpy as jnp
from jax import lax
from jax.experimental import pallas as pl
from jax.experimental.pallas import tpu as pltpu
from jax.sharding import PartitionSpec as P

D = 1024
H = 16
SEQ = 577
STEP = 10
HEAD = D // H
LANES = 128
BLOCKS = D // LANES
HALF = D // 2


norm_eps = 1e-06
beta_first = 0.9
beta_second = 0.999
adam_eps = 1e-08
decay_rate = 0.05

low = jnp.bfloat16
full = jnp.float32
big = pltpu.CompilerParams(vmem_limit_bytes=56 * 1024 * 1024)


def adam_step(weight, grad, first, second, rate, decay):
    first_new = beta_first * first + (1.0 - beta_first) * grad
    second_new = beta_second * second + (1.0 - beta_second) * grad * grad
    first_hat = first_new / (1.0 - beta_first**STEP)
    second_hat = second_new / (1.0 - beta_second**STEP)
    updated = weight - rate * (first_hat / (jnp.sqrt(second_hat) + adam_eps) + decay * weight)
    return (second_new, updated)


def dot_nn(left, right):
    return lax.dot_general(left, right, (((1,), (0,)), ((), ())), preferred_element_type=full)


def dot_nt(left, right):
    return lax.dot_general(left, right, (((1,), (1,)), ((), ())), preferred_element_type=full)


def dot_tn(left, right):
    return lax.dot_general(left, right, (((0,), (0,)), ((), ())), preferred_element_type=full)


def lane_block(order, at):
    return pl.ds(pl.multiple_of(order[at] * LANES, LANES), LANES)


def stat(values):
    center = values - jnp.mean(values, axis=-1, keepdims=True)
    inverse = lax.rsqrt(jnp.mean(center * center, axis=-1, keepdims=True) + norm_eps)
    return center * inverse, inverse


def norm_back(values, grad, gain):
    unit, inverse = stat(values)
    scaled = grad * gain
    part = inverse * (
        scaled
        - jnp.mean(scaled, axis=-1, keepdims=True)
        - unit * jnp.mean(scaled * unit, axis=-1, keepdims=True)
    )
    gain_sum = jnp.sum(grad * unit, axis=0, keepdims=True)
    shift_sum = jnp.sum(grad, axis=0, keepdims=True)
    return part, gain_sum, shift_sum


def start_kernel(order, tok, cot, gains, shifts, tok_out, normed, cot_out, cot_low, gains_out, shifts_out, cot_sum):
    values = tok[...]
    mean = jnp.mean(values, axis=-1, keepdims=True)
    center = values - mean
    inverse = lax.rsqrt(jnp.mean(center * center, axis=-1, keepdims=True) + norm_eps)
    cot_sum[...] = jnp.sum(cot[...], axis=0, keepdims=True)
    for at in range(BLOCKS):
        source = lane_block(order, at)
        place = slice(at * LANES, (at + 1) * LANES)
        block = tok[:, source]
        tok_out[:, place] = block
        gain = gains[:, source]
        shift = shifts[:, source]
        gains_out[:, place] = gain
        shifts_out[:, place] = shift
        normed[:, place] = ((block - mean) * inverse * gain[0:1] + shift[0:1]).astype(low)
        other = cot[:, source]
        cot_out[:, place] = other
        cot_low[:, place] = other.astype(low)


def piece_specs(pieces, width, lane=0):
    groups = pieces[0].shape[0]
    cut = groups // 2
    shape = (1, pieces[0].shape[1], width)
    same = pl.BlockSpec(shape, lambda n, *s: (n, 0, lane))
    first = pl.BlockSpec(shape, lambda n, *s: (jnp.minimum(n, cut - 1), 0, lane))
    second = pl.BlockSpec(shape, lambda n, *s: (jnp.maximum(n - cut, 0), 0, lane))
    return [same, same, same, first, second]


def assemble(refs, groups):
    near = [ref[0] for ref in refs[:3]]
    far = jnp.where(pl.program_id(0) < groups // 2, refs[3][0], refs[4][0])
    return jnp.concatenate(near + [far], axis=0)


def whole_spec(*shape):
    return pl.BlockSpec(shape, lambda n, *s: (0,) * len(shape))


def once_spec(*shape):
    return pl.BlockSpec(shape, lambda n, *s: (0,) * len(shape), pipeline_mode=pl.Buffered(1))


def twin_half(rows):
    return pl.BlockSpec((rows, HALF), lambda n, *s: (0, 1), pipeline_mode=pl.Buffered(1))


def group_spec(*shape):
    return pl.BlockSpec((1,) + shape, lambda n, *s: (n,) + (0,) * len(shape))


def grouped(kernel, groups, ins, outs, out_shapes, args, scratch=(), prefetch=0):
    return pl.pallas_call(
        kernel,
        grid_spec=pltpu.PrefetchScalarGridSpec(
            num_scalar_prefetch=prefetch,
            grid=(groups,),
            in_specs=ins,
            out_specs=outs,
            scratch_shapes=list(scratch),
        ),
        out_shape=out_shapes,
        compiler_params=big,
    )(*args)


def struct(shape, dtype):
    return jax.ShapeDtypeStruct(shape, dtype)


def attend_kernel(groups, *refs):
    x, bias = refs[:2]
    own, twin = refs[2:7], refs[7:12]
    packed, mixed, logs = refs[12:]
    value = dot_nn(x[:, :HALF], assemble(own, groups)) + dot_nn(x[:, HALF:], assemble(twin, groups)) + bias[0]
    width = value.shape[1] // 3
    value = value.astype(low)
    packed[0] = value
    lane = lax.broadcasted_iota(jnp.int32, (1, LANES), 1)
    scale = 1.0 / math.sqrt(HEAD)
    rows = value.shape[0]
    log_all = jnp.zeros((rows, LANES), full)
    for pair in range(width // LANES):
        cols = slice(pair * LANES, (pair + 1) * LANES)
        query = value[:, cols]
        key = value[:, width + pair * LANES : width + (pair + 1) * LANES]
        val = value[:, 2 * width + pair * LANES : 2 * width + (pair + 1) * LANES]
        outs = []
        for side in range(2):
            keep = jnp.where(lane // HEAD == side, scale, 0.0).astype(low)
            scores = dot_nt(query * keep, key)
            top = jnp.max(scores, axis=-1, keepdims=True)
            expon = jnp.exp(scores - top)
            total = jnp.sum(expon, axis=-1, keepdims=True)
            outs.append(dot_nn(expon.astype(low), val) / total)
            log_all = jnp.where(lane == 2 * pair + side, top + jnp.log(total), log_all)
        mixed[0, :, cols] = jnp.where(lane < HEAD, outs[0], outs[1]).astype(low)
    logs[0] = log_all.T[:8]


def attend(normed, bias, own, twin):
    groups, _, width = bias.shape
    rows = normed.shape[0]
    return grouped(
        functools.partial(attend_kernel, groups),
        groups,
        [whole_spec(rows, D), group_spec(1, width)] + piece_specs(own, width) + piece_specs(twin, width),
        [group_spec(rows, width), group_spec(rows, width // 3), group_spec(8, rows)],
        [struct((groups, rows, width), low), struct((groups, rows, width // 3), low), struct((groups, 8, rows), full)],
        (normed, bias, *own, *twin),
    )


def attend_back_kernel(groups, *refs):
    grad, packed, logs, normed = refs[:4]
    own, twin = refs[4:9], refs[9:14]
    out, sums, outer = refs[14:]
    upper = (dot_nn(grad[:, :HALF], assemble(own, groups)) + dot_nn(grad[:, HALF:], assemble(twin, groups))).astype(low)
    width = upper.shape[1]
    lane = lax.broadcasted_iota(jnp.int32, (1, LANES), 1)
    scale = 1.0 / math.sqrt(HEAD)
    for pair in range(width // LANES):
        cols = slice(pair * LANES, (pair + 1) * LANES)
        query = packed[0, :, cols]
        key = packed[0, :, width + pair * LANES : width + (pair + 1) * LANES]
        val = packed[0, :, 2 * width + pair * LANES : 2 * width + (pair + 1) * LANES]
        up = upper[:, cols]
        parts = []
        for side in range(2):
            head = 2 * pair + side
            inside = lane // HEAD == side
            scores = dot_nt(key * jnp.where(inside, scale, 0.0).astype(low), query)
            probs = jnp.exp(scores - logs[0, head : head + 1, :])
            val_grad = dot_nn(probs.astype(low), up)
            prob_grad = dot_nt(val * jnp.where(inside, 1.0, 0.0).astype(low), up)
            weighted = probs * prob_grad
            score_grad = (weighted - probs * jnp.sum(weighted, axis=0, keepdims=True)).astype(low)
            key_grad = dot_nn(score_grad, query) * scale
            query_grad = dot_tn(score_grad, key) * scale
            parts.append((query_grad, key_grad, val_grad))
        for kind in range(3):
            both = jnp.where(lane < HEAD, parts[0][kind], parts[1][kind])
            start = kind * width + pair * LANES
            out[0, :, start : start + LANES] = both.astype(low)
            if kind != 1:
                sums[0, kind // 2 : kind // 2 + 1, cols] = jnp.sum(both, axis=0, keepdims=True)
    outer[0] = dot_tn(normed[...], out[0]).astype(low)


def attend_back(grad, packed, logs, normed, own, twin, lane):
    groups, rows, width = packed.shape
    third = width // 3
    return grouped(
        functools.partial(attend_back_kernel, groups),
        groups,
        [whole_spec(rows, D), group_spec(rows, width), group_spec(8, rows), twin_half(rows)]
        + piece_specs(own, third, lane)
        + piece_specs(twin, third, lane),
        [group_spec(rows, width), group_spec(2, third), group_spec(HALF, width)],
        [
            struct((groups, rows, width), low),
            struct((groups, 2, third), full),
            struct((groups, HALF, width), low),
        ],
        (grad, packed, logs, normed, *own, *twin),
    )


def add_parts(groups, inner, own, twin, total):
    total[:, :HALF] += dot_nt(inner[0], assemble(own, groups))
    total[:, HALF:] += dot_nt(inner[0], assemble(twin, groups))


def middle_kernel(groups, *refs):
    mixed, tok, gains, shifts = refs[:4]
    own, twin = refs[4:9], refs[9:14]
    middle, normed, total = refs[14:]
    n = pl.program_id(0)

    @pl.when(n == 0)
    def _():
        total[...] = tok[...] + shifts[2:3]

    add_parts(groups, mixed, own, twin, total)

    @pl.when(n == groups - 1)
    def _():
        values = total[...]
        middle[...] = values
        unit, _ = stat(values)
        normed[...] = (unit * gains[1:2] + shifts[1:2]).astype(low)


def middle_call(mixed, tok, gains, shifts, own, twin, lane):
    groups, rows, width = mixed.shape
    return grouped(
        functools.partial(middle_kernel, groups),
        groups,
        [group_spec(rows, width), whole_spec(rows, D), whole_spec(2, D), whole_spec(4, D)]
        + piece_specs(own, width, lane)
        + piece_specs(twin, width, lane),
        [whole_spec(rows, D), whole_spec(rows, D)],
        [struct((rows, D), full), struct((rows, D), low)],
        (mixed, tok, gains, shifts, *own, *twin),
        scratch=[pltpu.VMEM((rows, D), full)],
    )


def expand_kernel(groups, *refs):
    x, bias, cot = refs[:3]
    own, twin = refs[3:8], refs[8:13]
    active, slope, outer = refs[13:]
    value = dot_nn(x[:, :HALF], assemble(own, groups)) + dot_nn(x[:, HALF:], assemble(twin, groups)) + bias[0]
    phi = 0.5 * (1.0 + lax.erf(value * math.sqrt(0.5)))
    low_active = (value * phi).astype(low)
    active[0] = low_active
    outer[0] = dot_tn(cot[...], low_active).astype(low)
    slope[0] = (phi + value * (jnp.exp(-0.5 * value * value) * (1.0 / math.sqrt(2.0 * math.pi)))).astype(low)


def expand(normed, bias, cot, own, twin):
    groups, rows, width = bias.shape[0], normed.shape[0], bias.shape[2]
    shape = struct((groups, rows, width), low)
    return grouped(
        functools.partial(expand_kernel, groups),
        groups,
        [whole_spec(rows, D), group_spec(1, width), twin_half(rows)]
        + piece_specs(own, width)
        + piece_specs(twin, width),
        [group_spec(rows, width)] * 2 + [group_spec(HALF, width)],
        [shape, shape, struct((groups, HALF, width), low)],
        (normed, bias, cot, *own, *twin),
    )


def hidden_back_kernel(groups, order, *refs):
    grad, slope, active, middle, cot, gains, shifts, normed = refs[:8]
    shrink_own, shrink_twin = refs[8:13], refs[13:18]
    expand_own, expand_twin = refs[18:23], refs[23:28]
    inner, sums, outer, layer, out, out_low, two_sums, total, result = refs[28:]
    n = pl.program_id(0)

    @pl.when(n == 0)
    def _():
        total[...] = jnp.zeros_like(total)
        result[...] = middle[...] + shifts[3:4]

    own, twin = assemble(shrink_own, groups), assemble(shrink_twin, groups)
    value = (dot_nn(grad[:, :HALF], own) + dot_nn(grad[:, HALF:], twin)) * slope[0].astype(full)
    sums[0] = jnp.sum(value, axis=0, keepdims=True)
    low_value = value.astype(low)
    inner[0] = low_value
    result[:, :HALF] += dot_nt(active[0], own)
    result[:, HALF:] += dot_nt(active[0], twin)
    outer[0] = dot_tn(normed[...], low_value).astype(low)
    add_parts(groups, inner, expand_own, expand_twin, total)

    @pl.when(n == groups - 1)
    def _():
        part, gain_sum, shift_sum = norm_back(middle[...], total[...], gains[1:2])
        grad_out = cot[...] + part
        out[...] = grad_out
        out_low[...] = grad_out.astype(low)
        grad_sum = jnp.sum(grad_out, axis=0, keepdims=True)
        for at in range(BLOCKS):
            place = lane_block(order, at)
            cols = slice(at * LANES, (at + 1) * LANES)
            layer[:, place] = result[:, cols]
            two_sums[0:1, place] = gain_sum[:, cols]
            two_sums[1:2, place] = shift_sum[:, cols]
            two_sums[2:3, place] = grad_sum[:, cols]


def hidden_back(order, grad, slope, active, middle, cot, gains, shifts, normed, shrink_own, shrink_twin, own, twin):
    groups, rows, width = slope.shape
    group = group_spec(rows, width)
    pieces = piece_specs(own, width)
    once = once_spec(rows, D)
    return grouped(
        functools.partial(hidden_back_kernel, groups),
        groups,
        [once, group, group, once, once, whole_spec(2, D), whole_spec(4, D), twin_half(rows)] + pieces * 4,
        [group, group_spec(1, width), group_spec(HALF, width), once, once, once, whole_spec(3, D)],
        [
            struct((groups, rows, width), low),
            struct((groups, 1, width), full),
            struct((groups, HALF, width), low),
            struct((rows, D), full),
            struct((rows, D), full),
            struct((rows, D), low),
            struct((3, D), full),
        ],
        (
            order,
            grad,
            slope,
            active,
            middle,
            cot,
            gains,
            shifts,
            normed,
            *shrink_own,
            *shrink_twin,
            *own,
            *twin,
        ),
        scratch=[pltpu.VMEM((rows, D), full), pltpu.VMEM((rows, D), full)],
        prefetch=1,
    )


def outer_twin_kernel(x, inner, out):
    out[0] = dot_tn(x[...], inner[0]).astype(low)


def outer_twin(x, inner):
    groups, rows, width = inner.shape
    return grouped(
        outer_twin_kernel,
        groups,
        [pl.BlockSpec((rows, HALF), lambda n: (0, 1)), group_spec(rows, width)],
        group_spec(HALF, width),
        struct((groups, HALF, width), low),
        (x, inner),
    )


def outer_own_kernel(groups, x, inner, other, mine, to_x, to_y, far_first, far_second):
    value = (dot_tn(x[...], inner[0]) + other[0].astype(full)).astype(low)
    rows = HALF // 4
    mine[0] = value[:rows]
    to_x[0] = value[rows : 2 * rows]
    to_y[0] = value[2 * rows : 3 * rows]
    n = pl.program_id(0)

    @pl.when(n < groups // 2)
    def _():
        far_first[0] = value[3 * rows :]

    @pl.when(n >= groups // 2)
    def _():
        far_second[0] = value[3 * rows :]


def outer_own(x, inner, other):
    groups, rows, width = inner.shape
    near = struct((groups, HALF // 4, width), low)
    far = struct((groups // 2, HALF // 4, width), low)
    shapes = [near, near, near, far, far]
    return grouped(
        functools.partial(outer_own_kernel, groups),
        groups,
        [pl.BlockSpec((rows, HALF), lambda n: (0, 0)), group_spec(rows, width), group_spec(HALF, width)],
        piece_specs(shapes, width),
        shapes,
        (x, inner, other),
    )


def norm_one_kernel(groups, order, *refs):
    inner, tok, grad, gains = refs[:4]
    own, twin = refs[4:9], refs[9:14]
    out, sums, total = refs[14:]
    n = pl.program_id(0)

    @pl.when(n == 0)
    def _():
        total[...] = jnp.zeros_like(total)

    add_parts(groups, inner, own, twin, total)

    @pl.when(n == groups - 1)
    def _():
        part, gain_sum, shift_sum = norm_back(tok[...], total[...], gains[0:1])
        result = grad[...] + part
        for at in range(BLOCKS):
            place = lane_block(order, at)
            cols = slice(at * LANES, (at + 1) * LANES)
            out[:, place] = result[:, cols]
            sums[0:1, place] = gain_sum[:, cols]
            sums[1:2, place] = shift_sum[:, cols]


def norm_one(order, inner, values, grad, gains, own, twin):
    groups, rows, width = inner.shape
    whole = whole_spec(rows, D)
    return grouped(
        functools.partial(norm_one_kernel, groups),
        groups,
        [group_spec(rows, width), whole, whole, whole_spec(2, D)] + piece_specs(own, width) + piece_specs(twin, width),
        [whole, whole_spec(2, D)],
        [struct((rows, D), full), struct((2, D), full)],
        (order, inner, values, grad, gains, *own, *twin),
        scratch=[pltpu.VMEM((rows, D), full)],
        prefetch=1,
    )


def turned_adam_kernel(rate, grad, weight, first, second, grad_out, second_out, weight_out):
    turned = grad[...].T
    grad_out[...] = turned
    second_new, updated = adam_step(weight[...], turned, first[...], second[...], rate, decay_rate)
    second_out[...] = second_new
    weight_out[...] = updated


def turned_adam(rate, grad, weight, first, second):
    return pl.pallas_call(
        functools.partial(turned_adam_kernel, rate),
        out_shape=[struct(weight.shape, full)] * 3,
        compiler_params=big,
    )(grad, weight, first, second)


def swap(values, bit):
    return lax.ppermute(values, "wide", [(at, at ^ bit) for at in range(8)])


def turn(values, step):
    return lax.ppermute(values, "narrow", [(at, (at + step) % 4) for at in range(4)])


def cross(values, bit):
    return lax.ppermute(values, "narrow", [(at, at ^ bit) for at in range(4)])


def fence(*values):
    return lax.optimization_barrier(values)


def plain_gather(block):
    groups = lax.all_gather(block, "narrow", axis=0, tiled=False)
    whole = lax.all_gather(groups, "wide", axis=1, tiled=True)
    rows, cut = HALF // 4, whole.shape[0] // 2
    sides = []
    for side in range(2):
        parts = [whole[:, side * HALF + at * rows : side * HALF + (at + 1) * rows] for at in range(4)]
        sides.append((*parts[:3], parts[3][:cut], parts[3][cut:]))
    return tuple(sides)


def plain_scatter(pieces, twin):
    far = jnp.concatenate(pieces[3:], axis=0)
    whole = jnp.concatenate([*pieces[:3], far, twin], axis=1)
    part = lax.psum_scatter(whole, "wide", scatter_dimension=1, tiled=True)
    return lax.psum_scatter(part, "narrow", scatter_dimension=0, tiled=False).astype(full)


def around(block):
    return [turn(block, step) for step in range(1, 4)]


def near_sends(pieces, from_y, from_x):
    cut = from_y.shape[0]
    to_x = jnp.concatenate([(pieces[1][:cut].astype(full) + from_y.astype(full)).astype(low), pieces[1][cut:]], axis=0)
    to_y = jnp.concatenate([pieces[2][:cut], (pieces[2][cut:].astype(full) + from_x.astype(full)).astype(low)], axis=0)
    return to_x, to_y


def last_sends(mine, over_x, over_y):
    part = (mine.astype(full) + over_x.astype(full) + over_y.astype(full)).astype(low)
    return tuple(part[at] for at in range(4))


def narrow_scatter(mine, over_x, over_y, places):
    part = (mine.astype(full) + over_x.astype(full) + over_y.astype(full)).astype(low)
    parts = [lax.dynamic_index_in_dim(part, places[at], 0, keepdims=False) for at in range(4)]
    return lax.psum_scatter(jnp.stack(parts), "narrow", scatter_dimension=0, tiled=False).astype(full)


def last_sum(first, rest):
    total = first.astype(full)
    for part in rest:
        total = total + part.astype(full)
    return total


def shards(
    tokens,
    cotangent,
    triple_weight,
    output_weight,
    expand_weight,
    shrink_weight,
    norm_gains,
    shift_biases,
    head_biases,
    expand_biases,
    triple_first,
    output_first,
    expand_first,
    shrink_first,
    gains_first,
    shifts_first,
    heads_first,
    widen_first,
    triple_second,
    output_second,
    expand_second,
    shrink_second,
    gains_second,
    shifts_second,
    heads_second,
    widen_second,
    *,
    wide,
    narrow,
):
    tuned = wide == 8 and narrow == 4
    rows = tokens.shape[0]
    local = head_biases.shape[1]
    hidden = expand_biases.shape[0]
    place = lax.axis_index("wide")
    at_narrow = lax.axis_index("narrow")
    if tuned:
        order = jnp.bitwise_xor(place, jnp.array([0, 2, 4, 6, 1, 3, 5, 7], jnp.int32)).astype(jnp.int32)
        steps = [lax.rem(at_narrow + (narrow - at), narrow) for at in range(narrow)]
    else:
        order = jnp.arange(BLOCKS, dtype=jnp.int32)
        steps = list(range(narrow))

    triple_block = jnp.concatenate([triple_weight[:, at].astype(low) for at in range(3)] + [output_weight.astype(low).T], axis=1)
    expand_block = expand_weight.astype(low)
    shrink_block = shrink_weight.astype(low).T
    zeros = jnp.zeros((local,), full)
    bias_rows = jnp.stack([jnp.concatenate([head_biases[0], zeros, head_biases[1], zeros]), expand_biases])

    def begin(order, tokens, cotangent):
        return pl.pallas_call(
            start_kernel,
            in_specs=[pl.BlockSpec(memory_space=pltpu.SMEM)] + [pl.BlockSpec(memory_space=pltpu.VMEM)] * 4,
            out_shape=[
                struct((rows, D), full),
                struct((rows, D), low),
                struct((rows, D), full),
                struct((rows, D), low),
                struct((2, D), full),
                struct((4, D), full),
                struct((1, D), full),
            ],
            compiler_params=big,
        )(order, tokens, cotangent, norm_gains, shift_biases)

    def split_bias(biases):
        return biases[:, 0:1, : 3 * local], biases[:, 1:2]

    if tuned:
        high = lax.reduce_precision(bias_rows, 8, 7)
        rest = bias_rows - high
        mid = lax.reduce_precision(rest, 8, 7)
        parts = jnp.concatenate([high, mid, rest - mid, jnp.zeros((10, hidden), full)]).astype(low)
        ridden = jnp.concatenate([triple_block, parts], axis=0)
        triple_turns = around(ridden)
        begun = begin(order, tokens, cotangent)
        triple_turns, begun, ridden, expand_block, shrink_block = fence(
            triple_turns, begun, ridden, expand_block, shrink_block
        )
        tok, normed, cot, cot_low, gains, shifts, cot_sum = begun
        depth = triple_block.shape[0]
        arrived = [ridden, *triple_turns]
        t_near = jnp.stack([block[:depth] for block in arrived])
        biases = jnp.stack([block[depth:] for block in arrived])
        t_x, t_y = swap(t_near, 2), swap(t_near, 4)
        expand_turns = around(expand_block)
        t_near, t_x, t_y, expand_turns, expand_block, normed, biases = fence(
            t_near, t_x, t_y, expand_turns, expand_block, normed, biases
        )
        t_f, t_g = swap(t_x[:2], 4), swap(t_y[2:], 2)
        t_near_c, t_x_c, t_y_c = swap(t_near, 1), swap(t_x, 1), swap(t_y, 1)
        e_near = jnp.stack([expand_block, *expand_turns])
        biases = biases.astype(full)
        triple_bias, widen_bias = split_bias(biases[:, 0:2] + biases[:, 2:4] + biases[:, 4:6])
        t_f, t_g, t_near_c, t_x_c, t_y_c, e_near, normed, triple_bias, shrink_block = fence(
            t_f, t_g, t_near_c, t_x_c, t_y_c, e_near, normed, triple_bias, shrink_block
        )
        e_x, e_y = swap(e_near, 2), swap(e_near, 4)
        t_f_c, t_g_c = swap(t_f, 1), swap(t_g, 1)
        triple_own = (t_near, t_x, t_y, t_f, t_g)
        triple_twin = (t_near_c, t_x_c, t_y_c, t_f_c, t_g_c)
        triple_twin, normed, shrink_block = fence(triple_twin, normed, shrink_block)
        shrink_turns = around(shrink_block)
        packed, mixed, logs = attend(normed, triple_bias, triple_own, triple_twin)
        e_near, e_x, e_y, mixed, shrink_turns, shrink_block, tok = fence(
            e_near, e_x, e_y, mixed, shrink_turns, shrink_block, tok
        )
        e_f, e_g = swap(e_x[:2], 4), swap(e_y[2:], 2)
        e_near_c, e_x_c, e_y_c = swap(e_near, 1), swap(e_x, 1), swap(e_y, 1)
        middle, normed_two = middle_call(mixed, tok, gains, shifts, triple_own, triple_twin, 3)
        s_near = jnp.stack([shrink_block, *shrink_turns])
        e_f, e_g, e_near_c, e_x_c, e_y_c, s_near, normed_two = fence(
            e_f, e_g, e_near_c, e_x_c, e_y_c, s_near, normed_two
        )
        s_x, s_y = swap(s_near, 2), swap(s_near, 4)
        expand_own = (e_near, e_x, e_y, e_f, e_g)
        expand_twin = (e_near_c, e_x_c, e_y_c, swap(e_f, 1), swap(e_g, 1))
    else:
        tok, normed, cot, cot_low, gains, shifts, cot_sum = begin(order, tokens, cotangent)
        triple_bias, widen_bias = split_bias(lax.all_gather(bias_rows, "narrow", axis=0, tiled=False))
        triple_own, triple_twin = plain_gather(triple_block)
        expand_own, expand_twin = plain_gather(expand_block)
        shrink_own, shrink_twin = plain_gather(shrink_block)
        packed, mixed, logs = attend(normed, triple_bias, triple_own, triple_twin)
        middle, normed_two = middle_call(mixed, tok, gains, shifts, triple_own, triple_twin, 3)

    active, slope, s_twin = expand(normed_two, widen_bias, cot_low, expand_own, expand_twin)
    if tuned:
        s_other = swap(s_twin, 1)
        s_near, s_x, s_y, cot_low, active = fence(s_near, s_x, s_y, cot_low, active)
        s_f, s_g = swap(s_x[:2], 4), swap(s_y[2:], 2)
        s_near_c, s_x_c = swap(s_near, 1), swap(s_x, 1)
        s_pieces = outer_own(cot_low, active, s_other)
        s_f, s_g, s_pieces, s_near_c, s_x_c, cot_low, slope = fence(
            s_f, s_g, s_pieces, s_near_c, s_x_c, cot_low, slope
        )
        from_y, from_x = swap(s_pieces[3], 4), swap(s_pieces[4], 2)
        shrink_own = (s_near, s_x, s_y, s_f, s_g)
        shrink_twin = (s_near_c, s_x_c, swap(s_y, 1), swap(s_f, 1), swap(s_g, 1))
    else:
        s_pieces = outer_own(cot_low, active, jnp.zeros_like(s_twin))
    expanded_low, widen_sum, e_twin, layer_output, middle_grad, middle_low, two_sums = hidden_back(
        order,
        cot_low,
        slope,
        active,
        middle,
        cot,
        gains,
        shifts,
        normed_two,
        shrink_own,
        shrink_twin,
        expand_own,
        expand_twin,
    )
    if tuned:
        from_y, from_x, expanded_low, e_twin, s_pieces = fence(from_y, from_x, expanded_low, e_twin, s_pieces)
        e_other = swap(e_twin, 1)
        to_x, to_y = near_sends(s_pieces, from_y, from_x)
        s_over_x, s_over_y = swap(to_x, 2), swap(to_y, 4)
    else:
        e_other = jnp.zeros_like(e_twin)
    o_twin = outer_twin(middle_low, mixed)
    if tuned:
        e_other, o_twin, expanded_low = fence(e_other, o_twin, expanded_low)
    e_pieces = outer_own(normed_two, expanded_low, e_other)
    if tuned:
        e_pieces, middle_low, packed, o_twin = fence(e_pieces, middle_low, packed, o_twin)
        from_y, from_x = swap(e_pieces[3], 4), swap(e_pieces[4], 2)
        o_other = swap(o_twin, 1)
    else:
        o_other = jnp.zeros_like(o_twin)
    triple_low, head_sums, t_twin = attend_back(middle_low, packed, logs, normed, triple_own, triple_twin, 3)
    if tuned:
        from_y, from_x, s_over_x, s_over_y, t_twin, triple_low, e_pieces, s_pieces, mixed, o_other = fence(
            from_y, from_x, s_over_x, s_over_y, t_twin, triple_low, e_pieces, s_pieces, mixed, o_other
        )
        t_other = swap(t_twin, 1)
        to_x, to_y = near_sends(e_pieces, from_y, from_x)
        to_x, to_y, t_other, triple_low, normed, o_other, s_over_x, s_over_y = fence(
            to_x, to_y, t_other, triple_low, normed, o_other, s_over_x, s_over_y
        )
        e_over_x, e_over_y = swap(to_x, 2), swap(to_y, 4)
    else:
        t_other = jnp.zeros_like(t_twin)
    t_pieces = outer_own(normed, triple_low, t_other)
    if tuned:
        t_pieces, triple_low, o_other, s_over_x, s_over_y = fence(t_pieces, triple_low, o_other, s_over_x, s_over_y)
        t_from_y, t_from_x = swap(t_pieces[3], 4), swap(t_pieces[4], 2)
        shrink_grad = narrow_scatter(s_pieces[0], s_over_x, s_over_y, steps)
    o_pieces = outer_own(middle_low, mixed, o_other)
    input_gradient, one_sums = norm_one(
        order, triple_low, tok, middle_grad, gains, triple_own, triple_twin
    )
    turned_heads = jnp.stack([lax.dynamic_index_in_dim(head_sums, step, 0, keepdims=False) for step in steps], axis=1)
    turned_widen = jnp.concatenate([lax.dynamic_index_in_dim(widen_sum, step, 0, keepdims=False) for step in steps])
    small = jnp.concatenate(
        [
            one_sums[0:1],
            two_sums[0:1],
            one_sums[1:2],
            two_sums[1:3],
            cot_sum,
            turned_heads.reshape(2, D),
            turned_widen.reshape(-1, D),
        ],
        axis=0,
    )
    if tuned:
        t_from_y, t_from_x, small, t_pieces, e_over_x, e_over_y, o_pieces = fence(
            t_from_y, t_from_x, small, t_pieces, e_over_x, e_over_y, o_pieces
        )
        to_x, to_y = near_sends(t_pieces, t_from_y, t_from_x)
        to_x, to_y, small, e_over_x, e_over_y, o_pieces = fence(to_x, to_y, small, e_over_x, e_over_y, o_pieces)
        t_over_x, t_over_y = swap(to_x, 2), swap(to_y, 4)
        expand_gradient = narrow_scatter(e_pieces[0], e_over_x, e_over_y, steps)
        from_y, from_x = swap(o_pieces[3], 4), swap(o_pieces[4], 2)
        to_x, to_y = near_sends(o_pieces, from_y, from_x)
        o_over_x, o_over_y = swap(to_x, 2), swap(to_y, 4)
        small = small + swap(small, 1)
        small = small + cross(small, 1)
        small = small + cross(small, 2)
        shrink_done = turned_adam(0.05, shrink_grad, shrink_weight, shrink_first, shrink_second)
        t_over_x, t_over_y, o_over_x, o_over_y, small, expand_gradient, shrink_done = fence(
            t_over_x, t_over_y, o_over_x, o_over_y, small, expand_gradient, shrink_done
        )
        t_last = last_sends(t_pieces[0], t_over_x, t_over_y)
        t_last, small, expand_gradient, o_over_x, o_over_y = fence(t_last, small, expand_gradient, o_over_x, o_over_y)
        small = small + swap(small, 2)
        small = small + swap(small, 4)
        t_back = [turn(t_last[step], -step) for step in range(1, 4)]
        output_grad = narrow_scatter(o_pieces[0], o_over_x, o_over_y, steps)
        output_done = turned_adam(1.0, output_grad, output_weight, output_first, output_second)
        t_back, output_done = fence(t_back, output_done)
        triple_grad = last_sum(t_last[0], t_back)
    else:
        small = lax.psum(small, ("wide", "narrow"))
        triple_grad = plain_scatter(t_pieces, t_twin)
        output_grad = plain_scatter(o_pieces, o_twin)
        expand_gradient = plain_scatter(e_pieces, e_twin)
        shrink_grad = plain_scatter(s_pieces, s_twin)
    triple_gradient = jnp.stack([triple_grad[:, at * local : (at + 1) * local] for at in range(3)], axis=1)
    if not tuned:
        shrink_done = turned_adam(0.05, shrink_grad, shrink_weight, shrink_first, shrink_second)
        output_done = turned_adam(1.0, output_grad, output_weight, output_first, output_second)
    gains_gradient = small[0:2]
    shifts_gradient = small[2:6]
    heads_gradient = lax.dynamic_slice_in_dim(small[6:8], at_narrow * local, local, 1)
    widen_gradient = lax.dynamic_slice_in_dim(small[8:].reshape(-1), at_narrow * hidden, hidden, 0)

    params = (
        triple_weight,
        output_weight,
        expand_weight,
        shrink_weight,
        norm_gains,
        shift_biases,
        head_biases,
        expand_biases,
    )
    gradients = (
        triple_gradient,
        output_done[0],
        expand_gradient,
        shrink_done[0],
        gains_gradient,
        shifts_gradient,
        heads_gradient,
        widen_gradient,
    )
    firsts = (
        triple_first,
        output_first,
        expand_first,
        shrink_first,
        gains_first,
        shifts_first,
        heads_first,
        widen_first,
    )
    seconds = (
        triple_second,
        output_second,
        expand_second,
        shrink_second,
        gains_second,
        shifts_second,
        heads_second,
        widen_second,
    )
    rates = (0.1, 1.0, 0.1, 0.05, 1.0, 0.3, 0.2, 0.3)
    decays = (decay_rate, decay_rate, decay_rate, decay_rate, 0.0, 0.0, 0.0, 0.0)
    results = [layer_output, input_gradient]
    for index in range(8):
        if index in (1, 3):
            results.extend(output_done if index == 1 else shrink_done)
            continue
        renewed, updated = adam_step(
            params[index],
            gradients[index],
            firsts[index],
            seconds[index],
            rates[index],
            decays[index],
        )
        if index == 5:
            results.extend([gradients[index], renewed[1:], renewed[0], updated])
        else:
            results.extend([gradients[index], renewed, updated])
    return tuple(results)


def solution(mesh):
    placed = (
        P(("wide", "narrow"), None),
        P(("wide", "narrow"), None),
        P("wide", None, "narrow"),
        P("narrow", "wide"),
        P("wide", "narrow"),
        P("narrow", "wide"),
        P(),
        P(),
        P(None, "narrow"),
        P("narrow"),
        P("wide", None, "narrow"),
        P("narrow", "wide"),
        P("wide", "narrow"),
        P("narrow", "wide"),
        P(),
        P(),
        P(None, "narrow"),
        P("narrow"),
        P("wide", None, "narrow"),
        P("narrow", "wide"),
        P("wide", "narrow"),
        P("narrow", "wide"),
        P(),
        P(),
        P(None, "narrow"),
        P("narrow"),
    )
    matrices = (P("wide", None, "narrow"), P("narrow", "wide"), P("wide", "narrow"), P("narrow", "wide"))
    outs = [P(("wide", "narrow"), None), P(("wide", "narrow"), None)]
    for spec in matrices:
        outs.extend([spec] * 3)
    outs.extend([P()] * 7)
    outs.extend([P(None, "narrow")] * 3)
    outs.extend([P("narrow")] * 3)
    return jax.shard_map(
        functools.partial(shards, wide=mesh.shape["wide"], narrow=mesh.shape["narrow"]),
        mesh=mesh,
        in_specs=placed,
        out_specs=tuple(outs),
        check_vma=False,
    )
```

```python
import functools
import math

import jax
import jax.numpy as jnp
from jax import lax
from jax.experimental import pallas as pl
from jax.experimental.pallas import tpu as pltpu
from jax.sharding import PartitionSpec as P

D = 1024
H = 16
SEQ = 577
STEP = 10
HEAD = D // H
LANES = 128
BLOCKS = D // LANES
HALF = D // 2


norm_eps = 1e-06
beta_first = 0.9
beta_second = 0.999
adam_eps = 1e-08
decay_rate = 0.05

low = jnp.bfloat16
full = jnp.float32
big = pltpu.CompilerParams(vmem_limit_bytes=56 * 1024 * 1024)


def adam_step(weight, grad, first, second, rate, decay):
    first_new = beta_first * first + (1.0 - beta_first) * grad
    second_new = beta_second * second + (1.0 - beta_second) * grad * grad
    first_hat = first_new / (1.0 - beta_first**STEP)
    second_hat = second_new / (1.0 - beta_second**STEP)
    updated = weight - rate * (first_hat / (jnp.sqrt(second_hat) + adam_eps) + decay * weight)
    return (second_new, updated)


def dot_nn(left, right):
    return lax.dot_general(left, right, (((1,), (0,)), ((), ())), preferred_element_type=full)


def dot_nt(left, right):
    return lax.dot_general(left, right, (((1,), (1,)), ((), ())), preferred_element_type=full)


def dot_tn(left, right):
    return lax.dot_general(left, right, (((0,), (0,)), ((), ())), preferred_element_type=full)


def lane_block(order, at):
    return pl.ds(pl.multiple_of(order[at] * LANES, LANES), LANES)


def stat(values):
    center = values - jnp.mean(values, axis=-1, keepdims=True)
    inverse = lax.rsqrt(jnp.mean(center * center, axis=-1, keepdims=True) + norm_eps)
    return center * inverse, inverse


def norm_back(values, grad, gain):
    unit, inverse = stat(values)
    scaled = grad * gain
    part = inverse * (
        scaled
        - jnp.mean(scaled, axis=-1, keepdims=True)
        - unit * jnp.mean(scaled * unit, axis=-1, keepdims=True)
    )
    gain_sum = jnp.sum(grad * unit, axis=0, keepdims=True)
    shift_sum = jnp.sum(grad, axis=0, keepdims=True)
    return part, gain_sum, shift_sum


def start_kernel(order, tok, cot, gains, shifts, tok_out, normed, cot_out, cot_low, gains_out, shifts_out, cot_sum):
    values = tok[...]
    mean = jnp.mean(values, axis=-1, keepdims=True)
    center = values - mean
    inverse = lax.rsqrt(jnp.mean(center * center, axis=-1, keepdims=True) + norm_eps)
    cot_sum[...] = jnp.sum(cot[...], axis=0, keepdims=True)
    for at in range(BLOCKS):
        source = lane_block(order, at)
        place = slice(at * LANES, (at + 1) * LANES)
        block = tok[:, source]
        tok_out[:, place] = block
        gain = gains[:, source]
        shift = shifts[:, source]
        gains_out[:, place] = gain
        shifts_out[:, place] = shift
        normed[:, place] = ((block - mean) * inverse * gain[0:1] + shift[0:1]).astype(low)
        other = cot[:, source]
        cot_out[:, place] = other
        cot_low[:, place] = other.astype(low)


def piece_specs(pieces, width, lane=0):
    groups = pieces[0].shape[0]
    cut = groups // 2
    shape = (1, pieces[0].shape[1], width)
    same = pl.BlockSpec(shape, lambda n, *s: (n, 0, lane))
    first = pl.BlockSpec(shape, lambda n, *s: (jnp.minimum(n, cut - 1), 0, lane))
    second = pl.BlockSpec(shape, lambda n, *s: (jnp.maximum(n - cut, 0), 0, lane))
    return [same, same, same, first, second]


def assemble(refs, groups):
    near = [ref[0] for ref in refs[:3]]
    far = jnp.where(pl.program_id(0) < groups // 2, refs[3][0], refs[4][0])
    return jnp.concatenate(near + [far], axis=0)


def whole_spec(*shape):
    return pl.BlockSpec(shape, lambda n, *s: (0,) * len(shape))


def once_spec(*shape):
    return pl.BlockSpec(shape, lambda n, *s: (0,) * len(shape), pipeline_mode=pl.Buffered(1))


def late_spec():
    return pl.BlockSpec(memory_space=pl.ANY)


def late_scratch(rows):
    return [pltpu.VMEM((rows, D), full), pltpu.VMEM((rows, D), full), pltpu.SemaphoreType.DMA((2,))]


def late_copies(sources, targets, sems):
    return [pltpu.make_async_copy(sources[at], targets[at], sems.at[at]) for at in range(2)]


def twin_half(rows):
    return pl.BlockSpec((rows, HALF), lambda n, *s: (0, 1), pipeline_mode=pl.Buffered(1))


def group_spec(*shape):
    return pl.BlockSpec((1,) + shape, lambda n, *s: (n,) + (0,) * len(shape))


def grouped(kernel, groups, ins, outs, out_shapes, args, scratch=(), prefetch=0):
    return pl.pallas_call(
        kernel,
        grid_spec=pltpu.PrefetchScalarGridSpec(
            num_scalar_prefetch=prefetch,
            grid=(groups,),
            in_specs=ins,
            out_specs=outs,
            scratch_shapes=list(scratch),
        ),
        out_shape=out_shapes,
        compiler_params=big,
    )(*args)


def struct(shape, dtype):
    return jax.ShapeDtypeStruct(shape, dtype)


def attend_kernel(groups, *refs):
    x, bias = refs[:2]
    own, twin = refs[2:7], refs[7:12]
    packed, mixed, logs = refs[12:]
    value = dot_nn(x[:, :HALF], assemble(own, groups)) + dot_nn(x[:, HALF:], assemble(twin, groups)) + bias[0]
    width = value.shape[1] // 3
    value = value.astype(low)
    packed[0] = value
    lane = lax.broadcasted_iota(jnp.int32, (1, LANES), 1)
    scale = 1.0 / math.sqrt(HEAD)
    rows = value.shape[0]
    log_all = jnp.zeros((rows, LANES), full)
    for pair in range(width // LANES):
        cols = slice(pair * LANES, (pair + 1) * LANES)
        query = value[:, cols]
        key = value[:, width + pair * LANES : width + (pair + 1) * LANES]
        val = value[:, 2 * width + pair * LANES : 2 * width + (pair + 1) * LANES]
        outs = []
        for side in range(2):
            keep = jnp.where(lane // HEAD == side, scale, 0.0).astype(low)
            scores = dot_nt(query * keep, key)
            top = jnp.max(scores, axis=-1, keepdims=True)
            expon = jnp.exp(scores - top)
            total = jnp.sum(expon, axis=-1, keepdims=True)
            outs.append(dot_nn(expon.astype(low), val) / total)
            log_all = jnp.where(lane == 2 * pair + side, top + jnp.log(total), log_all)
        mixed[0, :, cols] = jnp.where(lane < HEAD, outs[0], outs[1]).astype(low)
    logs[0] = log_all.T[:8]


def attend(normed, bias, own, twin):
    groups, _, width = bias.shape
    rows = normed.shape[0]
    return grouped(
        functools.partial(attend_kernel, groups),
        groups,
        [whole_spec(rows, D), group_spec(1, width)] + piece_specs(own, width) + piece_specs(twin, width),
        [group_spec(rows, width), group_spec(rows, width // 3), group_spec(8, rows)],
        [struct((groups, rows, width), low), struct((groups, rows, width // 3), low), struct((groups, 8, rows), full)],
        (normed, bias, *own, *twin),
    )


def attend_back_kernel(groups, *refs):
    grad, packed, logs, normed = refs[:4]
    own, twin = refs[4:9], refs[9:14]
    out, sums, outer = refs[14:]
    upper = (dot_nn(grad[:, :HALF], assemble(own, groups)) + dot_nn(grad[:, HALF:], assemble(twin, groups))).astype(low)
    width = upper.shape[1]
    lane = lax.broadcasted_iota(jnp.int32, (1, LANES), 1)
    scale = 1.0 / math.sqrt(HEAD)
    for pair in range(width // LANES):
        cols = slice(pair * LANES, (pair + 1) * LANES)
        query = packed[0, :, cols]
        key = packed[0, :, width + pair * LANES : width + (pair + 1) * LANES]
        val = packed[0, :, 2 * width + pair * LANES : 2 * width + (pair + 1) * LANES]
        up = upper[:, cols]
        parts = []
        for side in range(2):
            head = 2 * pair + side
            inside = lane // HEAD == side
            scores = dot_nt(key * jnp.where(inside, scale, 0.0).astype(low), query)
            probs = jnp.exp(scores - logs[0, head : head + 1, :])
            val_grad = dot_nn(probs.astype(low), up)
            prob_grad = dot_nt(val * jnp.where(inside, 1.0, 0.0).astype(low), up)
            weighted = probs * prob_grad
            score_grad = (weighted - probs * jnp.sum(weighted, axis=0, keepdims=True)).astype(low)
            key_grad = dot_nn(score_grad, query) * scale
            query_grad = dot_tn(score_grad, key) * scale
            parts.append((query_grad, key_grad, val_grad))
        for kind in range(3):
            both = jnp.where(lane < HEAD, parts[0][kind], parts[1][kind])
            start = kind * width + pair * LANES
            out[0, :, start : start + LANES] = both.astype(low)
            if kind != 1:
                sums[0, kind // 2 : kind // 2 + 1, cols] = jnp.sum(both, axis=0, keepdims=True)
    outer[0] = dot_tn(normed[...], out[0]).astype(low)


def attend_back(grad, packed, logs, normed, own, twin, lane):
    groups, rows, width = packed.shape
    third = width // 3
    return grouped(
        functools.partial(attend_back_kernel, groups),
        groups,
        [whole_spec(rows, D), group_spec(rows, width), group_spec(8, rows), twin_half(rows)]
        + piece_specs(own, third, lane)
        + piece_specs(twin, third, lane),
        [group_spec(rows, width), group_spec(2, third), group_spec(HALF, width)],
        [
            struct((groups, rows, width), low),
            struct((groups, 2, third), full),
            struct((groups, HALF, width), low),
        ],
        (grad, packed, logs, normed, *own, *twin),
    )


def add_parts(groups, inner, own, twin, total):
    total[:, :HALF] += dot_nt(inner[0], assemble(own, groups))
    total[:, HALF:] += dot_nt(inner[0], assemble(twin, groups))


def middle_kernel(groups, *refs):
    mixed, tok, gains, shifts = refs[:4]
    own, twin = refs[4:9], refs[9:14]
    middle, normed, total = refs[14:]
    n = pl.program_id(0)

    @pl.when(n == 0)
    def _():
        total[...] = tok[...] + shifts[2:3]

    add_parts(groups, mixed, own, twin, total)

    @pl.when(n == groups - 1)
    def _():
        values = total[...]
        middle[...] = values
        unit, _ = stat(values)
        normed[...] = (unit * gains[1:2] + shifts[1:2]).astype(low)


def middle_call(mixed, tok, gains, shifts, own, twin, lane):
    groups, rows, width = mixed.shape
    return grouped(
        functools.partial(middle_kernel, groups),
        groups,
        [group_spec(rows, width), whole_spec(rows, D), whole_spec(2, D), whole_spec(4, D)]
        + piece_specs(own, width, lane)
        + piece_specs(twin, width, lane),
        [whole_spec(rows, D), whole_spec(rows, D)],
        [struct((rows, D), full), struct((rows, D), low)],
        (mixed, tok, gains, shifts, *own, *twin),
        scratch=[pltpu.VMEM((rows, D), full)],
    )


def expand_kernel(groups, *refs):
    x, bias, cot = refs[:3]
    own, twin = refs[3:8], refs[8:13]
    active, slope, outer = refs[13:]
    value = dot_nn(x[:, :HALF], assemble(own, groups)) + dot_nn(x[:, HALF:], assemble(twin, groups)) + bias[0]
    phi = 0.5 * (1.0 + lax.erf(value * math.sqrt(0.5)))
    low_active = (value * phi).astype(low)
    active[0] = low_active
    outer[0] = dot_tn(cot[...], low_active).astype(low)
    slope[0] = (phi + value * (jnp.exp(-0.5 * value * value) * (1.0 / math.sqrt(2.0 * math.pi)))).astype(low)


def expand(normed, bias, cot, own, twin):
    groups, rows, width = bias.shape[0], normed.shape[0], bias.shape[2]
    shape = struct((groups, rows, width), low)
    return grouped(
        functools.partial(expand_kernel, groups),
        groups,
        [whole_spec(rows, D), group_spec(1, width), twin_half(rows)]
        + piece_specs(own, width)
        + piece_specs(twin, width),
        [group_spec(rows, width)] * 2 + [group_spec(HALF, width)],
        [shape, shape, struct((groups, HALF, width), low)],
        (normed, bias, cot, *own, *twin),
    )


def hidden_back_kernel(groups, order, *refs):
    grad, slope, active, middle, cot, gains, shifts, normed = refs[:8]
    shrink_own, shrink_twin = refs[8:13], refs[13:18]
    expand_own, expand_twin = refs[18:23], refs[23:28]
    inner, sums, outer, layer, out, out_low, two_sums, total, result, middle_late, cot_late, sems = refs[28:]
    n = pl.program_id(0)
    copies = late_copies((middle, cot), (middle_late, cot_late), sems)

    @pl.when(n == 0)
    def _():
        for copy in copies:
            copy.start()
        total[...] = jnp.zeros_like(total)
        result[...] = jnp.zeros_like(result)

    own, twin = assemble(shrink_own, groups), assemble(shrink_twin, groups)
    value = (dot_nn(grad[:, :HALF], own) + dot_nn(grad[:, HALF:], twin)) * slope[0].astype(full)
    sums[0] = jnp.sum(value, axis=0, keepdims=True)
    low_value = value.astype(low)
    inner[0] = low_value
    result[:, :HALF] += dot_nt(active[0], own)
    result[:, HALF:] += dot_nt(active[0], twin)
    outer[0] = dot_tn(normed[...], low_value).astype(low)
    add_parts(groups, inner, expand_own, expand_twin, total)

    @pl.when(n == groups - 1)
    def _():
        for copy in copies:
            copy.wait()
        part, gain_sum, shift_sum = norm_back(middle_late[...], total[...], gains[1:2])
        grad_out = cot_late[...] + part
        out[...] = grad_out
        out_low[...] = grad_out.astype(low)
        grad_sum = jnp.sum(grad_out, axis=0, keepdims=True)
        for at in range(BLOCKS):
            place = lane_block(order, at)
            cols = slice(at * LANES, (at + 1) * LANES)
            layer[:, place] = result[:, cols] + middle_late[:, cols] + shifts[3:4, cols]
            two_sums[0:1, place] = gain_sum[:, cols]
            two_sums[1:2, place] = shift_sum[:, cols]
            two_sums[2:3, place] = grad_sum[:, cols]


def hidden_back(order, grad, slope, active, middle, cot, gains, shifts, normed, shrink_own, shrink_twin, own, twin):
    groups, rows, width = slope.shape
    group = group_spec(rows, width)
    pieces = piece_specs(own, width)
    once = once_spec(rows, D)
    return grouped(
        functools.partial(hidden_back_kernel, groups),
        groups,
        [once, group, group, late_spec(), late_spec(), whole_spec(2, D), whole_spec(4, D), twin_half(rows)]
        + pieces * 4,
        [group, group_spec(1, width), group_spec(HALF, width), once, once, once, whole_spec(3, D)],
        [
            struct((groups, rows, width), low),
            struct((groups, 1, width), full),
            struct((groups, HALF, width), low),
            struct((rows, D), full),
            struct((rows, D), full),
            struct((rows, D), low),
            struct((3, D), full),
        ],
        (
            order,
            grad,
            slope,
            active,
            middle,
            cot,
            gains,
            shifts,
            normed,
            *shrink_own,
            *shrink_twin,
            *own,
            *twin,
        ),
        scratch=[pltpu.VMEM((rows, D), full), pltpu.VMEM((rows, D), full)] + late_scratch(rows),
        prefetch=1,
    )


def outer_twin_kernel(x, inner, out):
    out[0] = dot_tn(x[...], inner[0]).astype(low)


def outer_twin(x, inner):
    groups, rows, width = inner.shape
    return grouped(
        outer_twin_kernel,
        groups,
        [pl.BlockSpec((rows, HALF), lambda n: (0, 1)), group_spec(rows, width)],
        group_spec(HALF, width),
        struct((groups, HALF, width), low),
        (x, inner),
    )


def outer_own_kernel(groups, x, inner, other, mine, to_x, to_y, far_first, far_second):
    value = (dot_tn(x[...], inner[0]) + other[0].astype(full)).astype(low)
    rows = HALF // 4
    mine[0] = value[:rows]
    to_x[0] = value[rows : 2 * rows]
    to_y[0] = value[2 * rows : 3 * rows]
    n = pl.program_id(0)

    @pl.when(n < groups // 2)
    def _():
        far_first[0] = value[3 * rows :]

    @pl.when(n >= groups // 2)
    def _():
        far_second[0] = value[3 * rows :]


def outer_own(x, inner, other):
    groups, rows, width = inner.shape
    near = struct((groups, HALF // 4, width), low)
    far = struct((groups // 2, HALF // 4, width), low)
    shapes = [near, near, near, far, far]
    return grouped(
        functools.partial(outer_own_kernel, groups),
        groups,
        [pl.BlockSpec((rows, HALF), lambda n: (0, 0)), group_spec(rows, width), group_spec(HALF, width)],
        piece_specs(shapes, width),
        shapes,
        (x, inner, other),
    )


def norm_one_kernel(groups, order, *refs):
    inner, tok, grad, gains = refs[:4]
    own, twin = refs[4:9], refs[9:14]
    out, sums, total, tok_late, grad_late, sems = refs[14:]
    n = pl.program_id(0)
    copies = late_copies((tok, grad), (tok_late, grad_late), sems)

    @pl.when(n == 0)
    def _():
        for copy in copies:
            copy.start()
        total[...] = jnp.zeros_like(total)

    add_parts(groups, inner, own, twin, total)

    @pl.when(n == groups - 1)
    def _():
        for copy in copies:
            copy.wait()
        part, gain_sum, shift_sum = norm_back(tok_late[...], total[...], gains[0:1])
        result = grad_late[...] + part
        for at in range(BLOCKS):
            place = lane_block(order, at)
            cols = slice(at * LANES, (at + 1) * LANES)
            out[:, place] = result[:, cols]
            sums[0:1, place] = gain_sum[:, cols]
            sums[1:2, place] = shift_sum[:, cols]


def norm_one(order, inner, values, grad, gains, own, twin):
    groups, rows, width = inner.shape
    whole = whole_spec(rows, D)
    return grouped(
        functools.partial(norm_one_kernel, groups),
        groups,
        [group_spec(rows, width), late_spec(), late_spec(), whole_spec(2, D)]
        + piece_specs(own, width)
        + piece_specs(twin, width),
        [whole, whole_spec(2, D)],
        [struct((rows, D), full), struct((2, D), full)],
        (order, inner, values, grad, gains, *own, *twin),
        scratch=[pltpu.VMEM((rows, D), full)] + late_scratch(rows),
        prefetch=1,
    )


def turned_adam_kernel(rate, grad, weight, first, second, grad_out, second_out, weight_out):
    turned = grad[...].T
    grad_out[...] = turned
    second_new, updated = adam_step(weight[...], turned, first[...], second[...], rate, decay_rate)
    second_out[...] = second_new
    weight_out[...] = updated


def turned_adam(rate, grad, weight, first, second):
    return pl.pallas_call(
        functools.partial(turned_adam_kernel, rate),
        out_shape=[struct(weight.shape, full)] * 3,
        compiler_params=big,
    )(grad, weight, first, second)


def swap(values, bit):
    return lax.ppermute(values, "wide", [(at, at ^ bit) for at in range(8)])


def turn(values, step):
    return lax.ppermute(values, "narrow", [(at, (at + step) % 4) for at in range(4)])


def cross(values, bit):
    return lax.ppermute(values, "narrow", [(at, at ^ bit) for at in range(4)])


def fence(*values):
    return lax.optimization_barrier(values)


def plain_gather(block):
    groups = lax.all_gather(block, "narrow", axis=0, tiled=False)
    whole = lax.all_gather(groups, "wide", axis=1, tiled=True)
    rows, cut = HALF // 4, whole.shape[0] // 2
    sides = []
    for side in range(2):
        parts = [whole[:, side * HALF + at * rows : side * HALF + (at + 1) * rows] for at in range(4)]
        sides.append((*parts[:3], parts[3][:cut], parts[3][cut:]))
    return tuple(sides)


def plain_scatter(pieces, twin):
    far = jnp.concatenate(pieces[3:], axis=0)
    whole = jnp.concatenate([*pieces[:3], far, twin], axis=1)
    part = lax.psum_scatter(whole, "wide", scatter_dimension=1, tiled=True)
    return lax.psum_scatter(part, "narrow", scatter_dimension=0, tiled=False).astype(full)


def around(block):
    return [turn(block, step) for step in range(1, 4)]


def near_sends(pieces, from_y, from_x):
    cut = from_y.shape[0]
    to_x = jnp.concatenate([(pieces[1][:cut].astype(full) + from_y.astype(full)).astype(low), pieces[1][cut:]], axis=0)
    to_y = jnp.concatenate([pieces[2][:cut], (pieces[2][cut:].astype(full) + from_x.astype(full)).astype(low)], axis=0)
    return to_x, to_y


def last_sends(mine, over_x, over_y):
    part = (mine.astype(full) + over_x.astype(full) + over_y.astype(full)).astype(low)
    return tuple(part[at] for at in range(4))


def narrow_scatter(mine, over_x, over_y, places):
    part = (mine.astype(full) + over_x.astype(full) + over_y.astype(full)).astype(low)
    parts = [lax.dynamic_index_in_dim(part, places[at], 0, keepdims=False) for at in range(4)]
    return lax.psum_scatter(jnp.stack(parts), "narrow", scatter_dimension=0, tiled=False).astype(full)


def last_sum(first, rest):
    total = first.astype(full)
    for part in rest:
        total = total + part.astype(full)
    return total


def shards(
    tokens,
    cotangent,
    triple_weight,
    output_weight,
    expand_weight,
    shrink_weight,
    norm_gains,
    shift_biases,
    head_biases,
    expand_biases,
    triple_first,
    output_first,
    expand_first,
    shrink_first,
    gains_first,
    shifts_first,
    heads_first,
    widen_first,
    triple_second,
    output_second,
    expand_second,
    shrink_second,
    gains_second,
    shifts_second,
    heads_second,
    widen_second,
    *,
    wide,
    narrow,
):
    tuned = wide == 8 and narrow == 4
    rows = tokens.shape[0]
    local = head_biases.shape[1]
    hidden = expand_biases.shape[0]
    place = lax.axis_index("wide")
    at_narrow = lax.axis_index("narrow")
    if tuned:
        order = jnp.bitwise_xor(place, jnp.array([0, 2, 4, 6, 1, 3, 5, 7], jnp.int32)).astype(jnp.int32)
        steps = [lax.rem(at_narrow + (narrow - at), narrow) for at in range(narrow)]
    else:
        order = jnp.arange(BLOCKS, dtype=jnp.int32)
        steps = list(range(narrow))

    triple_block = jnp.concatenate([triple_weight[:, at].astype(low) for at in range(3)] + [output_weight.astype(low).T], axis=1)
    expand_block = expand_weight.astype(low)
    shrink_block = shrink_weight.astype(low).T
    zeros = jnp.zeros((local,), full)
    bias_rows = jnp.stack([jnp.concatenate([head_biases[0], zeros, head_biases[1], zeros]), expand_biases])

    def begin(order, tokens, cotangent):
        return pl.pallas_call(
            start_kernel,
            in_specs=[pl.BlockSpec(memory_space=pltpu.SMEM)] + [pl.BlockSpec(memory_space=pltpu.VMEM)] * 4,
            out_shape=[
                struct((rows, D), full),
                struct((rows, D), low),
                struct((rows, D), full),
                struct((rows, D), low),
                struct((2, D), full),
                struct((4, D), full),
                struct((1, D), full),
            ],
            compiler_params=big,
        )(order, tokens, cotangent, norm_gains, shift_biases)

    def split_bias(biases):
        return biases[:, 0:1, : 3 * local], biases[:, 1:2]

    if tuned:
        high = lax.reduce_precision(bias_rows, 8, 7)
        rest = bias_rows - high
        mid = lax.reduce_precision(rest, 8, 7)
        parts = jnp.concatenate([high, mid, rest - mid, jnp.zeros((10, hidden), full)]).astype(low)
        ridden = jnp.concatenate([triple_block, parts], axis=0)
        triple_turns = around(ridden)
        begun = begin(order, tokens, cotangent)
        triple_turns, begun, ridden, expand_block, shrink_block = fence(
            triple_turns, begun, ridden, expand_block, shrink_block
        )
        tok, normed, cot, cot_low, gains, shifts, cot_sum = begun
        depth = triple_block.shape[0]
        arrived = [ridden, *triple_turns]
        t_near = jnp.stack([block[:depth] for block in arrived])
        biases = jnp.stack([block[depth:] for block in arrived])
        t_x, t_y = swap(t_near, 2), swap(t_near, 4)
        expand_turns = around(expand_block)
        t_near, t_x, t_y, expand_turns, expand_block, normed, biases = fence(
            t_near, t_x, t_y, expand_turns, expand_block, normed, biases
        )
        t_f, t_g = swap(t_x[:2], 4), swap(t_y[2:], 2)
        t_near_c, t_x_c, t_y_c = swap(t_near, 1), swap(t_x, 1), swap(t_y, 1)
        e_near = jnp.stack([expand_block, *expand_turns])
        biases = biases.astype(full)
        triple_bias, widen_bias = split_bias(biases[:, 0:2] + biases[:, 2:4] + biases[:, 4:6])
        t_f, t_g, t_near_c, t_x_c, t_y_c, e_near, normed, triple_bias, shrink_block = fence(
            t_f, t_g, t_near_c, t_x_c, t_y_c, e_near, normed, triple_bias, shrink_block
        )
        e_x, e_y = swap(e_near, 2), swap(e_near, 4)
        t_f_c, t_g_c = swap(t_f, 1), swap(t_g, 1)
        triple_own = (t_near, t_x, t_y, t_f, t_g)
        triple_twin = (t_near_c, t_x_c, t_y_c, t_f_c, t_g_c)
        triple_twin, normed, shrink_block = fence(triple_twin, normed, shrink_block)
        shrink_turns = around(shrink_block)
        packed, mixed, logs = attend(normed, triple_bias, triple_own, triple_twin)
        e_near, e_x, e_y, mixed, shrink_turns, shrink_block, tok = fence(
            e_near, e_x, e_y, mixed, shrink_turns, shrink_block, tok
        )
        e_f, e_g = swap(e_x[:2], 4), swap(e_y[2:], 2)
        e_near_c, e_x_c, e_y_c = swap(e_near, 1), swap(e_x, 1), swap(e_y, 1)
        middle, normed_two = middle_call(mixed, tok, gains, shifts, triple_own, triple_twin, 3)
        s_near = jnp.stack([shrink_block, *shrink_turns])
        e_f, e_g, e_near_c, e_x_c, e_y_c, s_near, normed_two = fence(
            e_f, e_g, e_near_c, e_x_c, e_y_c, s_near, normed_two
        )
        s_x, s_y = swap(s_near, 2), swap(s_near, 4)
        expand_own = (e_near, e_x, e_y, e_f, e_g)
        expand_twin = (e_near_c, e_x_c, e_y_c, swap(e_f, 1), swap(e_g, 1))
    else:
        tok, normed, cot, cot_low, gains, shifts, cot_sum = begin(order, tokens, cotangent)
        triple_bias, widen_bias = split_bias(lax.all_gather(bias_rows, "narrow", axis=0, tiled=False))
        triple_own, triple_twin = plain_gather(triple_block)
        expand_own, expand_twin = plain_gather(expand_block)
        shrink_own, shrink_twin = plain_gather(shrink_block)
        packed, mixed, logs = attend(normed, triple_bias, triple_own, triple_twin)
        middle, normed_two = middle_call(mixed, tok, gains, shifts, triple_own, triple_twin, 3)

    active, slope, s_twin = expand(normed_two, widen_bias, cot_low, expand_own, expand_twin)
    if tuned:
        s_near, s_x, s_y, s_twin, cot_low, active = fence(s_near, s_x, s_y, s_twin, cot_low, active)
        s_f, s_g = swap(s_x[:2], 4), swap(s_y[2:], 2)
        s_other = swap(s_twin, 1)
        s_near_c, s_x_c = swap(s_near, 1), swap(s_x, 1)
        s_pieces = outer_own(cot_low, active, s_other)
        s_f, s_g, s_pieces, s_near_c, s_x_c, cot_low, slope = fence(
            s_f, s_g, s_pieces, s_near_c, s_x_c, cot_low, slope
        )
        from_y, from_x = swap(s_pieces[3], 4), swap(s_pieces[4], 2)
        shrink_own = (s_near, s_x, s_y, s_f, s_g)
        shrink_twin = (s_near_c, s_x_c, swap(s_y, 1), swap(s_f, 1), swap(s_g, 1))
    else:
        s_pieces = outer_own(cot_low, active, jnp.zeros_like(s_twin))
    expanded_low, widen_sum, e_twin, layer_output, middle_grad, middle_low, two_sums = hidden_back(
        order,
        cot_low,
        slope,
        active,
        middle,
        cot,
        gains,
        shifts,
        normed_two,
        shrink_own,
        shrink_twin,
        expand_own,
        expand_twin,
    )
    if tuned:
        from_y, from_x, expanded_low, e_twin, s_pieces = fence(from_y, from_x, expanded_low, e_twin, s_pieces)
        e_other = swap(e_twin, 1)
        to_x, to_y = near_sends(s_pieces, from_y, from_x)
        s_over_x, s_over_y = swap(to_x, 2), swap(to_y, 4)
    else:
        e_other = jnp.zeros_like(e_twin)
    o_twin = outer_twin(middle_low, mixed)
    if tuned:
        e_other, o_twin, expanded_low = fence(e_other, o_twin, expanded_low)
    e_pieces = outer_own(normed_two, expanded_low, e_other)
    if tuned:
        e_pieces, middle_low, packed, o_twin = fence(e_pieces, middle_low, packed, o_twin)
        from_y, from_x = swap(e_pieces[3], 4), swap(e_pieces[4], 2)
        o_other = swap(o_twin, 1)
    else:
        o_other = jnp.zeros_like(o_twin)
    triple_low, head_sums, t_twin = attend_back(middle_low, packed, logs, normed, triple_own, triple_twin, 3)
    if tuned:
        from_y, from_x, s_over_x, s_over_y, t_twin, triple_low, e_pieces, s_pieces, mixed, o_other = fence(
            from_y, from_x, s_over_x, s_over_y, t_twin, triple_low, e_pieces, s_pieces, mixed, o_other
        )
        t_other = swap(t_twin, 1)
        to_x, to_y = near_sends(e_pieces, from_y, from_x)
        e_over_x, e_over_y = swap(to_x, 2), swap(to_y, 4)
        shrink_grad = narrow_scatter(s_pieces[0], s_over_x, s_over_y, steps)
    else:
        t_other = jnp.zeros_like(t_twin)
    o_pieces = outer_own(middle_low, mixed, o_other)
    if tuned:
        t_other, o_pieces, triple_low, normed = fence(t_other, o_pieces, triple_low, normed)
    t_pieces = outer_own(normed, triple_low, t_other)
    if tuned:
        t_pieces, triple_low = fence(t_pieces, triple_low)
        t_from_y, t_from_x = swap(t_pieces[3], 4), swap(t_pieces[4], 2)
    input_gradient, one_sums = norm_one(
        order, triple_low, tok, middle_grad, gains, triple_own, triple_twin
    )
    turned_heads = jnp.stack([lax.dynamic_index_in_dim(head_sums, step, 0, keepdims=False) for step in steps], axis=1)
    turned_widen = jnp.concatenate([lax.dynamic_index_in_dim(widen_sum, step, 0, keepdims=False) for step in steps])
    small = jnp.concatenate(
        [
            one_sums[0:1],
            two_sums[0:1],
            one_sums[1:2],
            two_sums[1:3],
            cot_sum,
            turned_heads.reshape(2, D),
            turned_widen.reshape(-1, D),
        ],
        axis=0,
    )
    if tuned:
        t_from_y, t_from_x, small, t_pieces, e_over_x, e_over_y, o_pieces = fence(
            t_from_y, t_from_x, small, t_pieces, e_over_x, e_over_y, o_pieces
        )
        to_x, to_y = near_sends(t_pieces, t_from_y, t_from_x)
        to_x, to_y, small, e_over_x, e_over_y, o_pieces = fence(to_x, to_y, small, e_over_x, e_over_y, o_pieces)
        t_over_x, t_over_y = swap(to_x, 2), swap(to_y, 4)
        expand_gradient = narrow_scatter(e_pieces[0], e_over_x, e_over_y, steps)
        from_y, from_x = swap(o_pieces[3], 4), swap(o_pieces[4], 2)
        to_x, to_y = near_sends(o_pieces, from_y, from_x)
        o_over_x, o_over_y = swap(to_x, 2), swap(to_y, 4)
        small = small + swap(small, 1)
        small = small + cross(small, 1)
        shrink_done = turned_adam(0.05, shrink_grad, shrink_weight, shrink_first, shrink_second)
        t_over_x, t_over_y, o_over_x, o_over_y, small, expand_gradient, shrink_done = fence(
            t_over_x, t_over_y, o_over_x, o_over_y, small, expand_gradient, shrink_done
        )
        t_last = last_sends(t_pieces[0], t_over_x, t_over_y)
        t_last, small, expand_gradient, o_over_x, o_over_y = fence(t_last, small, expand_gradient, o_over_x, o_over_y)
        small = small + cross(small, 2)
        small = small + swap(small, 2)
        small = small + swap(small, 4)
        t_back = [turn(t_last[step], -step) for step in range(1, 4)]
        output_grad = narrow_scatter(o_pieces[0], o_over_x, o_over_y, steps)
        output_done = turned_adam(1.0, output_grad, output_weight, output_first, output_second)
        t_back, output_done = fence(t_back, output_done)
        triple_grad = last_sum(t_last[0], t_back)
    else:
        small = lax.psum(small, ("wide", "narrow"))
        triple_grad = plain_scatter(t_pieces, t_twin)
        output_grad = plain_scatter(o_pieces, o_twin)
        expand_gradient = plain_scatter(e_pieces, e_twin)
        shrink_grad = plain_scatter(s_pieces, s_twin)
    triple_gradient = jnp.stack([triple_grad[:, at * local : (at + 1) * local] for at in range(3)], axis=1)
    if not tuned:
        shrink_done = turned_adam(0.05, shrink_grad, shrink_weight, shrink_first, shrink_second)
        output_done = turned_adam(1.0, output_grad, output_weight, output_first, output_second)
    gains_gradient = small[0:2]
    shifts_gradient = small[2:6]
    heads_gradient = lax.dynamic_slice_in_dim(small[6:8], at_narrow * local, local, 1)
    widen_gradient = lax.dynamic_slice_in_dim(small[8:].reshape(-1), at_narrow * hidden, hidden, 0)

    params = (
        triple_weight,
        output_weight,
        expand_weight,
        shrink_weight,
        norm_gains,
        shift_biases,
        head_biases,
        expand_biases,
    )
    gradients = (
        triple_gradient,
        output_done[0],
        expand_gradient,
        shrink_done[0],
        gains_gradient,
        shifts_gradient,
        heads_gradient,
        widen_gradient,
    )
    firsts = (
        triple_first,
        output_first,
        expand_first,
        shrink_first,
        gains_first,
        shifts_first,
        heads_first,
        widen_first,
    )
    seconds = (
        triple_second,
        output_second,
        expand_second,
        shrink_second,
        gains_second,
        shifts_second,
        heads_second,
        widen_second,
    )
    rates = (0.1, 1.0, 0.1, 0.05, 1.0, 0.3, 0.2, 0.3)
    decays = (decay_rate, decay_rate, decay_rate, decay_rate, 0.0, 0.0, 0.0, 0.0)
    results = [layer_output, input_gradient]
    for index in range(8):
        if index in (1, 3):
            results.extend(output_done if index == 1 else shrink_done)
            continue
        renewed, updated = adam_step(
            params[index],
            gradients[index],
            firsts[index],
            seconds[index],
            rates[index],
            decays[index],
        )
        if index == 5:
            results.extend([gradients[index], renewed[1:], renewed[0], updated])
        else:
            results.extend([gradients[index], renewed, updated])
    return tuple(results)


def solution(mesh):
    placed = (
        P(("wide", "narrow"), None),
        P(("wide", "narrow"), None),
        P("wide", None, "narrow"),
        P("narrow", "wide"),
        P("wide", "narrow"),
        P("narrow", "wide"),
        P(),
        P(),
        P(None, "narrow"),
        P("narrow"),
        P("wide", None, "narrow"),
        P("narrow", "wide"),
        P("wide", "narrow"),
        P("narrow", "wide"),
        P(),
        P(),
        P(None, "narrow"),
        P("narrow"),
        P("wide", None, "narrow"),
        P("narrow", "wide"),
        P("wide", "narrow"),
        P("narrow", "wide"),
        P(),
        P(),
        P(None, "narrow"),
        P("narrow"),
    )
    matrices = (P("wide", None, "narrow"), P("narrow", "wide"), P("wide", "narrow"), P("narrow", "wide"))
    outs = [P(("wide", "narrow"), None), P(("wide", "narrow"), None)]
    for spec in matrices:
        outs.extend([spec] * 3)
    outs.extend([P()] * 7)
    outs.extend([P(None, "narrow")] * 3)
    outs.extend([P("narrow")] * 3)
    return jax.shard_map(
        functools.partial(shards, wide=mesh.shape["wide"], narrow=mesh.shape["narrow"]),
        mesh=mesh,
        in_specs=placed,
        out_specs=tuple(outs),
        check_vma=False,
    )
```
